32 devices in a mesh: row: 8 (over z, y), col: 4 (over x, core).
Axes of the slice: x: 2, y: 2, z: 4, core: 2. Of those that a mesh axis runs over, the one named last changes fastest.
Arguments:
- feature_map: bfloat16 [512, 32, 2048], P('row', 'col'), may hold values from -6 to 6
- image_ids: int32 [512, 32], P('row', 'col'), may hold values from 0 to 16, as said below
- point_weight: bfloat16 [2048, 256], replicated, may hold values from -0.125 to 0.125
- atrous_weight: bfloat16 [3, 3, 3, 2048, 256], replicated, may hold values from -0.046875 to 0.046875
- pool_weight: bfloat16 [2048, 256], replicated, may hold values from -0.125 to 0.125
- project_weight: bfloat16 [1280, 256], replicated, may hold values from -0.15625 to 0.15625
- bn_gain: float32 [6, 256], replicated, may hold values from 0.5 to 1.5
- bn_shift: float32 [6, 256], replicated, may hold values from -2.5 to 2.5
- out_grad: bfloat16 [512, 32, 256], P('row', 'col'), may hold values from -6 to 6
Outputs:
- output: bfloat16 [512, 32, 256], P('row', 'col')
- input_grad: bfloat16 [512, 32, 2048], P('row', 'col')
- point_grad: float32 [2048, 256], P('row')
- atrous_grad: float32 [3, 3, 3, 2048, 256], P(None, None, None, 'row')
- pool_grad: float32 [2048, 256], P('row')
- project_grad: float32 [1280, 256], replicated
- gain_grad: float32 [6, 256], replicated
- shift_grad: float32 [6, 256], replicated
The draws below stay inside these ranges and needn't reach their ends.
Inputs may be any that keep to these rules, and one draw needn't show every extreme that they name: `image_ids`: image 0 fills the first c columns of every row, 8 < c <= 24; the remaining columns of each row belong to one image; these images are numbered 1, 2, … from the top row downward, each 16 to 48 rows tall, so the map holds H / 32 + 1 images.
All inputs are finite; a program needn't handle non-finite values.
Results may differ from the reference program's by a relative error of at most 0.012.
Values may be sent and summed in bfloat16 or wider, within the bound.
No kernel may reach another device: no remote copies, remote signals or barrier semaphores. Data moves between devices by JAX's collectives and lax.ppermute only.
A program may use at most 448 MiB of HBM per device.

```python
from functools import partial
import jax
import jax.numpy as jnp
from jax import lax

C = 2048
F = 256
REACH = 18
IMG_ROWS = 32
H = 512
W = 32
IMAGES = 17


def draw_image_ids(key, part):
    key = jax.random.fold_in(key, 7)
    first, second = jax.random.split(key)
    split = jax.random.randint(first, (), W // 4 + 1, 3 * W // 4 + 1)
    jitter = jax.random.randint(second, (H // IMG_ROWS - 1,), -(IMG_ROWS // 4), IMG_ROWS // 4 + 1)
    bounds = IMG_ROWS * jnp.arange(1, H // IMG_ROWS, dtype=jnp.int32) + jitter
    rows = jnp.arange(H, dtype=jnp.int32)
    strip = 1 + jnp.sum((rows[:, None] >= bounds[None, :]).astype(jnp.int32), axis=1)
    columns = jnp.arange(W, dtype=jnp.int32)
    return jnp.where(columns[None, :] < split, 0, strip[:, None]).astype(jnp.int32)


def shard_levels(own_key, dims, pieces, least, high):
    level = 1.0
    for axis_at, shards_of in pieces:
        heights = jax.random.uniform(jax.random.fold_in(jax.random.fold_in(own_key, 6), axis_at), (shards_of,), jnp.float32, least / len(pieces), high / len(pieces))
        level = level * jnp.repeat(jnp.exp(heights), dims[axis_at] // shards_of).reshape((-1,) + (1,) * (len(dims) - 1 - axis_at))
    return level


def normal_values(stream_key, dims, scale, reach, cuts=(), kind=jnp.bfloat16):
    level = shard_levels(stream_key, dims, cuts, -0.22, 0.18) if cuts else 1.0
    drawn = jax.random.normal(stream_key, dims, jnp.float32) * scale * level
    return jnp.minimum(jnp.maximum(drawn, -reach), reach).astype(kind)


def setup_inputs(seed: int = 0) -> dict:
    splits = jax.random.split(jax.random.key(seed), 10)
    return {
        "feature_map": normal_values(splits[0], (H, W, C), 1.0, 6.0, ((0, 8), (1, 4))),
        "image_ids": draw_image_ids(jax.random.fold_in(splits[9], 71), 0),
        "point_weight": normal_values(splits[2], (C, F), C ** -0.5, 0.125),
        "atrous_weight": normal_values(splits[3], (3, 3, 3, C, F), (9 * C) ** -0.5, 0.046875),
        "pool_weight": normal_values(splits[4], (C, F), C ** -0.5, 0.125),
        "project_weight": normal_values(splits[5], (5 * F, F), (5 * F) ** -0.5, 0.15625),
        "bn_gain": jnp.clip(1.0 + 0.1 * jax.random.normal(splits[6], (6, F), jnp.float32), 0.5, 1.5),
        "bn_shift": normal_values(splits[7], (6, F), 0.5, 2.5, (), jnp.float32),
        "out_grad": normal_values(splits[8], (H, W, F), 1.0, 6.0, ((0, 8), (1, 4))),
    }


@jax.custom_vjp
def low(v):
    return lax.optimization_barrier(v.astype(jnp.bfloat16)).astype(jnp.float32)

@jax.custom_vjp
def low_back(v):
    return v

def low_keep(v):
    return (low(v), None)

def low_pass(kept, grad):
    return (grad,)

def back_keep(v):
    return (v, None)

def back_low(kept, grad):
    return (low(grad),)
low.defvjp(low_keep, low_pass)
low_back.defvjp(back_keep, back_low)

def product(left, right):
    return jnp.dot(left, right, precision=lax.Precision.HIGHEST)

def normalize(value, gain, shift):
    mean = lax.optimization_barrier(jnp.mean(value, axis=0))
    spread = lax.optimization_barrier(jnp.mean(value * value, axis=0)) - mean * mean
    scaled = (value - mean) * lax.rsqrt(spread + 1e-05)
    return jax.nn.gelu(scaled * gain + shift, approximate=True)

def layer(image_ids, feature_map, point_weight, atrous_weight, pool_weight, project_weight, bn_gain, bn_shift):
    flat = feature_map.reshape(H * W, C)
    marks = image_ids + 1
    padded = jnp.pad(feature_map, ((REACH, REACH), (REACH, REACH), (0, 0)))
    padded_marks = jnp.pad(marks, REACH)
    branches = [low_back(product(flat, point_weight))]
    for branch in range(3):
        spread = REACH * (branch + 1) // 3
        kernel = atrous_weight[branch].reshape(9, C, F)

        def one_tap(summed, tap, spread=spread, kernel=kernel):
            down = ((tap // 3 - 1) * spread + REACH).astype(jnp.int32)
            right = ((tap % 3 - 1) * spread + REACH).astype(jnp.int32)
            anchor = jnp.zeros((), jnp.int32)
            piece = lax.dynamic_slice(padded, (down, right, anchor), (H, W, C))
            near = lax.dynamic_slice(padded_marks, (down, right), (H, W))
            keep = (near == marks).astype(jnp.float32).reshape(H * W, 1)
            weight = lax.dynamic_index_in_dim(kernel, tap, 0, keepdims=False)
            return (summed + keep * product(piece.reshape(H * W, C), weight), None)
        summed, _ = lax.scan(jax.checkpoint(one_tap), jnp.zeros((H * W, F), jnp.float32), jnp.arange(9, dtype=jnp.int32))
        branches.append(low_back(summed))
    flat_ids = image_ids.reshape(H * W)
    table = (flat_ids[:, None] == jnp.arange(IMAGES, dtype=jnp.int32)[None, :]).astype(jnp.float32)
    counts = lax.optimization_barrier(jnp.sum(table, axis=0))
    pooled = low(product(table.T, flat) / counts[:, None])
    per_image = low_back(product(pooled, pool_weight))
    branches.append(per_image[flat_ids])
    activated = [normalize(value, bn_gain[k], bn_shift[k]) for k, value in enumerate(branches)]
    joined = low(jnp.concatenate(activated, axis=1))
    head = low_back(product(joined, project_weight))
    return normalize(head, bn_gain[5], bn_shift[5]).reshape(H, W, F)

def reference(feature_map, image_ids, point_weight, atrous_weight, pool_weight, project_weight, bn_gain, bn_shift, out_grad):
    inputs = (feature_map.astype(jnp.float32), point_weight.astype(jnp.float32), atrous_weight.astype(jnp.float32), pool_weight.astype(jnp.float32), project_weight.astype(jnp.float32), bn_gain, bn_shift)
    output, backward = jax.vjp(partial(layer, image_ids), *inputs)
    grads = backward(out_grad.astype(jnp.float32))
    return (output.astype(jnp.bfloat16), grads[0].astype(jnp.bfloat16), grads[1], grads[2], grads[3], grads[4], grads[5], grads[6])
```

```python
from functools import partial

import jax
import jax.numpy as jnp
from jax import lax
from jax.experimental import pallas as pl
from jax.experimental.pallas import tpu as pltpu
from jax.sharding import Mesh, PartitionSpec as P

REACH = 18
IMG_ROWS = 32
EPSILON = 1e-05
PAD = 32
SWAP = [(0, 1), (1, 0)]
BF = jnp.bfloat16
F32 = jnp.float32
VMEM_LIMIT = 60 * 2**20


def dot(a, b):
    return jnp.dot(a, b, preferred_element_type=F32)


def exact(a, b):
    return jnp.dot(a, b, precision=lax.Precision.HIGHEST, preferred_element_type=F32)


def swap(x, axis):
    return lax.ppermute(x, axis, SWAP)


def allsum(x, axes):
    for axis in axes:
        count = lax.axis_size(axis)
        step = 1
        while step < count:
            x = x + lax.ppermute(x, axis, [(i, i ^ step) for i in range(count)])
            step *= 2
    return x


def smooth(value):
    return jax.nn.gelu(value, approximate=True)


def smooth_slope(value):
    root = 0.7978845608028654
    square = value * value
    tanh = jnp.tanh(root * (value + 0.044715 * value * square))
    return 0.5 * (1.0 + tanh) + 0.5 * value * (1.0 - tanh * tanh) * root * (
        1.0 + 3 * 0.044715 * square
    )


def moments(value):
    return jnp.stack([jnp.sum(value, axis=0), jnp.sum(value * value, axis=0)])


def gather_window(info, mains, halos, window, sems):
    iy, ix, ik = info[0], info[1], info[2]
    copies = []
    for n, piece in enumerate(mains):
        dk, dy, dx = n // 4, n // 2 % 2, n % 2
        col = ((ix ^ dx) * 2 + (ik ^ dk)) * 8
        row = pl.multiple_of(PAD + (iy ^ dy) * 64, 32)
        copies.append(
            pltpu.make_async_copy(
                piece, window.at[pl.ds(col, 8), pl.ds(row, 64)], sems.at[n]
            )
        )
    for copy in copies:
        copy.start()
    for n, halo in enumerate(halos):
        dk, dy, dx = n // 4, n // 2 % 2, n % 2
        col = ((ix ^ dx) * 2 + (ik ^ dk)) * 8
        top = (iy ^ dy) == 1

        @pl.when(top)
        def _(halo=halo, col=col):
            for q in range(8):
                window[col + q, PAD - REACH : PAD, :] = halo[q]

        @pl.when(jnp.logical_not(top))
        def _(halo=halo, col=col):
            for q in range(8):
                window[col + q, PAD + 128 : PAD + 128 + REACH, :] = halo[q]

    return copies


def build(window, shifted, mask, spread, sign, cut, lanes, offset):
    low = mask[0]
    high = mask[1]

    def column(q, carry):
        for i in range(3):
            start = PAD + sign * (i - 1) * spread
            value = window[q, start : start + 128, :]
            if i != 1:
                keep = high if sign * (i - 1) > 0 else low
                keep = jnp.where(q >= cut, keep, jnp.ones_like(keep))
                value = value * jnp.concatenate([keep] * (lanes // 128), axis=1)
            shifted[offset + q, :, i * lanes : (i + 1) * lanes] = value
        return carry

    lax.fori_loop(0, 32, column, 0)


def column_sum(shifted, weights, col, spread, sign, cut, lanes, acc, fresh):
    wide = acc.shape[-1]
    first = dot(shifted[pl.ds(REACH + col, 4)].reshape(512, 3 * lanes), weights(1))
    first = first.reshape(4, 128, wide)
    if fresh:
        acc[...] = first
    else:
        acc[...] += first
    for j in (0, 2):
        source = col + sign * (j - 1) * spread
        oks = []
        for e in range(4):
            near = source + e
            oks.append((near >= 0) & (near < 32) & ((near < cut) == (col + e < cut)))

        @pl.when(oks[0] | oks[1] | oks[2] | oks[3])
        def _(j=j, source=source, oks=oks):
            part = dot(shifted[pl.ds(REACH + source, 4)].reshape(512, 3 * lanes), weights(j))
            part = part.reshape(4, 128, wide)
            for e in range(4):
                acc[e] += jnp.where(oks[e], part[e], 0.0)


def forward_kernel(spreads, pointed, split_x, lanes, info, *refs):
    mains, halos = refs[:8], refs[8:16]
    mask, point, weights, keep, send, window, shifted, acc, sems = refs[16:]
    iy, ix, ik, cut = info[0], info[1], info[2], info[3]
    for copy in gather_window(info, mains, halos, window, sems):
        copy.wait()

    def place(g, q, lane):
        for half in range(2):
            value = acc[:, half * 64 : half * 64 + 64, :]
            here = (ix == g) if split_x else (iy == half)
            other = (iy ^ half) if split_x else (ix ^ g)

            @pl.when(here)
            def _(value=value, other=other):
                keep[other, q : q + 4, :, lane : lane + 256] = value

            @pl.when(jnp.logical_not(here))
            def _(value=value, other=other):
                send[other, q : q + 4, :, lane : lane + 256] = value.astype(BF)

    lane = 0
    if pointed:
        for g in range(2):
            for q in (0, 4):
                col = g * 16 + ik * 8 + q
                source = window[pl.ds(col, 4), PAD : PAD + 128, :].reshape(512, lanes)
                acc[...] = dot(source, point[...]).reshape(4, 128, 256)
                place(g, q, lane)
        lane = 256
    for n, spread in enumerate(spreads):
        build(window, shifted, (mask[n, 0], mask[n, 1]), spread, 1, cut, lanes, REACH)
        for g in range(2):
            for q in (0, 4):
                col = g * 16 + ik * 8 + q
                column_sum(
                    shifted, lambda j: weights[n, j], col, spread, 1, cut, lanes, acc, True
                )
                place(g, q, lane)
        lane += 256


def input_kernel(spreads, lanes, info, *refs):
    count = len(spreads)
    mains, halos = refs[: 8 * (count + 1)], refs[8 * (count + 1) : 16 * count + 8]
    mask, point, weights, edge, strip = refs[16 * count + 8 : 16 * count + 13]
    outs = refs[16 * count + 13 : 16 * count + 17]
    window, shifted, acc, sems = refs[16 * count + 17 :]
    iy, ix, ik, cut = info[0], info[1], info[2], info[3]
    for copy in gather_window(info, mains[:8], (), window, sems):
        copy.wait()
    for g in range(2):
        for q in (0, 4):
            col = g * 16 + ik * 8 + q
            source = window[pl.ds(col, 4), PAD : PAD + 128, :].reshape(512, lanes)
            acc[g * 2 + q // 4] = dot(source, point[...]).reshape(4, 128, acc.shape[-1])
            for e in range(4):
                acc[g * 2 + q // 4, e] += jnp.where(col + e < cut, edge[...], strip[...])
    for n, spread in enumerate(spreads):
        copies = gather_window(
            info, mains[8 * n + 8 : 8 * n + 16], halos[8 * n : 8 * n + 8], window, sems
        )
        for copy in copies:
            copy.wait()
        build(window, shifted, (mask[n, 0], mask[n, 1]), spread, -1, cut, lanes, REACH)
        for g in range(2):
            for q in (0, 4):
                col = g * 16 + ik * 8 + q
                column_sum(
                    shifted,
                    lambda j: weights[n, j],
                    col,
                    spread,
                    -1,
                    cut,
                    lanes,
                    acc.at[g * 2 + q // 4],
                    False,
                )
    for g in range(2):
        for q in (0, 4):
            for half in range(2):
                value = acc[g * 2 + q // 4, :, half * 64 : half * 64 + 64, :].astype(BF)
                for dy in range(2):
                    for dx in range(2):

                        @pl.when(((iy ^ half) == dy) & ((ix ^ g) == dx))
                        def _(value=value, dy=dy, dx=dx, q=q):
                            outs[dy * 2 + dx][q : q + 4] = value


def weight_kernel(spread, pointed, lanes, info, *refs):
    mains, halos = refs[:8], refs[8:16]
    points = refs[16:24] if pointed else ()
    mask, across, out, window, shifted, zeroed, sems = refs[24 if pointed else 16 :]
    cut = info[3]
    parts = out.shape[0]
    each = out.shape[2]
    if pointed:
        for copy in gather_window(info, points, (), window, sems):
            copy.wait()
        source = window[:, PAD : PAD + 128, :].reshape(32 * 128, lanes)
        value = dot(across[...], source).astype(BF)
        for z in range(parts):
            out[z, 9] = value[z * each : (z + 1) * each]
    for copy in gather_window(info, mains, halos, window, sems):
        copy.wait()
    build(window, shifted, (mask[0], mask[1]), spread, -1, cut, lanes, 0)
    pixel = lax.broadcasted_iota(jnp.int32, (1, 32 * 128), 1) // 128
    clear = (pixel >= cut - spread) & (pixel < cut)
    zeroed[...] = jnp.where(clear, jnp.zeros_like(across[...]), across[...])

    def emit(j, value):
        for i in range(3):
            for z in range(parts):
                piece = value[z * each : (z + 1) * each, i * lanes : (i + 1) * lanes]
                out[z, 3 * i + j] = piece.astype(BF)

    short = 32 - spread
    emit(1, dot(across[...], shifted[...].reshape(32 * 128, 3 * lanes)))
    emit(
        0,
        dot(
            zeroed[:, : short * 128],
            shifted[spread:].reshape(short * 128, 3 * lanes),
        ),
    )

    def wipe(q, carry):
        shifted[q] = jnp.zeros(shifted.shape[1:], BF)
        return carry

    lax.fori_loop(jnp.maximum(cut - spread, 0), jnp.minimum(cut, 32), wipe, 0)
    emit(
        2,
        dot(
            across[:, spread * 128 :],
            shifted[:short].reshape(short * 128, 3 * lanes),
        ),
    )


VMEM = pl.BlockSpec(memory_space=pltpu.VMEM)
SMEM = pl.BlockSpec(memory_space=pltpu.SMEM)
ANY = pl.BlockSpec(memory_space=pl.ANY)


def call(kernel, name, flops, in_specs, out_shape, scratch, args):
    return pl.pallas_call(
        kernel,
        name=name,
        in_specs=in_specs,
        out_specs=jax.tree.map(lambda _: VMEM, out_shape),
        out_shape=out_shape,
        scratch_shapes=scratch,
        compiler_params=pltpu.CompilerParams(vmem_limit_bytes=VMEM_LIMIT),
        cost_estimate=pl.CostEstimate(flops=flops, bytes_accessed=10**7, transcendentals=0),
    )(*args)


def per_device(
    feature_map,
    image_ids,
    point_weight,
    atrous_weight,
    pool_weight,
    project_weight,
    bn_gain,
    bn_shift,
    out_grad,
):
    rows, cols, chans = feature_map.shape
    feat = point_weight.shape[1]
    pixels = rows * cols
    zs = lax.axis_size("z")
    axes = ("k", "x", "y", "z")
    iz, iy, ix, ik = (lax.axis_index(a) for a in ("z", "y", "x", "k"))
    row_count = 2 * zs
    total = float(pixels * row_count * 4)
    images = rows * row_count // IMG_ROWS + 1
    share = chans // (4 * zs)
    mine = chans // 4
    spreads = [REACH * (b + 1) // 3 for b in range(3)]
    toward = [(2 * z, 2 * z - 2) for z in range(1, zs)] + [
        (2 * z + 1, 2 * z + 3) for z in range(zs - 1)
    ]

    def pick(first, second, index):
        return jnp.where(index == 0, first, second)

    def rim(x):
        return pick(x[:, :REACH], x[:, rows - REACH :], iy)

    with jax.named_scope("spread_features"):
        packed = feature_map.reshape(rows, cols, zs, 2, 2, share)
        packed = packed.transpose(3, 4, 1, 0, 2, 5).reshape(2, 2, cols, rows, mine)
        packed = lax.dynamic_index_in_dim(packed, iy, 0, False), lax.dynamic_index_in_dim(
            packed, 1 - iy, 0, False
        )
        tiles = [
            lax.dynamic_index_in_dim(packed[dy], ix if dx == 0 else 1 - ix, 0, False)
            for dy in range(2)
            for dx in range(2)
        ]
        brims = [
            lax.ppermute(rim(tile), ("z", "y"), toward) for tile in tiles
        ]

        def exchange(parts):
            own, to_x, to_y, to_d = parts
            got = [own, swap(to_x, "x"), swap(to_y, "y")]
            got.append(lax.ppermute(to_d, ("y", "x"), [(i, 3 - i) for i in range(4)]))
            return got + [swap(g, "k") for g in got]

        mains = exchange(tiles)
        halos = exchange(brims)

    with jax.named_scope("marks"):
        strip_own = jnp.max(image_ids, axis=1)
        zero_own = jnp.sum((image_ids[0] == 0).astype(jnp.int32))
        for axis in ("k", "x"):
            both = jnp.concatenate([strip_own, zero_own[None]])
            other = swap(both, axis)
            strip_own = jnp.maximum(strip_own, other[:rows])
            zero_own = zero_own + other[rows]
        cut = zero_own
        edge_own = pick(strip_own[:REACH], strip_own[rows - REACH :], iy)
        edge = lax.ppermute(edge_own, ("z", "y"), toward)
        other = swap(jnp.concatenate([strip_own, edge]), "y")
        strip_plane = jnp.concatenate(
            [pick(strip_own, other[:rows], iy), pick(other[:rows], strip_own, iy)]
        )
        top, bottom = pick(other[rows:], edge, iy), pick(edge, other[rows:], iy)
        strip_tall = jnp.concatenate([top, strip_plane, bottom])
        masks = jnp.stack(
            [
                jnp.stack(
                    [
                        strip_plane
                        == lax.slice_in_dim(strip_tall, REACH + s * d, REACH + s * d + 2 * rows)
                        for s in (-1, 1)
                    ]
                )
                for d in spreads
            ]
        )
        masks = jnp.broadcast_to(masks[..., None], (3, 2, 2 * rows, 128)).astype(BF)
        info = jnp.stack([iy, ix, ik, cut]).astype(jnp.int32)

    local_ids = image_ids.T.reshape(pixels)
    image_range = jnp.arange(images, dtype=jnp.int32)
    table = local_ids[:, None] == image_range[None, :]

    with jax.named_scope("image_sums"):
        natural = image_ids.reshape(pixels)[:, None] == image_range[None, :]
        sums = jnp.einsum(
            "pi,pc->ic",
            natural.astype(BF),
            feature_map.reshape(pixels, chans),
            preferred_element_type=F32,
        )
        sums = sums.reshape(images, zs, 2, 2, share).transpose(2, 3, 0, 1, 4)
        sums = sums.reshape(2, 2, images, mine)
        ysent = lax.dynamic_index_in_dim(sums, 1 - iy, 0, False)
        ykept = lax.dynamic_index_in_dim(sums, iy, 0, False) + swap(ysent, "y")
        xsent = lax.dynamic_index_in_dim(ykept, 1 - ix, 0, False)
        xkept = lax.dynamic_index_in_dim(ykept, ix, 0, False) + swap(xsent, "x")
        strip_rows = jnp.sum(
            (strip_plane[:, None] == image_range[None, :]).astype(F32), axis=0
        )
        tall = jnp.concatenate(
            [allsum(xkept, ("k",)), jnp.broadcast_to(strip_rows[:, None], (images, 128))], axis=1
        )
        tall = allsum(tall, ("z",))
        image_sums = tall[:, :mine]
        whole = 4 * cols
        counts = jnp.where(
            image_range == 0,
            (cut * (rows * row_count)).astype(F32),
            tall[:, mine] * (whole - cut).astype(F32),
        )
        pooled = (image_sums / counts[:, None]).astype(BF)
        pool_mine = pool_weight.reshape(zs, 2, 2, share, feat)
        pool_mine = lax.dynamic_slice(
            pool_mine, (0, iy, ix, 0, 0), (zs, 1, 1, share, feat)
        ).reshape(mine, feat)
        per_image = allsum(dot(pooled, pool_mine), ("x", "y"))

    with jax.named_scope("weights"):
        point_mine = lax.dynamic_slice(
            point_weight.reshape(zs, 2, 2, share, feat),
            (0, iy, ix, 0, 0),
            (zs, 1, 1, share, feat),
        ).reshape(mine, feat)
        atrous = lax.dynamic_slice(
            atrous_weight.reshape(3, 3, 3, zs, 2, 2, share, feat),
            (0, 0, 0, 0, iy, ix, 0, 0),
            (3, 3, 3, zs, 1, 1, share, feat),
        ).reshape(3, 3, 3, mine, feat)
        forward_weights = atrous.transpose(0, 2, 1, 3, 4).reshape(3, 3, 3 * mine, feat)
        back_weights = atrous.transpose(0, 2, 1, 4, 3).reshape(3, 3, 3 * feat, mine)
        point_back = point_mine.T

    def forward(chosen, pointed, split_x):
        n = len(chosen)
        width = 256 * (n + pointed)
        shape = (2, cols, rows, width)
        return call(
            partial(forward_kernel, [spreads[b] for b in chosen], pointed, split_x, mine),
            "forward_taps",
            2 * 2048 * mine * 256 * 9 * n,
            [SMEM] + [ANY] * 8 + [VMEM] * 8 + [VMEM] * 3,
            [jax.ShapeDtypeStruct(shape, F32), jax.ShapeDtypeStruct(shape, BF)],
            [
                pltpu.VMEM((32, 2 * PAD + 128, mine), BF),
                pltpu.VMEM((32 + 2 * REACH, 128, 3 * mine), BF),
                pltpu.VMEM((4, 128, feat), F32),
                pltpu.SemaphoreType.DMA((8,)),
            ],
            [info, *mains, *halos]
            + [masks[chosen[0] : chosen[0] + n], point_mine]
            + [forward_weights[chosen[0] : chosen[0] + n]],
        )

    keep_a, send_a = forward([0], True, True)
    got_a = swap(send_a, "x")
    keep_b, send_b = forward([1, 2], False, False)
    got_b = swap(send_b, "y")
    own_a = keep_a[0] + got_a[0].astype(F32)
    own_b = keep_b[0] + got_b[0].astype(F32)
    last_a = swap((keep_a[1] + got_a[1].astype(F32)).astype(BF), "y")
    last_b = swap((keep_b[1] + got_b[1].astype(F32)).astype(BF), "x")
    pair_a = (own_a + last_a.astype(F32)).reshape(pixels, 2 * feat)
    pair_b = (own_b + last_b.astype(F32)).reshape(pixels, 2 * feat)

    with jax.named_scope("across"):
        half = share // 2
        columns = []
        for x in range(2):
            for k in range(2):
                stack = []
                for y in range(2):
                    options = [
                        mains[dk * 4 + dy * 2 + dx] for dk in range(2) for dy in range(2) for dx in range(2)
                    ]
                    index = ((ik ^ k) * 4 + (iy ^ y) * 2 + (ix ^ x)).astype(jnp.int32)
                    stack.append(lax.select_n(index, *options))
                columns.append(jnp.concatenate(stack, axis=1))
        plane = jnp.concatenate(columns, axis=0).reshape(32, 2 * rows, zs, 2, half)
        plane = lax.dynamic_index_in_dim(plane, ik, 3, False)
        across = plane.reshape(32 * 2 * rows, mine // 2).T

    moments_mine = jnp.concatenate([moments(pair_a), moments(pair_b)], axis=1)
    first = allsum(moments_mine, axes)
    weighted = counts[:, None] * per_image
    pool_stats = jnp.stack([jnp.sum(weighted, axis=0), jnp.sum(weighted * per_image, axis=0)])
    four = 4 * feat
    flat_gain, flat_shift = bn_gain[:4].reshape(four), bn_shift[:4].reshape(four)
    mean = first[0] / total
    scale = lax.rsqrt(first[1] / total - mean * mean + EPSILON)
    normed = (jnp.concatenate([pair_a, pair_b], axis=1) - mean) * scale
    lifted = normed * flat_gain + flat_shift
    mean4 = pool_stats[0] / total
    scale4 = lax.rsqrt(pool_stats[1] / total - mean4 * mean4 + EPSILON)
    normed4 = (per_image - mean4) * scale4
    lifted4 = normed4 * bn_gain[4] + bn_shift[4]
    joined = smooth(lifted).astype(BF)
    joined4 = smooth(lifted4).astype(BF)
    table_float = table.astype(F32)
    head = dot(joined, project_weight[:four]) + exact(
        table_float, dot(joined4, project_weight[four:])
    )
    head_stats = allsum(moments(head), axes)
    head_mean = head_stats[0] / total
    head_scale = lax.rsqrt(head_stats[1] / total - head_mean * head_mean + EPSILON)
    head_norm = (head - head_mean) * head_scale
    head_lift = head_norm * bn_gain[5] + bn_shift[5]
    output = smooth(head_lift).astype(BF).reshape(cols, rows, feat).transpose(1, 0, 2)
    cotangent = out_grad.transpose(1, 0, 2).reshape(pixels, feat).astype(F32)
    head_grad = cotangent * smooth_slope(head_lift)
    head_back = allsum(
        jnp.stack([jnp.sum(head_grad, axis=0), jnp.sum(head_grad * head_norm, axis=0)]), axes
    )
    head_slope = (
        bn_gain[5]
        * head_scale
        * (head_grad - head_back[0] / total - head_norm * head_back[1] / total)
    ).astype(BF)
    joined_grad = lax.dot_general(
        head_slope, project_weight[:four], (((1,), (1,)), ((), ())), preferred_element_type=F32
    )
    grads = joined_grad * smooth_slope(lifted)
    image_heads = jnp.einsum(
        "pi,pf->if", table.astype(BF), head_slope, preferred_element_type=F32
    )
    rear = jnp.concatenate(
        [
            jnp.stack([jnp.sum(grads, axis=0), jnp.sum(grads * normed, axis=0)]).reshape(8, feat),
            image_heads,
        ],
        axis=0,
    )
    rear = allsum(rear, axes)
    shift_back, gain_back = rear[:4].reshape(four), rear[4:8].reshape(four)
    slopes = (
        flat_gain * scale * (grads - shift_back / total - normed * gain_back / total)
    ).astype(BF)

    with jax.named_scope("spread_slopes"):
        pieces = []
        for k in (0, 3, 2, 1):
            tile = slopes[:, k * feat : (k + 1) * feat].reshape(cols, rows, feat)
            brim = None if k == 0 else lax.ppermute(rim(tile), ("z", "y"), toward)
            sets = []
            for part in (tile, brim):
                if part is None:
                    sets.append([])
                    continue
                from_x, from_y = swap(part, "x"), swap(part, "y")
                cross_x = swap(from_y[: cols // 2], "x")
                cross_y = swap(from_x[cols // 2 :], "y")
                got = [part, from_x, from_y, jnp.concatenate([cross_x, cross_y], axis=0)]
                sets.append(got + [swap(g, "k") for g in got])
            pieces.append(sets)
        pieces = [pieces[0], pieces[3], pieces[2], pieces[1]]

    image_heads = rear[8:]
    grads4 = smooth_slope(lifted4) * exact(image_heads, project_weight[four:].astype(F32).T)
    shift4, gain4 = jnp.sum(grads4, axis=0), jnp.sum(grads4 * normed4, axis=0)
    image_slope = (
        bn_gain[4]
        * scale4
        * (grads4 - counts[:, None] * (shift4 / total + normed4 * gain4 / total))
    )
    image_low = image_slope.astype(BF)
    spread_back = (
        lax.dot_general(
            image_low, pool_mine, (((1,), (1,)), ((), ())), preferred_element_type=F32
        )
        / counts[:, None]
    )
    strip_table = (strip_plane[:, None] == image_range[None, :]).astype(F32)
    strip_back = exact(strip_table, spread_back)
    pooled_mine = lax.dynamic_slice_in_dim(pooled, iz * share + ik * half, half, 1)
    pool_part = jnp.einsum("ic,if->cf", pooled_mine, image_low, preferred_element_type=F32)

    def weight_grad(b, pointed):
        taps = 10 if pointed else 9
        main, halo = pieces[b + 1]
        extra = pieces[0][0] if pointed else []
        return call(
            partial(weight_kernel, spreads[b], pointed, feat),
            "weight_taps",
            2 * 4096 * (mine // 2) * 256 * 9,
            [SMEM] + [ANY] * 8 + [VMEM] * 8 + [ANY] * len(extra) + [VMEM] * 2,
            jax.ShapeDtypeStruct((zs, taps, half, feat), BF),
            [
                pltpu.VMEM((32, 2 * PAD + 128, feat), BF),
                pltpu.VMEM((32, 128, 3 * feat), BF),
                pltpu.VMEM((mine // 2, 4096), BF),
                pltpu.SemaphoreType.DMA((8,)),
            ],
            [info, *main, *halo, *extra, masks[b], across],
        )

    def collect(part, extra=None):
        done = lax.psum_scatter(part, "z", scatter_dimension=0, tiled=True)[0]
        if extra is not None:
            done = jnp.concatenate([done, extra[None].astype(BF)], axis=0)
        pair = jnp.stack([done, swap(done, "x")])
        both = jnp.stack([pair, swap(pair, "k")], axis=1)
        both = jnp.stack([pick(both[:, 0], both[:, 1], ik), pick(both[:, 1], both[:, 0], ik)], 1)
        both = jnp.stack([pick(both[0], both[1], ix), pick(both[1], both[0], ix)])
        taps = done.shape[0]
        return both.transpose(2, 0, 1, 3, 4).reshape(taps, 4 * half, feat).astype(F32)

    part3 = weight_grad(2, False)
    part2 = weight_grad(1, False)
    part1 = weight_grad(0, True)
    grad3 = collect(part3)
    grad2 = collect(part2)
    grad1 = collect(part1, pool_part)
    atrous_grad = jnp.concatenate([grad1[:9], grad2, grad3], axis=0)
    atrous_grad = atrous_grad.reshape(3, 3, 3, 4 * half, feat)
    point_grad, pool_grad = grad1[9], grad1[10]

    with jax.named_scope("input_grad"):
        shape = jax.ShapeDtypeStruct((cols, rows, mine), BF)
        mains_back = [m for p in pieces for m in p[0]]
        halos_back = [h for p in pieces[1:] for h in p[1]]
        own, to_x, to_y, to_d = call(
            partial(input_kernel, spreads, feat),
            "input_taps",
            2 * 2048 * mine * 256 * 28,
            [SMEM] + [ANY] * 32 + [VMEM] * 24 + [VMEM] * 5,
            [shape] * 4,
            [
                pltpu.VMEM((32, 2 * PAD + 128, feat), BF),
                pltpu.VMEM((32 + 2 * REACH, 128, 3 * feat), BF),
                pltpu.VMEM((4, 4, 128, mine), F32),
                pltpu.SemaphoreType.DMA((8,)),
            ],
            [info, *mains_back, *halos_back, masks, point_back, back_weights]
            + [spread_back[:1], strip_back],
        )
        got = [own, swap(to_x, "x"), swap(to_y, "y")]
        got.append(lax.ppermute(to_d, ("y", "x"), [(i, 3 - i) for i in range(4)]))
        planes = []
        for y in range(2):
            for x in range(2):
                index = ((iy ^ y) * 2 + (ix ^ x)).astype(jnp.int32)
                planes.append(lax.select_n(index, *got).reshape(cols, rows, zs, share))
        input_grad = jnp.stack(planes, axis=3).reshape(cols, rows, chans).transpose(1, 0, 2)

    project_part = lax.dot_general(
        joined, head_slope, (((0,), (0,)), ((), ())), preferred_element_type=F32
    )
    project_sum = lax.psum(project_part, axes)
    project_pool = lax.dot_general(
        joined4.astype(F32),
        image_heads,
        (((0,), (0,)), ((), ())),
        precision=lax.Precision.HIGHEST,
    )
    project_grad = jnp.concatenate([project_sum, project_pool], axis=0)
    gain_grad = jnp.concatenate([rear[4:8], gain4[None], head_back[1][None]], axis=0)
    shift_grad = jnp.concatenate([rear[:4], shift4[None], head_back[0][None]], axis=0)
    return (
        output,
        input_grad,
        point_grad,
        atrous_grad,
        pool_grad,
        project_grad,
        gain_grad,
        shift_grad,
    )


def solution(mesh):
    row, col = mesh.devices.shape
    fine = Mesh(mesh.devices.reshape(row // 2, 2, col // 2, 2), ("z", "y", "x", "k"))
    rows, cols = ("z", "y"), ("x", "k")
    placed = (
        P(rows, cols, None),
        P(rows, cols),
        P(),
        P(),
        P(),
        P(),
        P(),
        P(),
        P(rows, cols, None),
    )
    return jax.shard_map(
        per_device,
        mesh=fine,
        in_specs=placed,
        out_specs=(
            P(rows, cols, None),
            P(rows, cols, None),
            P(rows, None),
            P(None, None, None, rows, None),
            P(rows, None),
            P(),
            P(),
            P(),
        ),
        check_vma=False,
    )
```

```python
from functools import partial

import jax
import jax.numpy as jnp
from jax import lax
from jax.experimental import pallas as pl
from jax.experimental.pallas import tpu as pltpu
from jax.sharding import Mesh, PartitionSpec as P

REACH = 18
IMG_ROWS = 32
EPSILON = 1e-05
PAD = 32
SWAP = [(0, 1), (1, 0)]
BF = jnp.bfloat16
F32 = jnp.float32
VMEM_LIMIT = 60 * 2**20


def dot(a, b):
    return jnp.dot(a, b, preferred_element_type=F32)


def exact(a, b):
    return jnp.dot(a, b, precision=lax.Precision.HIGHEST, preferred_element_type=F32)


def swap(x, axis):
    return lax.ppermute(x, axis, SWAP)


def crossed(x):
    return lax.ppermute(x, ("y", "x"), [(i, 3 - i) for i in range(4)])


def quad(x, axes):
    near, far, last = (
        lax.ppermute(x, axes, [(i, i ^ step) for i in range(4)]) for step in (1, 2, 3)
    )
    return (x + near) + (far + last)


def z_sum(x):
    count = lax.axis_size("z")
    if count == 4:
        return quad(x, "z")
    step = 1
    while step < count:
        x = x + lax.ppermute(x, "z", [(i, i ^ step) for i in range(count)])
        step *= 2
    return x


def plane_sum(x):
    return quad(x, ("y", "x"))


def allsum(x):
    x = plane_sum(z_sum(x))
    return x + swap(x, "k")


def smooth(value):
    return jax.nn.gelu(value, approximate=True)


def smooth_slope(value):
    root = 0.7978845608028654
    square = value * value
    tanh = jnp.tanh(root * (value + 0.044715 * value * square))
    return 0.5 * (1.0 + tanh) + 0.5 * value * (1.0 - tanh * tanh) * root * (
        1.0 + 3 * 0.044715 * square
    )


def moments(value):
    return jnp.stack([jnp.sum(value, axis=0), jnp.sum(value * value, axis=0)])


def place_of(info, n):
    dk, dy, dx = n // 4, n // 2 % 2, n % 2
    col = ((info[1] ^ dx) * 2 + (info[2] ^ dk)) * 8
    return REACH + col, info[0] ^ dy


def tile_copies(info, tiles, window, sems, lane=0):
    width = window.shape[-1]
    copies = []
    for n, tile in enumerate(tiles):
        col, y = place_of(info, n)
        row = pl.multiple_of(PAD + y * 64, 16)
        copies.append(
            pltpu.make_async_copy(
                tile.at[:, pl.ds(0, 64), pl.ds(lane, width)],
                window.at[pl.ds(col, 8), pl.ds(row, 64)],
                sems.at[n],
            )
        )
        rim = tile.shape[1] - 64
        if rim:
            row = pl.multiple_of(jnp.where(y == 0, PAD + 128, PAD - rim), 16)
            copies.append(
                pltpu.make_async_copy(
                    tile.at[:, pl.ds(64, rim), pl.ds(lane, width)],
                    window.at[pl.ds(col, 8), pl.ds(row, rim)],
                    sems.at[8 + n],
                )
            )
    for copy in copies:
        copy.start()
    return copies


def place_rims(info, rims, window):
    for dk, rim in enumerate(rims):
        for n in range(4):
            col = REACH + ((n % 2) * 2 + (info[2] ^ dk)) * 8
            row = PAD + 128 if n < 2 else PAD - REACH
            for q in range(8):
                window[col + q, row : row + REACH, :] = rim[n, q]


def shift_rows(window, masks, b, q, i, spread, sign, cut, ok=None):
    start = PAD + sign * (i - 1) * spread
    value = window[REACH + q, start : start + 128, :]
    if i != 1:
        keep = masks[b, 1 if sign * (i - 1) > 0 else 0]
        keep = jnp.where(q >= cut, keep, jnp.ones_like(keep))
        if ok is not None:
            keep = jnp.where(ok, keep, jnp.zeros_like(keep))
        value = value * jnp.concatenate([keep] * (value.shape[1] // 128), axis=1)
    elif ok is not None:
        value = jnp.where(ok, value, jnp.zeros_like(value))
    return value


def tap_rows(window, masks, b, col, width, spread, sign, cut):
    return jnp.concatenate(
        [
            jnp.concatenate(
                [shift_rows(window, masks, b, col + u, i, spread, sign, cut) for i in range(3)],
                axis=1,
            )
            for u in range(width)
        ],
        axis=0,
    )


def branch_sum(window, masks, b, col, spread, sign, cut, product, acc, fresh):
    width = 2

    def inside(j, e):
        source = col + e + sign * (j - 1) * spread
        return (source >= 0) & (source < 32) & ((source < cut) == (col + e < cut))

    def center(e):
        return product(1, tap_rows(window, masks, b, col + e, width, spread, sign, cut))

    def side(j, e):
        source = col + e + sign * (j - 1) * spread
        part = product(j, tap_rows(window, masks, b, source, width, spread, sign, cut))
        return jnp.concatenate(
            [
                jnp.where(inside(j, e + u), part[u * 128 : u * 128 + 128], 0.0)
                for u in range(width)
            ],
            axis=0,
        )

    def put(e, value, first):
        value = value.reshape(width, 128, acc.shape[-1])
        if first:
            acc[e : e + width] = value
        else:
            acc[e : e + width] += value

    dense = spread == REACH // 3
    for e in range(0, 8, width):
        value = center(e)
        if dense:
            value = value + side(0, e) + side(2, e)
        put(e, value, fresh)
    if dense:
        return
    for j in (0, 2):
        some = inside(j, 0)
        for e in range(1, 8):
            some = some | inside(j, e)

        @pl.when(some)
        def _(j=j):
            for e in range(0, 8, width):
                put(e, side(j, e), False)


def forward_kernel(units, spreads, lanes, info, *refs):
    mains, rims = refs[:8], refs[8:10]
    masks, point, weights = refs[10:13]
    outs = refs[13:17]
    window, point_buf, weight_buf, acc, sems, weight_sems = refs[17:]
    iy, ix, ik, cut = info[0], info[1], info[2], info[3]
    copies = tile_copies(info, mains, window, sems)
    loads = []
    for n, b in enumerate(units):
        if b is None:
            loads.append(
                [pltpu.make_async_copy(point.at[:, iy, ix], point_buf, weight_sems.at[n, 0])]
            )
        else:
            loads.append(
                [
                    pltpu.make_async_copy(
                        weights.at[b, i, j, :, iy, ix],
                        weight_buf.at[n, j, i],
                        weight_sems.at[n, 3 * j + i],
                    )
                    for j in range(3)
                    for i in range(3)
                ]
            )
        for copy in loads[n]:
            copy.start()
    place_rims(info, rims, window)
    for copy in copies:
        copy.wait()
    for n, b in enumerate(units):
        for copy in loads[n]:
            copy.wait()
        keep, send = outs[2 * n : 2 * n + 2]
        for dx in (1, 0):
            col = (ix ^ dx) * 16 + ik * 8
            if b is None:
                source = window[pl.ds(REACH + col, 8), PAD : PAD + 128, :].reshape(1024, lanes)
                acc[...] = dot(source, point_buf[...].reshape(lanes, 256)).reshape(8, 128, 256)
            else:

                def product(j, rows, n=n):
                    return dot(rows, weight_buf[n, j].reshape(3 * lanes, 256))

                branch_sum(window, masks, b, col, spreads[b], 1, cut, product, acc, True)
            for dy in range(2):
                row = pl.multiple_of((iy ^ dy) * 64, 64)
                value = acc[:, pl.ds(row, 64), :]
                if (dy if n else dx) == 0:
                    keep[dx if n else dy] = value
                else:
                    send[dx if n else dy] = value.astype(BF)


def input_kernel(chosen, spreads, lanes, pointed, info, *refs):
    count = 8 * (1 + max(c[1] for c in chosen))
    tiles, masks, point, weights = refs[:count], refs[count], refs[count + 1], refs[count + 2]
    rest = refs[count + 3 :]
    if pointed:
        before, edge, strip = rest[:3]
        outs = rest[3:7]
        windows, weight_buf, point_buf, acc, sems, weight_sems = rest[7:]
    else:
        (result,) = rest[:1]
        windows, weight_buf, sems, weight_sems = rest[1:]
        acc = result
    iy, ix, ik, cut = info[0], info[1], info[2], info[3]
    mine = acc.shape[-1]
    fetches, loads = [], []
    for n, (b, first, lane) in enumerate(chosen):
        group = tiles[8 * first : 8 * first + 8]
        fetches.append(tile_copies(info, group, windows.at[n], sems.at[n], lane))
        if b is None:
            loads.append(
                [pltpu.make_async_copy(point.at[:, iy, ix], point_buf, weight_sems.at[n, 0])]
            )
        else:
            loads.append(
                [
                    pltpu.make_async_copy(
                        weights.at[b, i, j, :, iy, ix],
                        weight_buf.at[n, j, :, :, pl.ds(i * lanes, lanes)],
                        weight_sems.at[n, 3 * j + i],
                    )
                    for j in range(3)
                    for i in range(3)
                ]
            )
        for copy in loads[n]:
            copy.start()

    def times(a, w):
        return lax.dot_general(
            a, w.reshape(mine, w.shape[-1]), (((1,), (1,)), ((), ())), preferred_element_type=F32
        )

    for n, (b, _, _) in enumerate(chosen):
        for copy in fetches[n] + loads[n]:
            copy.wait()
        window = windows.at[n]
        for dx in range(2):
            col = (ix ^ dx) * 16 + ik * 8
            if b is None:
                for e in range(0, 8, 2):
                    source = window[pl.ds(REACH + col + e, 2), PAD : PAD + 128, :]
                    value = times(source.reshape(256, lanes), point_buf[...])
                    for u in range(2):
                        pool = jnp.where(col + e + u < cut, edge[...], strip[...])
                        acc[dx, e + u] += (
                            before[dx, e + u] + value[u * 128 : u * 128 + 128] + pool
                        )
            else:

                def product(j, rows, n=n):
                    return times(rows, weight_buf[n, j])

                branch_sum(
                    window, masks, b, col, spreads[b], -1, cut, product, acc.at[dx], n == 0
                )
    if pointed:
        for dx in range(2):
            for dy in range(2):
                row = pl.multiple_of((iy ^ dy) * 64, 64)
                outs[dy * 2 + dx][...] = acc[dx, :, pl.ds(row, 64), :].astype(BF)


def weight_kernel(spread, b, sources, lanes, info, *refs):
    tiles = refs[:8]
    masks, across = refs[8:10]
    outs = refs[10:-4]
    windows, out, sems, out_sems = refs[-4:]
    cut = info[3]
    parts = out.shape[0]
    each = out.shape[2]
    paired = len(outs) == 2
    fetches = [
        tile_copies(info, tiles, windows.at[n], sems.at[n], lane)
        for n, lane in enumerate(sources)
    ]

    def emit(t, value):
        for z in range(parts):
            out[info[4] ^ z if paired else z, t] = value[z * each : (z + 1) * each].astype(BF)

    for copy in fetches[0]:
        copy.wait()
    window = windows.at[0]
    for j in (1, 0, 2):
        move = (j - 1) * spread
        columns = [p for p in range(32) if 0 <= p + move < 32]
        total = None
        for at in range(0, len(columns), 8):
            group = columns[at : at + 8]
            right = []
            for p in group:
                ok = None if j == 1 else ((p < cut) == (p + move < cut))
                right.append(
                    jnp.concatenate(
                        [shift_rows(window, masks, b, p, i, spread, -1, cut, ok) for i in range(3)],
                        axis=1,
                    )
                )
            first, last = (group[0] + move) * 128, (group[-1] + move + 1) * 128
            part = dot(across[:, first:last], jnp.concatenate(right, axis=0))
            total = part if total is None else total + part
        for i in range(3):
            emit(3 * i + j, total[:, i * lanes : (i + 1) * lanes])
    if len(sources) > 1:
        for copy in fetches[1]:
            copy.wait()
        plain = windows[1, REACH : REACH + 32, PAD : PAD + 128, :].reshape(32 * 128, lanes)
        emit(9, dot(across[...], plain))
    if paired:
        moves = [(0, outs[0].at[0]), (3, outs[0].at[1]), (1, outs[1].at[0]), (2, outs[1].at[1])]
        moves = [(out.at[m], target) for m, target in moves]
    else:
        moves = [(out, outs[0])]
    copies = [
        pltpu.make_async_copy(source, target, out_sems.at[n])
        for n, (source, target) in enumerate(moves)
    ]
    for copy in copies:
        copy.start()
    for copy in copies:
        copy.wait()


def collect_kernel(first, count, extra, info, *refs):
    pieces = refs[:4]
    outs = refs[len(refs) - 3 - extra : len(refs) - 2]
    buf, sem = refs[len(refs) - 2 :]
    ix, ik = info[1], info[2]
    for n, piece in enumerate(pieces):
        index = (ix ^ (n // 2)) * 2 + (ik ^ (n % 2))
        for t in range(count):
            buf[t, index] = piece[t].astype(F32)
        for e in range(extra):
            outs[1 + e][index] = piece[count + e].astype(F32)
    copy = pltpu.make_async_copy(buf, outs[0].at[pl.ds(first, count)], sem)
    copy.start()
    copy.wait()


def pack_kernel(share, info, full, *refs):
    iy, ix = info[0], info[1]
    rims = refs[4]
    for n in range(4):
        other = (iy ^ (n // 2)) * 2 + (ix ^ (n % 2))
        for z in range(full.shape[-1] // (4 * share)):
            lane = pl.multiple_of((z * 4 + other) * share, 128)
            value = full[:, :, pl.ds(lane, share)]
            refs[n][:, :, z * share : (z + 1) * share] = value

            @pl.when(iy == 0)
            def _(value=value, other=other, z=z):
                rims[other, :, :, z * share : (z + 1) * share] = value[:, :REACH]

            @pl.when(iy == 1)
            def _(value=value, other=other, z=z):
                rims[other, :, :, z * share : (z + 1) * share] = value[:, 64 - REACH :]


def unpack_kernel(share, info, *refs):
    iy, ix = info[0], info[1]
    full = refs[4]
    for n in range(4):
        other = (iy ^ (n // 2)) * 2 + (ix ^ (n % 2))
        for z in range(full.shape[-1] // (4 * share)):
            lane = pl.multiple_of((z * 4 + other) * share, 128)
            full[:, :, pl.ds(lane, share)] = refs[n][:, :, z * share : (z + 1) * share]


def across_kernel(share, info, *refs):
    tiles, out, rows, zero = refs[:8], *refs[8:11]
    window, acc, sems = refs[11:]
    ik, cut = info[2], info[3]
    for copy in tile_copies(info, tiles, window, sems):
        copy.wait()
    acc[...] = jnp.zeros_like(acc)
    for q in range(32):
        value = window[REACH + q, PAD : PAD + 128, :]
        turned = value.T
        for z in range(turned.shape[0] // share):
            low = turned[z * share : z * share + share // 2]
            high = turned[z * share + share // 2 : (z + 1) * share]
            out[z * share // 2 : (z + 1) * share // 2, q * 128 : (q + 1) * 128] = jnp.where(
                ik == 0, low, high
            )
        acc[(q >= cut).astype(jnp.int32)] += value.astype(F32)
    rows[...] = acc[1]
    zero[...] = jnp.sum(acc[0], axis=0, keepdims=True)


VMEM = pl.BlockSpec(memory_space=pltpu.VMEM)
SMEM = pl.BlockSpec(memory_space=pltpu.SMEM)
ANY = pl.BlockSpec(memory_space=pl.ANY)


def call(kernel, name, flops, in_specs, out_shape, scratch, args, out_specs=None, aliases=None):
    return pl.pallas_call(
        kernel,
        name=name,
        in_specs=in_specs,
        out_specs=out_specs or jax.tree.map(lambda _: VMEM, out_shape),
        out_shape=out_shape,
        input_output_aliases=aliases or {},
        scratch_shapes=scratch,
        compiler_params=pltpu.CompilerParams(vmem_limit_bytes=VMEM_LIMIT),
        cost_estimate=pl.CostEstimate(flops=flops, bytes_accessed=10**7, transcendentals=0),
    )(*args)


def per_device(
    feature_map,
    image_ids,
    point_weight,
    atrous_weight,
    pool_weight,
    project_weight,
    bn_gain,
    bn_shift,
    out_grad,
):
    rows, cols, chans = feature_map.shape
    feat = point_weight.shape[1]
    pixels = rows * cols
    zs = lax.axis_size("z")
    axes = ("k", "x", "y", "z")
    iz, iy, ix, ik = (lax.axis_index(a) for a in ("z", "y", "x", "k"))
    row_count = 2 * zs
    total = float(pixels * row_count * 4)
    images = rows * row_count // IMG_ROWS + 1
    share = chans // (4 * zs)
    mine = chans // 4
    spreads = [REACH * (b + 1) // 3 for b in range(3)]
    def pick(first, second, index):
        return jnp.where(index == 0, first, second)

    def rim(x, depth):
        return pick(x[:, :depth], x[:, rows - depth :], iy)

    def beyond(x, dy, dx):
        pairs = []
        for z in range(zs):
            for y in range(2):
                far = z - 1 + 2 * y
                if 0 <= far < zs:
                    for i in range(2):
                        target = (far * 2 + (y ^ dy)) * 2 + (i ^ dx)
                        pairs.append(((z * 2 + y) * 2 + i, target))
        return lax.ppermute(x, ("z", "y", "x"), pairs)

    with jax.named_scope("marks"):
        strip_own = jnp.max(image_ids, axis=1)
        zero_own = jnp.sum((image_ids[0] == 0).astype(jnp.int32))
        both = jnp.concatenate([strip_own, zero_own[None]])
        others = [
            lax.ppermute(both, ("x", "k"), [(i, i ^ step) for i in range(4)]) for step in (1, 2, 3)
        ]
        for other in others:
            strip_own = jnp.maximum(strip_own, other[:rows])
            zero_own = zero_own + other[rows]
        cut = zero_own
    places = jnp.stack([iy, ix, ik, ik, iz]).astype(jnp.int32)
    turned = feature_map.transpose(1, 0, 2)
    aligned = share % 128 == 0
    with jax.named_scope("spread_features"):
        if aligned:
            tile_shape = jax.ShapeDtypeStruct((cols, rows, mine), BF)
            *tiles, brims = call(
                partial(pack_kernel, share),
                "pack",
                0,
                [SMEM, VMEM],
                [tile_shape] * 4 + [jax.ShapeDtypeStruct((4, cols, REACH, mine), BF)],
                [],
                [places, turned],
            )
        else:
            packed = turned.reshape(cols, rows, zs, 2, 2, share).transpose(3, 4, 0, 1, 2, 5)
            packed = packed.reshape(4, cols, rows, mine)
            tiles = [
                lax.dynamic_index_in_dim(packed, (iy ^ dy) * 2 + (ix ^ dx), 0, False)
                for dy in range(2)
                for dx in range(2)
            ]
            brims = pick(packed[:, :, :REACH], packed[:, :, rows - REACH :], iy)
        halo = lax.all_to_all(beyond(brims, 0, 0), ("y", "x"), 0, 0)
        halos = [halo, swap(halo, "k")]
        own, to_x, to_y, to_d = tiles
        mains = [own, swap(to_x, "x"), swap(to_y, "y"), crossed(to_d)]

    with jax.named_scope("marks"):
        strip_own, mains[1] = lax.optimization_barrier((strip_own, mains[1]))
        edge_own = pick(strip_own[:REACH], strip_own[rows - REACH :], iy)
        edge, cross = beyond(edge_own, 0, 0), beyond(edge_own, 1, 0)
        other = swap(strip_own, "y")
    mains = mains + [swap(g, "k") for g in mains]
    with jax.named_scope("marks"):
        strip_plane = jnp.concatenate([pick(strip_own, other, iy), pick(other, strip_own, iy)])
        top, bottom = pick(cross, edge, iy), pick(edge, cross, iy)
        strip_tall = jnp.concatenate([top, strip_plane, bottom])
        masks = jnp.stack(
            [
                jnp.stack(
                    [
                        strip_plane
                        == lax.slice_in_dim(strip_tall, REACH + s * d, REACH + s * d + 2 * rows)
                        for s in (-1, 1)
                    ]
                )
                for d in spreads
            ]
        )
        masks = jnp.broadcast_to(masks[..., None], (3, 2, 2 * rows, 128)).astype(BF)
        info = jnp.stack([iy, ix, ik, cut, iz]).astype(jnp.int32)


    local_ids = image_ids.T.reshape(pixels)
    image_range = jnp.arange(images, dtype=jnp.int32)
    table = local_ids[:, None] == image_range[None, :]

    point_view = point_weight.reshape(zs, 2, 2, share, feat)
    atrous_view = atrous_weight.reshape(3, 3, 3, zs, 2, 2, share, feat)

    def forward(units):
        shape = (2, cols, rows, feat)
        return call(
            partial(forward_kernel, units, spreads, mine),
            "forward_taps",
            2 * 2048 * mine * 256 * 15,
            [SMEM] + [ANY] * 8 + [VMEM] * 3 + [ANY] * 2,
            [jax.ShapeDtypeStruct(shape, F32), jax.ShapeDtypeStruct(shape, BF)] * 2,
            [
                pltpu.VMEM((32 + 2 * REACH, 2 * PAD + 128, mine), BF),
                pltpu.VMEM((zs, share, feat), BF),
                pltpu.VMEM((2, 3, 3, zs, share, feat), BF),
                pltpu.VMEM((8, 128, feat), F32),
                pltpu.SemaphoreType.DMA((16,)),
                pltpu.SemaphoreType.DMA((2, 9)),
            ],
            [info, *mains, *halos, masks, point_view, atrous_view],
        )

    def reduce_first(parts):
        keep_x, send_x, keep_y, send_y = parts
        return keep_x, swap(send_x, "x"), keep_y, swap(send_y, "y")

    def reduce_middle(parts):
        keep_x, got_x, keep_y, got_y = parts
        more_x = (keep_x[1] + got_x[1].astype(F32)).astype(BF)
        more_y = (keep_y[1] + got_y[1].astype(F32)).astype(BF)
        return more_x, more_y

    def reduce_last(parts, last_x, last_y):
        keep_x, got_x, keep_y, got_y = parts
        value_x = keep_x[0] + got_x[0].astype(F32) + last_x.astype(F32)
        value_y = keep_y[0] + got_y[0].astype(F32) + last_y.astype(F32)
        return [value_x.reshape(pixels, feat), value_y.reshape(pixels, feat)]

    early = forward([None, 0])
    early_got = reduce_first(early)
    late = forward([1, 2])
    early_got, late = lax.optimization_barrier((early_got, late))
    late_got = reduce_first(late)
    early_more = reduce_middle(early_got)
    early_last = [swap(early_more[0], "y"), swap(early_more[1], "x")]

    half = share // 2
    strip_table = strip_plane[:, None] == image_range[None, :]
    with jax.named_scope("across"):
        mains_late, early_last = lax.optimization_barrier((mains, early_last))
        if aligned:
            across, row_sums, zero_sums = call(
                partial(across_kernel, share),
                "across",
                2 * 10**9,
                [SMEM] + [ANY] * 8,
                [
                    jax.ShapeDtypeStruct((mine // 2, 32 * 2 * rows), BF),
                    jax.ShapeDtypeStruct((2 * rows, mine), F32),
                    jax.ShapeDtypeStruct((1, mine), F32),
                ],
                [
                    pltpu.VMEM((32 + 2 * REACH, 2 * PAD + 128, mine), BF),
                    pltpu.VMEM((2, 2 * rows, mine), F32),
                    pltpu.SemaphoreType.DMA((16,)),
                ],
                [info, *mains_late],
            )
        else:
            columns = []
            for x in range(2):
                for k in range(2):
                    index = [(ik ^ k) * 4 + (iy ^ y) * 2 + (ix ^ x) for y in range(2)]
                    stack = [lax.select_n(n.astype(jnp.int32), *mains_late) for n in index]
                    columns.append(jnp.concatenate(stack, axis=1))
            plane = jnp.concatenate(columns, axis=0)
            in_strip = (jnp.arange(32) >= cut)[:, None, None]
            row_sums = jnp.sum(jnp.where(in_strip, plane.astype(F32), 0.0), axis=0)
            zero_sums = jnp.sum(jnp.where(in_strip, 0.0, plane.astype(F32)), axis=(0, 1))[None]
            plane = plane.reshape(32, 2 * rows, zs, 2, half)
            plane = lax.dynamic_index_in_dim(plane, ik, 3, False)
            across = plane.reshape(32 * 2 * rows, mine // 2).T

    with jax.named_scope("image_sums"):
        sums = lax.dot_general(
            strip_table.astype(F32),
            row_sums,
            (((0,), (0,)), ((), ())),
            precision=lax.Precision.HIGHEST,
        )
        sums = jnp.where(image_range[:, None] == 0, zero_sums, sums)
        strip_rows = jnp.sum(strip_table.astype(F32), axis=0)
        tall = jnp.concatenate(
            [sums, jnp.broadcast_to(strip_rows[:, None], (images, 128))], axis=1
        )
        tall = z_sum(tall)
        image_sums = tall[:, :mine]
        whole = 4 * cols
        counts = jnp.where(
            image_range == 0,
            (cut * (rows * row_count)).astype(F32),
            tall[:, mine] * (whole - cut).astype(F32),
        )
        pooled = (image_sums / counts[:, None]).astype(BF)
        pool_mine = pool_weight.reshape(zs, 2, 2, share, feat)
        pool_mine = lax.dynamic_slice(
            pool_mine, (0, iy, ix, 0, 0), (zs, 1, 1, share, feat)
        ).reshape(mine, feat)
        per_image = plane_sum(dot(pooled, pool_mine))

    late_got, across = lax.optimization_barrier((late_got, across))
    late_more = reduce_middle(late_got)
    branches = reduce_last(early_got, *early_last)
    branches += reduce_last(late_got, swap(late_more[0], "y"), swap(late_more[1], "x"))

    moments_mine = jnp.concatenate([moments(value) for value in branches], axis=1)
    first = allsum(moments_mine)
    weighted = counts[:, None] * per_image
    pool_stats = jnp.stack([jnp.sum(weighted, axis=0), jnp.sum(weighted * per_image, axis=0)])
    four = 4 * feat
    flat_gain, flat_shift = bn_gain[:4].reshape(four), bn_shift[:4].reshape(four)
    mean = first[0] / total
    scale = lax.rsqrt(first[1] / total - mean * mean + EPSILON)
    normed = (jnp.concatenate(branches, axis=1) - mean) * scale
    lifted = normed * flat_gain + flat_shift
    mean4 = pool_stats[0] / total
    scale4 = lax.rsqrt(pool_stats[1] / total - mean4 * mean4 + EPSILON)
    normed4 = (per_image - mean4) * scale4
    lifted4 = normed4 * bn_gain[4] + bn_shift[4]
    joined = smooth(lifted).astype(BF)
    joined4 = smooth(lifted4).astype(BF)
    table_float = table.astype(F32)
    head = dot(joined, project_weight[:four]) + exact(
        table_float, dot(joined4, project_weight[four:])
    )
    head_stats = allsum(moments(head))
    head_mean = head_stats[0] / total
    head_scale = lax.rsqrt(head_stats[1] / total - head_mean * head_mean + EPSILON)
    head_norm = (head - head_mean) * head_scale
    head_lift = head_norm * bn_gain[5] + bn_shift[5]
    output = smooth(head_lift).astype(BF).reshape(cols, rows, feat).transpose(1, 0, 2)
    cotangent = out_grad.transpose(1, 0, 2).reshape(pixels, feat).astype(F32)
    head_grad = cotangent * smooth_slope(head_lift)
    head_back = allsum(
        jnp.stack([jnp.sum(head_grad, axis=0), jnp.sum(head_grad * head_norm, axis=0)])
    )
    head_slope = (
        bn_gain[5]
        * head_scale
        * (head_grad - head_back[0] / total - head_norm * head_back[1] / total)
    ).astype(BF)
    joined_grad = lax.dot_general(
        head_slope, project_weight[:four], (((1,), (1,)), ((), ())), preferred_element_type=F32
    )
    grads = joined_grad * smooth_slope(lifted)
    image_heads = jnp.einsum(
        "pi,pf->if", table.astype(BF), head_slope, preferred_element_type=F32
    )
    rear = jnp.concatenate(
        [
            jnp.stack([jnp.sum(grads, axis=0), jnp.sum(grads * normed, axis=0)]).reshape(8, feat),
            image_heads,
        ],
        axis=0,
    )
    rear = allsum(rear)
    shift_back, gain_back = rear[:4].reshape(four), rear[4:8].reshape(four)
    slopes = (
        flat_gain * scale * (grads - shift_back / total - normed * gain_back / total)
    ).astype(BF)

    with jax.named_scope("project_grad"):
        project_part = lax.dot_general(
            joined, head_slope, (((0,), (0,)), ((), ())), preferred_element_type=F32
        )

    with jax.named_scope("spread_slopes"):
        tiles_out = [
            slopes[:, first * feat : last * feat].reshape(cols, rows, -1)
            for first, last in ((3, 4), (2, 3), (0, 2))
        ]
        brim = beyond(rim(tiles_out[0], 32), 0, 0)
        brims = beyond(
            jnp.concatenate([rim(tiles_out[1], 16), rim(tiles_out[2], 16)], axis=2), 0, 0
        )
        def both_cores(got):
            return got + [swap(g, "k") for g in got]

        tile3 = jnp.concatenate([tiles_out[0], brim], axis=1)
        tile2 = jnp.concatenate([tiles_out[1], brims[:, :, :feat]], axis=1)
        tile1 = jnp.concatenate([tiles_out[2], brims[:, :, feat:]], axis=1)
        blocks = project_part.astype(BF).reshape(8, four // 8, feat)
        blocks, tile3 = lax.optimization_barrier((blocks, tile3))
        blocks = lax.all_to_all(blocks, ("y", "x", "k"), 0, 0)
        group3 = both_cores([tile3, swap(tile3, "x"), swap(tile3, "y"), crossed(tile3)])
        tile2, group3 = lax.optimization_barrier((tile2, group3))
        arrived2 = [tile2, swap(tile2, "x"), swap(tile2, "y"), crossed(tile2)]

    image_heads = rear[8:]
    grads4 = smooth_slope(lifted4) * exact(image_heads, project_weight[four:].astype(F32).T)
    shift4, gain4 = jnp.sum(grads4, axis=0), jnp.sum(grads4 * normed4, axis=0)
    image_slope = (
        bn_gain[4]
        * scale4
        * (grads4 - counts[:, None] * (shift4 / total + normed4 * gain4 / total))
    )
    image_low = image_slope.astype(BF)
    spread_back = (
        lax.dot_general(
            image_low, pool_mine, (((1,), (1,)), ((), ())), preferred_element_type=F32
        )
        / counts[:, None]
    )
    strip_back = exact(strip_table.astype(F32), spread_back)
    pooled_mine = lax.dynamic_slice_in_dim(pooled, iz * share + ik * half, half, 1)
    pool_part = jnp.einsum("ic,if->cf", pooled_mine, image_low, preferred_element_type=F32)

    def weight_grad(b, tiles, lanes_at):
        taps = 8 + len(lanes_at)
        return call(
            partial(weight_kernel, spreads[b], b, lanes_at, feat),
            "weight_taps",
            2 * 4096 * (mine // 2) * 256 * 15,
            [SMEM] + [ANY] * 8 + [VMEM] * 2,
            [jax.ShapeDtypeStruct((2, taps, half, feat), BF)] * 2
            if zs == 4
            else [jax.ShapeDtypeStruct((zs, taps, half, feat), BF)],
            [
                pltpu.VMEM((len(lanes_at), 32 + 2 * REACH, 2 * PAD + 128, feat), BF),
                pltpu.VMEM((zs, taps, half, feat), BF),
                pltpu.SemaphoreType.DMA((2, 16)),
                pltpu.SemaphoreType.DMA((4,)),
            ],
            [info, *tiles, masks, across],
            out_specs=[ANY] * (2 if zs == 4 else 1),
        )

    def z_scatter(part, behind):
        if zs != 4:
            return lax.psum_scatter(part[0], "z", scatter_dimension=0, tiled=True)[0].astype(F32)
        keep, send = part
        got = lax.ppermute(send, "z", [(i, i ^ 1) for i in range(4)])
        got, _ = lax.optimization_barrier((got, behind))
        more = (keep[1].astype(F32) + got[1].astype(F32)).astype(BF)
        last = lax.ppermute(more, "z", [(i, i ^ 3) for i in range(4)])
        return keep[0].astype(F32) + got[0].astype(F32) + last.astype(F32)

    def collect(part, first, extra, buffer, behind):
        done = z_scatter(part, behind)
        if extra is not None:
            done = jnp.concatenate([done, extra[None]], axis=0)
        done = done.astype(BF)
        from_x = swap(done, "x")
        pieces = [done, swap(done, "k"), from_x, swap(from_x, "k")]
        more = done.shape[0] - 9
        grad = jax.ShapeDtypeStruct((27, 4, half, feat), F32)
        side = jax.ShapeDtypeStruct((4, half, feat), F32)
        return call(
            partial(collect_kernel, first, 9, more),
            "collect",
            0,
            [SMEM] + [VMEM] * 4 + [ANY] * len(buffer),
            [grad] + [side] * more,
            [pltpu.VMEM((9, 4, half, feat), F32), pltpu.SemaphoreType.DMA],
            [places, *pieces, *buffer],
            out_specs=[ANY] + [VMEM] * more,
            aliases={5: 0} if buffer else {},
        )

    part3 = weight_grad(2, group3, [0])
    arrived2, part3 = lax.optimization_barrier((arrived2, part3))
    group2 = both_cores(arrived2)
    tile1, group2 = lax.optimization_barrier((tile1, group2))
    from_x, from_y = swap(tile1, "x"), swap(tile1, "y")
    part2 = weight_grad(1, group2, [0])
    from_x, from_y, part2 = lax.optimization_barrier((from_x, from_y, part2))
    cross_x = swap(from_y[: cols // 2], "x")
    cross_y = swap(from_x[cols // 2 :], "y")
    group2, part2 = lax.optimization_barrier((group2, part2))

    def input_part(chosen, groups, pointed, more, outs):
        n = len(chosen)
        scratch = [
            pltpu.VMEM((n, 32 + 2 * REACH, 2 * PAD + 128, feat), BF),
            pltpu.VMEM((n, 3, zs, share, 3 * feat), BF),
        ]
        if pointed:
            scratch += [pltpu.VMEM((zs, share, feat), BF), pltpu.VMEM((2, 8, 128, mine), F32)]
        scratch += [pltpu.SemaphoreType.DMA((n, 16)), pltpu.SemaphoreType.DMA((n, 9))]
        return call(
            partial(input_kernel, chosen, spreads, feat, pointed),
            "input_taps",
            2 * 2048 * mine * 256 * 20,
            [SMEM] + [ANY] * 8 * len(groups) + [VMEM] + [ANY] * 2 + [VMEM] * len(more),
            outs,
            scratch,
            [info, *[t for g in groups for t in g], masks, point_view, atrous_view, *more],
        )

    with jax.named_scope("input_grad"):
        sums_so_far = input_part(
            [(2, 0, 0), (1, 1, 0)],
            [group3, group2],
            False,
            [],
            jax.ShapeDtypeStruct((2, cols, 2 * rows, mine), F32),
        )
    cross_x, cross_y, sums_so_far = lax.optimization_barrier((cross_x, cross_y, sums_so_far))
    group1 = both_cores([tile1, from_x, from_y, jnp.concatenate([cross_x, cross_y], axis=0)])
    part1 = weight_grad(0, group1, [feat, 0])
    with jax.named_scope("input_grad"):
        group1, part1 = lax.optimization_barrier((group1, part1))
        shape = jax.ShapeDtypeStruct((cols, rows, mine), BF)
        own, to_x, to_y, to_d = input_part(
            [(0, 0, feat), (None, 0, 0)],
            [group1],
            True,
            [sums_so_far, spread_back[:1], strip_back],
            [shape] * 4,
        )
        got = [own, swap(to_x, "x"), swap(to_y, "y"), crossed(to_d)]
        if aligned:
            input_turned = call(
                partial(unpack_kernel, share),
                "unpack",
                0,
                [SMEM] + [VMEM] * 4,
                jax.ShapeDtypeStruct((cols, rows, chans), BF),
                [],
                [places, *got],
            )
        else:
            planes = []
            for y in range(2):
                for x in range(2):
                    index = ((iy ^ y) * 2 + (ix ^ x)).astype(jnp.int32)
                    planes.append(lax.select_n(index, *got).reshape(cols, rows, zs, share))
            input_turned = jnp.stack(planes, axis=3).reshape(cols, rows, chans)
        input_grad = input_turned.transpose(1, 0, 2)

    with jax.named_scope("project_grad"):
        blocks, _ = lax.optimization_barrier((blocks, part3))
        project_sum = z_sum(jnp.sum(blocks.astype(F32), axis=0)).astype(BF)
        project_sum, _ = lax.optimization_barrier((project_sum, sums_so_far))
        project_sum = lax.all_to_all(
            jnp.broadcast_to(project_sum[None], (8, four // 8, feat)), ("y", "x", "k"), 0, 0
        ).reshape(four, feat)
        project_pool = lax.dot_general(
            joined4.astype(F32),
            image_heads,
            (((0,), (0,)), ((), ())),
            precision=lax.Precision.HIGHEST,
        )
        project_grad = jnp.concatenate([project_sum.astype(F32), project_pool], axis=0)

    (grad,) = collect(part3, 18, None, [], part2)
    (grad,) = collect(part2, 9, None, [grad], sums_so_far)
    grad, point_grad, pool_grad = collect(part1, 0, pool_part, [grad], own)
    atrous_grad = grad.reshape(3, 3, 3, 4 * half, feat)
    point_grad, pool_grad = (v.reshape(4 * half, feat) for v in (point_grad, pool_grad))

    gain_grad = jnp.concatenate([rear[4:8], gain4[None], head_back[1][None]], axis=0)
    shift_grad = jnp.concatenate([rear[:4], shift4[None], head_back[0][None]], axis=0)
    return (
        output,
        input_grad,
        point_grad,
        atrous_grad,
        pool_grad,
        project_grad,
        gain_grad,
        shift_grad,
    )


def solution(mesh):
    row, col = mesh.devices.shape
    fine = Mesh(mesh.devices.reshape(row // 2, 2, col // 2, 2), ("z", "y", "x", "k"))
    rows, cols = ("z", "y"), ("x", "k")
    placed = (
        P(rows, cols, None),
        P(rows, cols),
        P(),
        P(),
        P(),
        P(),
        P(),
        P(),
        P(rows, cols, None),
    )
    return jax.shard_map(
        per_device,
        mesh=fine,
        in_specs=placed,
        out_specs=(
            P(rows, cols, None),
            P(rows, cols, None),
            P(rows, None),
            P(None, None, None, rows, None),
            P(rows, None),
            P(),
            P(),
            P(),
        ),
        check_vma=False,
    )
```

```python
from functools import partial

import jax
import jax.numpy as jnp
from jax import lax
from jax.experimental import pallas as pl
from jax.experimental.pallas import tpu as pltpu
from jax.sharding import Mesh, PartitionSpec as P

REACH = 18
IMG_ROWS = 32
EPSILON = 1e-05
PAD = 32
RIM = 24
SWAP = [(0, 1), (1, 0)]
BF = jnp.bfloat16
F32 = jnp.float32
VMEM_LIMIT = 60 * 2**20


def dot(a, b):
    return jnp.dot(a, b, preferred_element_type=F32)


def exact(a, b):
    return jnp.dot(a, b, precision=lax.Precision.HIGHEST, preferred_element_type=F32)


def gate(x, *deps):
    return lax.optimization_barrier((x, deps))[0]


def swap(x, axis):
    return lax.ppermute(x, axis, SWAP)


def z_swap(x, step):
    count = lax.axis_size("z")
    return lax.ppermute(x, "z", [(i, i ^ step) for i in range(count)])


def crossed(x):
    return lax.ppermute(x, ("y", "x"), [(i, 3 - i) for i in range(4)])


def quad(x, axes):
    near, far, last = (
        lax.ppermute(x, axes, [(i, i ^ step) for i in range(4)]) for step in (1, 2, 3)
    )
    return (x + near) + (far + last)


def z_sum(x):
    count = lax.axis_size("z")
    if count == 4:
        return quad(x, "z")
    step = 1
    while step < count:
        x = x + lax.ppermute(x, "z", [(i, i ^ step) for i in range(count)])
        step *= 2
    return x


def plane_sum(x):
    return quad(x, ("y", "x"))


def allsum(x):
    x = plane_sum(z_sum(x))
    return x + swap(x, "k")


def smooth(value):
    return jax.nn.gelu(value, approximate=True)


def smooth_slope(value):
    root = 0.7978845608028654
    square = value * value
    tanh = jnp.tanh(root * (value + 0.044715 * value * square))
    return 0.5 * (1.0 + tanh) + 0.5 * value * (1.0 - tanh * tanh) * root * (
        1.0 + 3 * 0.044715 * square
    )


def moments(value):
    return jnp.stack([jnp.sum(value, axis=0), jnp.sum(value * value, axis=0)])


def place_of(info, n):
    dk, dy, dx = n // 4, n // 2 % 2, n % 2
    col = ((info[1] ^ dx) * 2 + (info[2] ^ dk)) * 8
    return REACH + col, info[0] ^ dy


def tile_copies(info, tiles, window, sems, lane=0):
    width = window.shape[-1]
    copies = []
    for n, tile in enumerate(tiles):
        col, y = place_of(info, n)
        row = pl.multiple_of(PAD + y * 64, 16)
        copies.append(
            pltpu.make_async_copy(
                tile.at[:, pl.ds(0, 64), pl.ds(lane, width)],
                window.at[pl.ds(col, 8), pl.ds(row, 64)],
                sems.at[n],
            )
        )
        rim = tile.shape[1] - 64
        if rim:
            row = pl.multiple_of(jnp.where(y == 0, PAD + 128, PAD - rim), 16)
            copies.append(
                pltpu.make_async_copy(
                    tile.at[:, pl.ds(64, rim), pl.ds(lane, width)],
                    window.at[pl.ds(col, 8), pl.ds(row, rim)],
                    sems.at[8 + n],
                )
            )
    for copy in copies:
        copy.start()
    return copies


def place_rims(info, rims, window):
    for dk, rim in enumerate(rims):
        for n in range(4):
            col = REACH + ((n % 2) * 2 + (info[2] ^ dk)) * 8
            row = PAD + 128 if n < 2 else PAD - REACH
            for q in range(8):
                window[col + q, row : row + REACH, :] = rim[n, q, :REACH]


def shift_rows(window, masks, b, q, i, spread, sign, cut, ok=None):
    start = PAD + sign * (i - 1) * spread
    value = window[REACH + q, start : start + 128, :]
    if i != 1:
        keep = masks[b, 1 if sign * (i - 1) > 0 else 0]
        keep = jnp.where(q >= cut, keep, jnp.ones_like(keep))
        if ok is not None:
            keep = jnp.where(ok, keep, jnp.zeros_like(keep))
        value = value * jnp.concatenate([keep] * (value.shape[1] // 128), axis=1)
    elif ok is not None:
        value = jnp.where(ok, value, jnp.zeros_like(value))
    return value


def tap_rows(window, masks, b, col, width, spread, sign, cut):
    return jnp.concatenate(
        [
            jnp.concatenate(
                [shift_rows(window, masks, b, col + u, i, spread, sign, cut) for i in range(3)],
                axis=1,
            )
            for u in range(width)
        ],
        axis=0,
    )


def branch_sum(window, masks, b, col, spread, sign, cut, product, acc, fresh):
    width = 2

    def inside(j, e):
        source = col + e + sign * (j - 1) * spread
        return (source >= 0) & (source < 32) & ((source < cut) == (col + e < cut))

    def center(e):
        return product(1, tap_rows(window, masks, b, col + e, width, spread, sign, cut))

    def side(j, e):
        source = col + e + sign * (j - 1) * spread
        part = product(j, tap_rows(window, masks, b, source, width, spread, sign, cut))
        return jnp.concatenate(
            [
                jnp.where(inside(j, e + u), part[u * 128 : u * 128 + 128], 0.0)
                for u in range(width)
            ],
            axis=0,
        )

    def put(e, value, first):
        value = value.reshape(width, 128, acc.shape[-1])
        if first:
            acc[e : e + width] = value
        else:
            acc[e : e + width] += value

    dense = spread == REACH // 3
    for e in range(0, 8, width):
        value = center(e)
        if dense:
            value = value + side(0, e) + side(2, e)
        put(e, value, fresh)
    if dense:
        return
    for j in (0, 2):
        for half in (0, 4):
            some = inside(j, half)
            for e in range(1, 4):
                some = some | inside(j, half + e)

            @pl.when(some)
            def _(j=j, half=half):
                for e in range(half, half + 4, width):
                    put(e, side(j, e), False)


def forward_kernel(units, spreads, lanes, info, *refs):
    mains, rims = refs[:8], refs[8:10]
    masks, point, weights = refs[10:13]
    outs = refs[13:17]
    window, point_buf, weight_buf, acc, sems, weight_sems = refs[17:]
    iy, ix, ik, cut = info[0], info[1], info[2], info[3]
    copies = tile_copies(info, mains, window, sems)
    loads = []
    for n, b in enumerate(units):
        if b is None:
            loads.append(
                [pltpu.make_async_copy(point.at[:, iy, ix], point_buf, weight_sems.at[n, 0])]
            )
        else:
            loads.append(
                [
                    pltpu.make_async_copy(
                        weights.at[b, i, j, :, iy, ix],
                        weight_buf.at[n, j, i],
                        weight_sems.at[n, 3 * j + i],
                    )
                    for j in range(3)
                    for i in range(3)
                ]
            )
        for copy in loads[n]:
            copy.start()
    place_rims(info, rims, window)
    for copy in copies:
        copy.wait()
    for n, b in enumerate(units):
        for copy in loads[n]:
            copy.wait()
        keep, send = outs[2 * n : 2 * n + 2]
        for dx in (1, 0):
            col = (ix ^ dx) * 16 + ik * 8
            if b is None:
                source = window[pl.ds(REACH + col, 8), PAD : PAD + 128, :].reshape(1024, lanes)
                acc[...] = dot(source, point_buf[...].reshape(lanes, 256)).reshape(8, 128, 256)
            else:

                def product(j, rows, n=n):
                    return dot(rows, weight_buf[n, j].reshape(3 * lanes, 256))

                branch_sum(window, masks, b, col, spreads[b], 1, cut, product, acc, True)
            for dy in range(2):
                row = pl.multiple_of((iy ^ dy) * 64, 64)
                value = acc[:, pl.ds(row, 64), :]
                if (dy if n else dx) == 0:
                    keep[dx if n else dy] = value
                else:
                    send[dx if n else dy] = value.astype(BF)


def input_kernel(chosen, spreads, lanes, pointed, info, *refs):
    count = 8 * (1 + max(c[1] for c in chosen))
    tiles, masks, point, weights = refs[:count], refs[count], refs[count + 1], refs[count + 2]
    rest = refs[count + 3 :]
    if pointed:
        before, edge, strip = rest[:3]
        outs = rest[3:7]
        windows, weight_buf, point_buf, acc, sems, weight_sems = rest[7:]
    else:
        (result,) = rest[:1]
        windows, weight_buf, sems, weight_sems = rest[1:]
        acc = result
    iy, ix, ik, cut = info[0], info[1], info[2], info[3]
    mine = acc.shape[-1]
    fetches, loads = [], []
    for n, (b, first, lane) in enumerate(chosen):
        group = tiles[8 * first : 8 * first + 8]
        fetches.append(tile_copies(info, group, windows.at[n], sems.at[n], lane))
        if b is None:
            loads.append(
                [pltpu.make_async_copy(point.at[:, iy, ix], point_buf, weight_sems.at[n, 0])]
            )
        else:
            loads.append(
                [
                    pltpu.make_async_copy(
                        weights.at[b, i, j, :, iy, ix],
                        weight_buf.at[n, j, :, :, pl.ds(i * lanes, lanes)],
                        weight_sems.at[n, 3 * j + i],
                    )
                    for j in range(3)
                    for i in range(3)
                ]
            )
        for copy in loads[n]:
            copy.start()

    def times(a, w):
        return lax.dot_general(
            a, w.reshape(mine, w.shape[-1]), (((1,), (1,)), ((), ())), preferred_element_type=F32
        )

    for n, (b, _, _) in enumerate(chosen):
        for copy in fetches[n] + loads[n]:
            copy.wait()
        window = windows.at[n]
        for dx in range(2):
            col = (ix ^ dx) * 16 + ik * 8
            if b is None:
                for e in range(0, 8, 2):
                    source = window[pl.ds(REACH + col + e, 2), PAD : PAD + 128, :]
                    value = times(source.reshape(256, lanes), point_buf[...])
                    for u in range(2):
                        pool = jnp.where(col + e + u < cut, edge[...], strip[...])
                        acc[dx, e + u] += (
                            before[dx, e + u] + value[u * 128 : u * 128 + 128] + pool
                        )
            else:

                def product(j, rows, n=n):
                    return times(rows, weight_buf[n, j])

                branch_sum(
                    window, masks, b, col, spreads[b], -1, cut, product, acc.at[dx], n == 0
                )
    if pointed:
        for dx in range(2):
            for dy in range(2):
                row = pl.multiple_of((iy ^ dy) * 64, 64)
                outs[dy * 2 + dx][...] = acc[dx, :, pl.ds(row, 64), :].astype(BF)


def weight_kernel(spread, b, sources, lanes, info, *refs):
    tiles = refs[:8]
    masks, across = refs[8:10]
    pooled = len(sources) > 1
    outs = refs[10 + pooled : -4]
    windows, out, sems, out_sems = refs[-4:]
    cut = info[3]
    parts = out.shape[0]
    each = out.shape[2]
    paired = len(outs) == 2
    fetches = [
        tile_copies(info, tiles, windows.at[n], sems.at[n], lane)
        for n, lane in enumerate(sources)
    ]

    def emit(t, value):
        for z in range(parts):
            out[info[4] ^ z if paired else z, t] = value[z * each : (z + 1) * each].astype(BF)

    for copy in fetches[0]:
        copy.wait()
    window = windows.at[0]
    for j in (1, 0, 2):
        move = (j - 1) * spread
        columns = [p for p in range(32) if 0 <= p + move < 32]
        total = None
        for at in range(0, len(columns), 8):
            group = columns[at : at + 8]
            right = []
            for p in group:
                ok = None if j == 1 else ((p < cut) == (p + move < cut))
                right.append(
                    jnp.concatenate(
                        [shift_rows(window, masks, b, p, i, spread, -1, cut, ok) for i in range(3)],
                        axis=1,
                    )
                )
            first, last = (group[0] + move) * 128, (group[-1] + move + 1) * 128
            part = dot(across[:, first:last], jnp.concatenate(right, axis=0))
            total = part if total is None else total + part
        for i in range(3):
            emit(3 * i + j, total[:, i * lanes : (i + 1) * lanes])
    if len(sources) > 1:
        for copy in fetches[1]:
            copy.wait()
        plain = windows[1, REACH : REACH + 32, PAD : PAD + 128, :].reshape(32 * 128, lanes)
        emit(9, dot(across[...], plain))
        emit(10, refs[10][...])
    if paired:
        moves = [(0, outs[0].at[0]), (3, outs[0].at[1]), (1, outs[1].at[0]), (2, outs[1].at[1])]
        moves = [(out.at[m], target) for m, target in moves]
    else:
        moves = [(out, outs[0])]
    copies = [
        pltpu.make_async_copy(source, target, out_sems.at[n])
        for n, (source, target) in enumerate(moves)
    ]
    for copy in copies:
        copy.start()
    for copy in copies:
        copy.wait()


def collect_kernel(first, count, extras, info, *refs):
    pieces = refs[:4]
    outs = refs[len(refs) - 3 - len(extras) : len(refs) - 2]
    buf, sem = refs[len(refs) - 2 :]
    ix, ik = info[1], info[2]
    for n, piece in enumerate(pieces):
        index = (ix ^ (n // 2)) * 2 + (ik ^ (n % 2))
        for t in range(count):
            buf[t, index] = piece[t].astype(F32)
        at = count
        for e, length in enumerate(extras):
            for t in range(length):
                outs[1 + e][index, t] = piece[at + t].astype(F32)
            at += length
    copy = pltpu.make_async_copy(buf, outs[0].at[pl.ds(first, count)], sem)
    copy.start()
    copy.wait()


def pack_kernel(share, info, full, marks, *refs):
    iy, ix = info[0], info[1]
    rims = refs[4]
    for n in range(4):
        other = (iy ^ (n // 2)) * 2 + (ix ^ (n % 2))
        for z in range(full.shape[-1] // (4 * share)):
            lane = pl.multiple_of((z * 4 + other) * share, 128)
            value = full[:, :, pl.ds(lane, share)]
            refs[n][:, :, z * share : (z + 1) * share] = value

            @pl.when(iy == 0)
            def _(value=value, other=other, z=z):
                rims[other, :, :RIM, z * share : (z + 1) * share] = value[:, :RIM]

            @pl.when(iy == 1)
            def _(value=value, other=other, z=z):
                rims[other, :, :REACH, z * share : (z + 1) * share] = value[:, 64 - REACH :]

    for n in range(4):
        for q in range(8):
            rims[n, q, REACH : REACH + 1, :] = marks[...]


def unpack_kernel(share, info, *refs):
    iy, ix = info[0], info[1]
    full = refs[4]
    for n in range(4):
        other = (iy ^ (n // 2)) * 2 + (ix ^ (n % 2))
        for z in range(full.shape[-1] // (4 * share)):
            lane = pl.multiple_of((z * 4 + other) * share, 128)
            full[:, :, pl.ds(lane, share)] = refs[n][:, :, z * share : (z + 1) * share]


def across_kernel(share, info, *refs):
    tiles, out, rows, zero = refs[:8], *refs[8:11]
    window, acc, sems = refs[11:]
    ik, cut = info[2], info[3]
    for copy in tile_copies(info, tiles, window, sems):
        copy.wait()
    acc[...] = jnp.zeros_like(acc)
    for q in range(32):
        value = window[REACH + q, PAD : PAD + 128, :]
        turned = value.T
        for z in range(turned.shape[0] // share):
            low = turned[z * share : z * share + share // 2]
            high = turned[z * share + share // 2 : (z + 1) * share]
            out[z * share // 2 : (z + 1) * share // 2, q * 128 : (q + 1) * 128] = jnp.where(
                ik == 0, low, high
            )
        acc[(q >= cut).astype(jnp.int32)] += value.astype(F32)
    rows[...] = acc[1]
    zero[...] = jnp.sum(acc[0], axis=0, keepdims=True)


VMEM = pl.BlockSpec(memory_space=pltpu.VMEM)
SMEM = pl.BlockSpec(memory_space=pltpu.SMEM)
ANY = pl.BlockSpec(memory_space=pl.ANY)


def call(kernel, name, flops, in_specs, out_shape, scratch, args, out_specs=None, aliases=None):
    return pl.pallas_call(
        kernel,
        name=name,
        in_specs=in_specs,
        out_specs=out_specs or jax.tree.map(lambda _: VMEM, out_shape),
        out_shape=out_shape,
        input_output_aliases=aliases or {},
        scratch_shapes=scratch,
        compiler_params=pltpu.CompilerParams(vmem_limit_bytes=VMEM_LIMIT),
        cost_estimate=pl.CostEstimate(flops=flops, bytes_accessed=10**7, transcendentals=0),
    )(*args)


def per_device(
    feature_map,
    image_ids,
    point_weight,
    atrous_weight,
    pool_weight,
    project_weight,
    bn_gain,
    bn_shift,
    out_grad,
):
    rows, cols, chans = feature_map.shape
    feat = point_weight.shape[1]
    pixels = rows * cols
    zs = lax.axis_size("z")
    axes = ("k", "x", "y", "z")
    iz, iy, ix, ik = (lax.axis_index(a) for a in ("z", "y", "x", "k"))
    row_count = 2 * zs
    total = float(pixels * row_count * 4)
    images = rows * row_count // IMG_ROWS + 1
    share = chans // (4 * zs)
    mine = chans // 4
    spreads = [REACH * (b + 1) // 3 for b in range(3)]
    def pick(first, second, index):
        return jnp.where(index == 0, first, second)

    def rim(x, depth):
        return pick(x[:, :depth], x[:, rows - depth :], iy)

    def beyond(x, dy, dx):
        pairs = []
        for z in range(zs):
            for y in range(2):
                far = z - 1 + 2 * y
                if 0 <= far < zs:
                    for i in range(2):
                        target = (far * 2 + (y ^ dy)) * 2 + (i ^ dx)
                        pairs.append(((z * 2 + y) * 2 + i, target))
        return lax.ppermute(x, ("z", "y", "x"), pairs)

    with jax.named_scope("marks"):
        strip_own = jnp.max(image_ids, axis=1)
        edge_own = pick(strip_own[:REACH], strip_own[rows - REACH :], iy)
        zero_own = jnp.sum((image_ids[0] == 0).astype(jnp.int32))
        marks = jnp.concatenate([strip_own, edge_own, zero_own[None]])
        marks = jnp.pad(marks, (0, mine - marks.shape[0])).astype(BF)[None]

    places = jnp.stack([iy, ix, ik, ik, iz]).astype(jnp.int32)
    turned = feature_map.transpose(1, 0, 2)
    aligned = share % 128 == 0
    with jax.named_scope("spread_features"):
        if aligned:
            tile_shape = jax.ShapeDtypeStruct((cols, rows, mine), BF)
            *tiles, brims = call(
                partial(pack_kernel, share),
                "pack",
                0,
                [SMEM, VMEM, VMEM],
                [tile_shape] * 4 + [jax.ShapeDtypeStruct((4, cols, RIM, mine), BF)],
                [],
                [places, turned, marks],
            )
        else:
            packed = turned.reshape(cols, rows, zs, 2, 2, share).transpose(3, 4, 0, 1, 2, 5)
            packed = packed.reshape(4, cols, rows, mine)
            tiles = [
                lax.dynamic_index_in_dim(packed, (iy ^ dy) * 2 + (ix ^ dx), 0, False)
                for dy in range(2)
                for dx in range(2)
            ]
            brims = pick(packed[:, :, :REACH], packed[:, :, rows - REACH :], iy)
            brims = jnp.pad(brims, ((0, 0), (0, 0), (0, RIM - REACH), (0, 0)))
            brims = brims.at[:, :, REACH].set(marks)
        own, to_x, to_y, to_d = tiles
        mains = [own, swap(to_x, "x"), swap(to_y, "y"), crossed(to_d)]
        halo, mains = lax.optimization_barrier((beyond(brims, 0, 0), mains))
        halo = halo.at[:, :, REACH + 1].set(marks)
        halo = lax.all_to_all(halo, ("y", "x"), 0, 0)
        halos = [halo, swap(halo, "k")]

    mains = mains + [swap(g, "k") for g in mains]
    with jax.named_scope("marks"):
        told = jnp.stack([h[:, 0, REACH : REACH + 2] for h in halos]).astype(jnp.int32)
        told = told.reshape(2, 2, 2, 2, mine)
        strips = jnp.max(told[:, :, :, 1, :rows], axis=(0, 2))
        edges = jnp.max(told[:, :, :, 0, rows : rows + REACH], axis=(0, 2))
        cut = jnp.sum(told[:, 0, :, 1, rows + REACH])
        strip_plane = strips.reshape(2 * rows)
        top, bottom = edges[1], edges[0]
        strip_tall = jnp.concatenate([top, strip_plane, bottom])
        masks = jnp.stack(
            [
                jnp.stack(
                    [
                        strip_plane
                        == lax.slice_in_dim(strip_tall, REACH + s * d, REACH + s * d + 2 * rows)
                        for s in (-1, 1)
                    ]
                )
                for d in spreads
            ]
        )
        masks = jnp.broadcast_to(masks[..., None], (3, 2, 2 * rows, 128)).astype(BF)
        info = jnp.stack([iy, ix, ik, cut, iz]).astype(jnp.int32)


    local_ids = image_ids.T.reshape(pixels)
    image_range = jnp.arange(images, dtype=jnp.int32)
    table = local_ids[:, None] == image_range[None, :]

    point_view = point_weight.reshape(zs, 2, 2, share, feat)
    atrous_view = atrous_weight.reshape(3, 3, 3, zs, 2, 2, share, feat)

    def forward(units):
        shape = (2, cols, rows, feat)
        return call(
            partial(forward_kernel, units, spreads, mine),
            "forward_taps",
            2 * 2048 * mine * 256 * 15,
            [SMEM] + [ANY] * 8 + [VMEM] * 3 + [ANY] * 2,
            [jax.ShapeDtypeStruct(shape, F32), jax.ShapeDtypeStruct(shape, BF)] * 2,
            [
                pltpu.VMEM((32 + 2 * REACH, 2 * PAD + 128, mine), BF),
                pltpu.VMEM((zs, share, feat), BF),
                pltpu.VMEM((2, 3, 3, zs, share, feat), BF),
                pltpu.VMEM((8, 128, feat), F32),
                pltpu.SemaphoreType.DMA((16,)),
                pltpu.SemaphoreType.DMA((2, 9)),
            ],
            [info, *mains, *halos, masks, point_view, atrous_view],
        )

    def reduce_first(parts):
        keep_x, send_x, keep_y, send_y = parts
        return keep_x, swap(send_x, "x"), keep_y, swap(send_y, "y")

    def reduce_middle(parts):
        keep_x, got_x, keep_y, got_y = parts
        more_x = (keep_x[1] + got_x[1].astype(F32)).astype(BF)
        more_y = (keep_y[1] + got_y[1].astype(F32)).astype(BF)
        return more_x, more_y

    def reduce_last(parts, last_x, last_y):
        keep_x, got_x, keep_y, got_y = parts
        value_x = keep_x[0] + got_x[0].astype(F32) + last_x.astype(F32)
        value_y = keep_y[0] + got_y[0].astype(F32) + last_y.astype(F32)
        return [value_x.reshape(pixels, feat), value_y.reshape(pixels, feat)]

    early = forward([None, 0])
    early_got = reduce_first(early)
    late = forward([1, 2])
    early_got, late = lax.optimization_barrier((early_got, late))
    late_got = reduce_first(late)
    early_more = reduce_middle(early_got)
    early_last = [swap(early_more[0], "y"), swap(early_more[1], "x")]

    half = share // 2
    strip_table = strip_plane[:, None] == image_range[None, :]
    with jax.named_scope("across"):
        mains_late, early_last = lax.optimization_barrier((mains, early_last))
        if aligned:
            across, row_sums, zero_sums = call(
                partial(across_kernel, share),
                "across",
                2 * 10**9,
                [SMEM] + [ANY] * 8,
                [
                    jax.ShapeDtypeStruct((mine // 2, 32 * 2 * rows), BF),
                    jax.ShapeDtypeStruct((2 * rows, mine), F32),
                    jax.ShapeDtypeStruct((1, mine), F32),
                ],
                [
                    pltpu.VMEM((32 + 2 * REACH, 2 * PAD + 128, mine), BF),
                    pltpu.VMEM((2, 2 * rows, mine), F32),
                    pltpu.SemaphoreType.DMA((16,)),
                ],
                [info, *mains_late],
            )
        else:
            columns = []
            for x in range(2):
                for k in range(2):
                    index = [(ik ^ k) * 4 + (iy ^ y) * 2 + (ix ^ x) for y in range(2)]
                    stack = [lax.select_n(n.astype(jnp.int32), *mains_late) for n in index]
                    columns.append(jnp.concatenate(stack, axis=1))
            plane = jnp.concatenate(columns, axis=0)
            in_strip = (jnp.arange(32) >= cut)[:, None, None]
            row_sums = jnp.sum(jnp.where(in_strip, plane.astype(F32), 0.0), axis=0)
            zero_sums = jnp.sum(jnp.where(in_strip, 0.0, plane.astype(F32)), axis=(0, 1))[None]
            plane = plane.reshape(32, 2 * rows, zs, 2, half)
            plane = lax.dynamic_index_in_dim(plane, ik, 3, False)
            across = plane.reshape(32 * 2 * rows, mine // 2).T

    with jax.named_scope("image_sums"):
        sums = lax.dot_general(
            strip_table.astype(F32),
            row_sums,
            (((0,), (0,)), ((), ())),
            precision=lax.Precision.HIGHEST,
        )
        sums = jnp.where(image_range[:, None] == 0, zero_sums, sums)
        pool_mine = pool_weight.reshape(zs, 2, 2, share, feat)
        pool_mine = lax.dynamic_slice(
            pool_mine, (0, iy, ix, 0, 0), (zs, 1, 1, share, feat)
        ).reshape(mine, feat)
        per_image_part = 0.5 * exact(sums, pool_mine.astype(F32))
        strip_rows = jnp.sum(strip_table.astype(F32), axis=0)
        strip_rows = jnp.where((iy == 0) & (ix == 0) & (ik == 0), strip_rows, 0.0)
        strip_rows = jnp.pad(strip_rows, (0, -images % feat)).reshape(-1, feat)

    late_got, across, sums = lax.optimization_barrier((late_got, across, sums))
    late_more = reduce_middle(late_got)
    branches = reduce_last(early_got, *early_last)
    branches += reduce_last(late_got, swap(late_more[0], "y"), swap(late_more[1], "x"))

    first = jnp.concatenate([moments(value) for value in branches], axis=0)
    first = allsum(jnp.concatenate([first, per_image_part, strip_rows], axis=0))
    strip_rows = first[8 + images :].reshape(-1)[:images]
    counts = jnp.where(
        image_range == 0,
        (cut * (rows * row_count)).astype(F32),
        strip_rows * (4 * cols - cut).astype(F32),
    )
    per_image = first[8 : 8 + images] / counts[:, None]
    first = first[:8].reshape(4, 2, feat).transpose(1, 0, 2).reshape(2, 4 * feat)
    weighted = counts[:, None] * per_image
    pool_stats = jnp.stack([jnp.sum(weighted, axis=0), jnp.sum(weighted * per_image, axis=0)])
    four = 4 * feat
    flat_gain, flat_shift = bn_gain[:4].reshape(four), bn_shift[:4].reshape(four)
    mean = first[0] / total
    scale = lax.rsqrt(first[1] / total - mean * mean + EPSILON)
    normed = (jnp.concatenate(branches, axis=1) - mean) * scale
    lifted = normed * flat_gain + flat_shift
    mean4 = pool_stats[0] / total
    scale4 = lax.rsqrt(pool_stats[1] / total - mean4 * mean4 + EPSILON)
    normed4 = (per_image - mean4) * scale4
    lifted4 = normed4 * bn_gain[4] + bn_shift[4]
    joined = smooth(lifted).astype(BF)
    joined4 = smooth(lifted4).astype(BF)
    table_float = table.astype(F32)
    head = dot(joined, project_weight[:four]) + exact(
        table_float, dot(joined4, project_weight[four:])
    )
    head_stats = allsum(moments(head))
    head_mean = head_stats[0] / total
    head_scale = lax.rsqrt(head_stats[1] / total - head_mean * head_mean + EPSILON)
    head_norm = (head - head_mean) * head_scale
    head_lift = head_norm * bn_gain[5] + bn_shift[5]
    output = smooth(head_lift).astype(BF).reshape(cols, rows, feat)
    cotangent = out_grad.transpose(1, 0, 2).reshape(pixels, feat).astype(F32)
    head_grad = cotangent * smooth_slope(head_lift)
    head_back = allsum(
        jnp.stack([jnp.sum(head_grad, axis=0), jnp.sum(head_grad * head_norm, axis=0)])
    )
    head_slope = (
        bn_gain[5]
        * head_scale
        * (head_grad - head_back[0] / total - head_norm * head_back[1] / total)
    ).astype(BF)
    joined_grad = lax.dot_general(
        head_slope, project_weight[:four], (((1,), (1,)), ((), ())), preferred_element_type=F32
    )
    grads = joined_grad * smooth_slope(lifted)
    image_heads = jnp.einsum(
        "pi,pf->if", table.astype(BF), head_slope, preferred_element_type=F32
    )
    rear = jnp.concatenate(
        [
            jnp.stack([jnp.sum(grads, axis=0), jnp.sum(grads * normed, axis=0)]).reshape(8, feat),
            image_heads,
        ],
        axis=0,
    )
    rear = allsum(rear)
    shift_back, gain_back = rear[:4].reshape(four), rear[4:8].reshape(four)
    slopes = (
        flat_gain * scale * (grads - shift_back / total - normed * gain_back / total)
    ).astype(BF)

    with jax.named_scope("project_grad"):
        project_inputs = joined, head_slope

    with jax.named_scope("spread_slopes"):
        tiles_out = [
            slopes[:, first * feat : last * feat].reshape(cols, rows, -1)
            for first, last in ((3, 4), (2, 3), (0, 2))
        ]
        brim = beyond(rim(tiles_out[0], 32), 0, 0)
        shallow = [rim(tile, 16) for tile in tiles_out[1:]]
        brims = beyond(jnp.concatenate(shallow, axis=2), 0, 0)
        def both_cores(got):
            return got + [swap(g, "k") for g in got]

        tile3 = jnp.concatenate([tiles_out[0], brim], axis=1)
        got3 = [tile3, swap(tile3, "x"), swap(tile3, "y"), crossed(tile3)]
        left, right = gate(project_inputs, tile3)
        project_part = lax.dot_general(
            left, right, (((0,), (0,)), ((), ())), preferred_element_type=F32
        )
        blocks = project_part.astype(BF).reshape(4, feat, feat)
        blocks = lax.all_to_all(blocks, ("x", "k"), 0, 0)
        across, blocks = lax.optimization_barrier((across, blocks))
        project_sum = jnp.sum(blocks.astype(F32), axis=0)
        project_got = z_swap(project_sum, 1)
        got3, brims = lax.optimization_barrier((got3, brims))
        tile2 = jnp.concatenate([tiles_out[1], brims[:, :, :feat]], axis=1)
        tile1 = jnp.concatenate([tiles_out[2], brims[:, :, feat:]], axis=1)
        group3 = both_cores(got3)
        tile2, group3, output = lax.optimization_barrier((tile2, group3, output))
        output = output.transpose(1, 0, 2)
        arrived2 = [tile2, swap(tile2, "x"), swap(tile2, "y"), crossed(tile2)]

    rear, sums = gate((rear, sums), tile3)
    image_heads = rear[8:]
    grads4 = smooth_slope(lifted4) * exact(image_heads, project_weight[four:].astype(F32).T)
    shift4, gain4 = jnp.sum(grads4, axis=0), jnp.sum(grads4 * normed4, axis=0)
    image_slope = (
        bn_gain[4]
        * scale4
        * (grads4 - counts[:, None] * (shift4 / total + normed4 * gain4 / total))
    )
    image_low = image_slope.astype(BF)
    spread_back = (
        lax.dot_general(
            image_low, pool_mine, (((1,), (1,)), ((), ())), preferred_element_type=F32
        )
        / counts[:, None]
    )
    strip_back = exact(strip_table.astype(F32), spread_back)
    sums_mine = lax.dynamic_index_in_dim(sums.reshape(images, zs, 2, half), ik, 2, False)
    pool_part = lax.dot_general(
        sums_mine.reshape(images, mine // 2),
        image_low.astype(F32) / counts[:, None],
        (((0,), (0,)), ((), ())),
        precision=lax.Precision.HIGHEST,
    )

    def weight_grad(b, tiles, lanes_at, more=()):
        taps = 8 + len(lanes_at) + len(more)
        return call(
            partial(weight_kernel, spreads[b], b, lanes_at, feat),
            "weight_taps",
            2 * 4096 * (mine // 2) * 256 * 15,
            [SMEM] + [ANY] * 8 + [VMEM] * (2 + len(more)),
            [jax.ShapeDtypeStruct((2, taps, half, feat), BF)] * 2
            if zs == 4
            else [jax.ShapeDtypeStruct((zs, taps, half, feat), BF)],
            [
                pltpu.VMEM((len(lanes_at), 32 + 2 * REACH, 2 * PAD + 128, feat), BF),
                pltpu.VMEM((zs, taps, half, feat), BF),
                pltpu.SemaphoreType.DMA((2, 16)),
                pltpu.SemaphoreType.DMA((4,)),
            ],
            [info, *tiles, masks, across, *more],
            out_specs=[ANY] * (2 if zs == 4 else 1),
        )

    def collect(pieces, first, buffer):
        count = 9 if buffer else 18
        extras = [1, 1] if buffer else [pieces[0].shape[0] - count]
        grad = jax.ShapeDtypeStruct((27, 4, half, feat), F32)
        sides = [jax.ShapeDtypeStruct((4, n, half, feat), F32) for n in extras]
        return call(
            partial(collect_kernel, first, count, extras),
            "collect",
            6 * 10**9,
            [SMEM] + [VMEM] * 4 + [ANY] * len(buffer),
            [grad, *sides],
            [pltpu.VMEM((count, 4, half, feat), F32), pltpu.SemaphoreType.DMA],
            [places, *pieces, *buffer],
            out_specs=[ANY] + [VMEM] * len(extras),
            aliases={5: 0} if buffer else {},
        )

    def scatter_first(part):
        if zs != 4:
            return lax.psum_scatter(part[0], "z", scatter_dimension=0, tiled=True), None
        return part[0], z_swap(part[1], 1)

    def scatter_second(state):
        keep, got = state
        if zs != 4:
            return keep, None
        more = (keep[1].astype(F32) + got[1].astype(F32)).astype(BF)
        return keep[0].astype(F32) + got[0].astype(F32), z_swap(more, 3)

    def scatter_last(state):
        keep, got = state
        if zs != 4:
            return keep[0]
        return (keep + got.astype(F32)).astype(BF)

    across, pool_part, spread_back, strip_back = lax.optimization_barrier(
        (across, pool_part, spread_back, strip_back)
    )
    part3 = weight_grad(2, group3, [0])
    arrived2, part3, project_got = lax.optimization_barrier((arrived2, part3, project_got))
    project_sum = project_sum + project_got
    step = 2
    while step < zs // 2:
        project_sum = project_sum + z_swap(project_sum, step)
        step *= 2
    project_got = z_swap(project_sum, step)
    group2 = both_cores(arrived2)
    tile1, group2 = lax.optimization_barrier((tile1, group2))
    arrived1 = [tile1, swap(tile1, "x"), swap(tile1, "y"), crossed(tile1)]
    sums3 = scatter_first(part3)
    part2 = weight_grad(1, group2, [0])
    part2, group2, project_got, sums3 = lax.optimization_barrier(
        (part2, group2, project_got, sums3)
    )
    sums2, sums3 = scatter_first(part2), scatter_second(sums3)
    project_sum = gate(project_sum + project_got, part2)

    def input_part(chosen, groups, pointed, more, outs):
        n = len(chosen)
        scratch = [
            pltpu.VMEM((n, 32 + 2 * REACH, 2 * PAD + 128, feat), BF),
            pltpu.VMEM((n, 3, zs, share, 3 * feat), BF),
        ]
        if pointed:
            scratch += [pltpu.VMEM((zs, share, feat), BF), pltpu.VMEM((2, 8, 128, mine), F32)]
        scratch += [pltpu.SemaphoreType.DMA((n, 16)), pltpu.SemaphoreType.DMA((n, 9))]
        return call(
            partial(input_kernel, chosen, spreads, feat, pointed),
            "input_taps",
            2 * 2048 * mine * 256 * 20,
            [SMEM] + [ANY] * 8 * len(groups) + [VMEM] + [ANY] * 2 + [VMEM] * len(more),
            outs,
            scratch,
            [info, *[t for g in groups for t in g], masks, point_view, atrous_view, *more],
        )

    with jax.named_scope("input_grad"):
        sums_so_far = input_part(
            [(2, 0, 0), (1, 1, 0)],
            [group3, group2],
            False,
            [],
            jax.ShapeDtypeStruct((2, cols, 2 * rows, mine), F32),
        )
    arrived1, sums_so_far, sums2, sums3 = lax.optimization_barrier(
        (arrived1, sums_so_far, sums2, sums3)
    )
    group1 = both_cores(arrived1)
    sums2 = scatter_second(sums2)
    project_got = swap(gate(project_sum, arrived1), "y")
    part1 = weight_grad(0, group1, [feat, 0], [pool_part])
    sums3, sums2, project_got, part1 = lax.optimization_barrier(
        (sums3, sums2, project_got, part1)
    )
    project_sum = (project_sum + project_got).astype(BF).reshape(feat // half, half, feat)
    joint = jnp.concatenate([scatter_last(sums2), scatter_last(sums3), project_sum], axis=0)
    joint_x = swap(joint, "x")
    sums1 = scatter_first(part1)
    with jax.named_scope("input_grad"):
        group1, part1 = lax.optimization_barrier((group1, part1))
        shape = jax.ShapeDtypeStruct((cols, rows, mine), BF)
        own, to_x, to_y, to_d = input_part(
            [(0, 0, feat), (None, 0, 0)],
            [group1],
            True,
            [sums_so_far, spread_back[:1], strip_back],
            [shape] * 4,
        )
        sums1, joint_x = gate((sums1, joint_x), own)
        got = [own, swap(to_x, "x"), swap(to_y, "y"), crossed(to_d)]
        sums1 = scatter_second(gate(sums1, got[1]))
        joint, joint_x = lax.optimization_barrier((joint, joint_x))
        pieces32 = [joint, swap(joint, "k"), joint_x, swap(joint_x, "k")]
        grad, project_all = collect(pieces32, 9, [])
        got, sums1, grad = lax.optimization_barrier((got, sums1, grad))
        if aligned:
            input_turned = call(
                partial(unpack_kernel, share),
                "unpack",
                4 * 10**9,
                [SMEM] + [VMEM] * 4,
                jax.ShapeDtypeStruct((cols, rows, chans), BF),
                [],
                [places, *got],
            )
        else:
            planes = []
            for y in range(2):
                for x in range(2):
                    index = ((iy ^ y) * 2 + (ix ^ x)).astype(jnp.int32)
                    planes.append(lax.select_n(index, *got).reshape(cols, rows, zs, share))
            input_turned = jnp.stack(planes, axis=3).reshape(cols, rows, chans)
        input_grad = input_turned.transpose(1, 0, 2)

    with jax.named_scope("project_grad"):
        project_pool = lax.dot_general(
            joined4.astype(F32),
            image_heads,
            (((0,), (0,)), ((), ())),
            precision=lax.Precision.HIGHEST,
        )
        project_grad = jnp.concatenate([project_all.reshape(four, feat), project_pool], axis=0)

    done = scatter_last(sums1)
    done_x = swap(done, "x")
    done_x, grad, input_grad = lax.optimization_barrier((done_x, grad, input_grad))
    pieces1 = [done, swap(done, "k"), done_x, swap(done_x, "k")]
    grad, point_grad, pool_grad = collect(pieces1, 0, [grad])
    atrous_grad = grad.reshape(3, 3, 3, 4 * half, feat)
    point_grad, pool_grad = (v.reshape(4 * half, feat) for v in (point_grad, pool_grad))

    gain_grad = jnp.concatenate([rear[4:8], gain4[None], head_back[1][None]], axis=0)
    shift_grad = jnp.concatenate([rear[:4], shift4[None], head_back[0][None]], axis=0)
    return (
        output,
        input_grad,
        point_grad,
        atrous_grad,
        pool_grad,
        project_grad,
        gain_grad,
        shift_grad,
    )


def solution(mesh):
    row, col = mesh.devices.shape
    fine = Mesh(mesh.devices.reshape(row // 2, 2, col // 2, 2), ("z", "y", "x", "k"))
    rows, cols = ("z", "y"), ("x", "k")
    placed = (
        P(rows, cols, None),
        P(rows, cols),
        P(),
        P(),
        P(),
        P(),
        P(),
        P(),
        P(rows, cols, None),
    )
    return jax.shard_map(
        per_device,
        mesh=fine,
        in_specs=placed,
        out_specs=(
            P(rows, cols, None),
            P(rows, cols, None),
            P(rows, None),
            P(None, None, None, rows, None),
            P(rows, None),
            P(),
            P(),
            P(),
        ),
        check_vma=False,
    )
```

```python
from functools import partial

import jax
import jax.numpy as jnp
from jax import lax
from jax.experimental import pallas as pl
from jax.experimental.pallas import tpu as pltpu
from jax.sharding import Mesh, PartitionSpec as P

REACH = 18
IMG_ROWS = 32
EPSILON = 1e-05
PAD = 32
RIM = 24
SWAP = [(0, 1), (1, 0)]
BF = jnp.bfloat16
F32 = jnp.float32
VMEM_LIMIT = 60 * 2**20


def dot(a, b):
    return jnp.dot(a, b, preferred_element_type=F32)


def exact(a, b):
    return jnp.dot(a, b, precision=lax.Precision.HIGHEST, preferred_element_type=F32)


def gate(x, *deps):
    return lax.optimization_barrier((x, deps))[0]


def swap(x, axis):
    return lax.ppermute(x, axis, SWAP)


def z_swap(x, step):
    count = lax.axis_size("z")
    return lax.ppermute(x, "z", [(i, i ^ step) for i in range(count)])


def crossed(x):
    return lax.ppermute(x, ("y", "x"), [(i, 3 - i) for i in range(4)])


def quad(x, axes):
    near, far, last = (
        lax.ppermute(x, axes, [(i, i ^ step) for i in range(4)]) for step in (1, 2, 3)
    )
    return (x + near) + (far + last)


def z_sum(x):
    count = lax.axis_size("z")
    if count == 4:
        return quad(x, "z")
    step = 1
    while step < count:
        x = x + lax.ppermute(x, "z", [(i, i ^ step) for i in range(count)])
        step *= 2
    return x


def plane_sum(x):
    return quad(x, ("y", "x"))


def allsum(x):
    x = plane_sum(z_sum(x))
    return x + swap(x, "k")


def smooth(value):
    return jax.nn.gelu(value, approximate=True)


def smooth_slope(value):
    root = 0.7978845608028654
    square = value * value
    tanh = jnp.tanh(root * (value + 0.044715 * value * square))
    return 0.5 * (1.0 + tanh) + 0.5 * value * (1.0 - tanh * tanh) * root * (
        1.0 + 3 * 0.044715 * square
    )


def moments(value):
    return jnp.stack([jnp.sum(value, axis=0), jnp.sum(value * value, axis=0)])


def place_of(info, n):
    dk, dy, dx = n // 4, n // 2 % 2, n % 2
    col = ((info[1] ^ dx) * 2 + (info[2] ^ dk)) * 8
    return REACH + col, info[0] ^ dy


def tile_copies(info, tiles, window, sems, main=0, rim=0):
    copies = []
    for n, tile in enumerate(tiles):
        col, y = place_of(info, n)
        row = pl.multiple_of(PAD + y * 64, 16)
        copies.append(
            pltpu.make_async_copy(
                tile.at[:, pl.ds(main, 64)],
                window.at[pl.ds(col, 8), pl.ds(row, 64)],
                sems.at[n],
            )
        )
        if rim:
            row = pl.multiple_of(jnp.where(y == 0, PAD + 128, PAD - rim), 16)
            copies.append(
                pltpu.make_async_copy(
                    tile.at[:, pl.ds(main + 64, rim)],
                    window.at[pl.ds(col, 8), pl.ds(row, rim)],
                    sems.at[8 + n],
                )
            )
    for copy in copies:
        copy.start()
    return copies


def place_rims(info, rims, window):
    for dk, rim in enumerate(rims):
        for n in range(4):
            col = REACH + ((n % 2) * 2 + (info[2] ^ dk)) * 8
            row = PAD + 128 if n < 2 else PAD - REACH
            for q in range(8):
                window[col + q, row : row + REACH, :] = rim[n, q, :REACH]


def shift_rows(window, masks, b, q, i, spread, sign, cut, ok=None):
    start = PAD + sign * (i - 1) * spread
    value = window[REACH + q, start : start + 128, :]
    if i != 1:
        keep = masks[b, 1 if sign * (i - 1) > 0 else 0]
        keep = jnp.where(q >= cut, keep, jnp.ones_like(keep))
        if ok is not None:
            keep = jnp.where(ok, keep, jnp.zeros_like(keep))
        value = value * jnp.concatenate([keep] * (value.shape[1] // 128), axis=1)
    elif ok is not None:
        value = jnp.where(ok, value, jnp.zeros_like(value))
    return value


def tap_rows(window, masks, b, col, width, spread, sign, cut):
    return jnp.concatenate(
        [
            jnp.concatenate(
                [shift_rows(window, masks, b, col + u, i, spread, sign, cut) for i in range(3)],
                axis=1,
            )
            for u in range(width)
        ],
        axis=0,
    )


def branch_sum(window, masks, b, col, spread, sign, cut, product, acc, fresh):
    width = 2

    def inside(j, e):
        source = col + e + sign * (j - 1) * spread
        return (source >= 0) & (source < 32) & ((source < cut) == (col + e < cut))

    def center(e):
        return product(1, tap_rows(window, masks, b, col + e, width, spread, sign, cut))

    def side(j, e):
        source = col + e + sign * (j - 1) * spread
        part = product(j, tap_rows(window, masks, b, source, width, spread, sign, cut))
        return jnp.concatenate(
            [
                jnp.where(inside(j, e + u), part[u * 128 : u * 128 + 128], 0.0)
                for u in range(width)
            ],
            axis=0,
        )

    def put(e, value, first):
        value = value.reshape(width, 128, acc.shape[-1])
        if first:
            acc[e : e + width] = value
        else:
            acc[e : e + width] += value

    dense = spread == REACH // 3
    for e in range(0, 8, width):
        value = center(e)
        if dense:
            value = value + side(0, e) + side(2, e)
        put(e, value, fresh)
    if dense:
        return
    for j in (0, 2):
        for half in (0, 4):
            some = inside(j, half)
            for e in range(1, 4):
                some = some | inside(j, half + e)

            @pl.when(some)
            def _(j=j, half=half):
                for e in range(half, half + 4, width):
                    put(e, side(j, e), False)


def forward_kernel(units, spreads, lanes, info, *refs):
    mains, rims = refs[:8], refs[8:10]
    masks, point, weights = refs[10:13]
    outs = refs[13:17]
    window, point_buf, weight_buf, acc, sems, weight_sems = refs[17:]
    iy, ix, ik, cut = info[0], info[1], info[2], info[3]
    copies = tile_copies(info, mains, window, sems)
    loads = []
    for n, b in enumerate(units):
        if b is None:
            loads.append(
                [pltpu.make_async_copy(point.at[:, iy, ix], point_buf, weight_sems.at[n, 0])]
            )
        else:
            loads.append(
                [
                    pltpu.make_async_copy(
                        weights.at[b, i, j, :, iy, ix],
                        weight_buf.at[n, j, i],
                        weight_sems.at[n, 3 * j + i],
                    )
                    for j in range(3)
                    for i in range(3)
                ]
            )
        for copy in loads[n]:
            copy.start()
    place_rims(info, rims, window)
    for copy in copies:
        copy.wait()
    for n, b in enumerate(units):
        for copy in loads[n]:
            copy.wait()
        keep, send = outs[2 * n : 2 * n + 2]
        for dx in (1, 0):
            col = (ix ^ dx) * 16 + ik * 8
            if b is None:
                source = window[pl.ds(REACH + col, 8), PAD : PAD + 128, :].reshape(1024, lanes)
                acc[...] = dot(source, point_buf[...].reshape(lanes, 256)).reshape(8, 128, 256)
            else:

                def product(j, rows, n=n):
                    return dot(rows, weight_buf[n, j].reshape(3 * lanes, 256))

                branch_sum(window, masks, b, col, spreads[b], 1, cut, product, acc, True)
            for dy in range(2):
                row = pl.multiple_of((iy ^ dy) * 64, 64)
                value = acc[:, pl.ds(row, 64), :]
                if (dy if n else dx) == 0:
                    keep[dx if n else dy] = value
                else:
                    send[dx if n else dy] = value.astype(BF)


def input_kernel(chosen, spreads, lanes, pointed, info, *refs):
    count = 8 * (1 + max(c[1] for c in chosen))
    tiles, masks, point, weights = refs[:count], refs[count], refs[count + 1], refs[count + 2]
    rest = refs[count + 3 :]
    if pointed:
        before, edge, strip = rest[:3]
        outs = rest[3:7]
        windows, weight_buf, point_buf, acc, sems, weight_sems = rest[7:]
    else:
        (result,) = rest[:1]
        windows, weight_buf, sems, weight_sems = rest[1:]
        acc = result
    iy, ix, ik, cut = info[0], info[1], info[2], info[3]
    mine = acc.shape[-1]
    fetches, loads = [], []
    for n, (b, first, main, rim) in enumerate(chosen):
        group = tiles[8 * first : 8 * first + 8]
        fetches.append(tile_copies(info, group, windows.at[n], sems.at[n], main, rim))
        if b is None:
            loads.append(
                [pltpu.make_async_copy(point.at[:, iy, ix], point_buf, weight_sems.at[n, 0])]
            )
        else:
            loads.append(
                [
                    pltpu.make_async_copy(
                        weights.at[b, i, j, :, iy, ix],
                        weight_buf.at[n, j, :, :, pl.ds(i * lanes, lanes)],
                        weight_sems.at[n, 3 * j + i],
                    )
                    for j in range(3)
                    for i in range(3)
                ]
            )
        for copy in loads[n]:
            copy.start()

    def times(a, w):
        return lax.dot_general(
            a, w.reshape(mine, w.shape[-1]), (((1,), (1,)), ((), ())), preferred_element_type=F32
        )

    for n, (b, _, _, _) in enumerate(chosen):
        for copy in fetches[n] + loads[n]:
            copy.wait()
        window = windows.at[n]
        for dx in range(2):
            col = (ix ^ dx) * 16 + ik * 8
            if b is None:
                for e in range(0, 8, 2):
                    source = window[pl.ds(REACH + col + e, 2), PAD : PAD + 128, :]
                    value = times(source.reshape(256, lanes), point_buf[...])
                    for u in range(2):
                        pool = jnp.where(col + e + u < cut, edge[...], strip[...])
                        acc[dx, e + u] += (
                            before[dx, e + u] + value[u * 128 : u * 128 + 128] + pool
                        )
            else:

                def product(j, rows, n=n):
                    return times(rows, weight_buf[n, j])

                branch_sum(
                    window, masks, b, col, spreads[b], -1, cut, product, acc.at[dx], n == 0
                )
    if pointed:
        for dx in range(2):
            for dy in range(2):
                row = pl.multiple_of((iy ^ dy) * 64, 64)
                outs[dy * 2 + dx][...] = acc[dx, :, pl.ds(row, 64), :].astype(BF)


def weight_kernel(spread, b, sources, lanes, info, *refs):
    tiles = refs[:8]
    masks, across = refs[8:10]
    pooled = len(sources) > 1
    outs = refs[10 + pooled : -4]
    windows, out, sems, out_sems = refs[-4:]
    cut = info[3]
    parts = out.shape[0]
    each = out.shape[2]
    paired = len(outs) == 2
    fetches = [
        tile_copies(info, tiles, windows.at[n], sems.at[n], main, rim)
        for n, (main, rim) in enumerate(sources)
    ]

    def emit(t, value):
        for z in range(parts):
            out[info[4] ^ z if paired else z, t] = value[z * each : (z + 1) * each].astype(BF)

    for copy in fetches[0]:
        copy.wait()
    window = windows.at[0]
    for j in (1, 0, 2):
        move = (j - 1) * spread
        columns = [p for p in range(32) if 0 <= p + move < 32]
        total = None
        for at in range(0, len(columns), 8):
            group = columns[at : at + 8]
            right = []
            for p in group:
                ok = None if j == 1 else ((p < cut) == (p + move < cut))
                right.append(
                    jnp.concatenate(
                        [shift_rows(window, masks, b, p, i, spread, -1, cut, ok) for i in range(3)],
                        axis=1,
                    )
                )
            first, last = (group[0] + move) * 128, (group[-1] + move + 1) * 128
            part = dot(across[:, first:last], jnp.concatenate(right, axis=0))
            total = part if total is None else total + part
        for i in range(3):
            emit(3 * i + j, total[:, i * lanes : (i + 1) * lanes])
    if len(sources) > 1:
        for copy in fetches[1]:
            copy.wait()
        plain = windows[1, REACH : REACH + 32, PAD : PAD + 128, :].reshape(32 * 128, lanes)
        emit(9, dot(across[...], plain))
        emit(10, refs[10][...])
    if paired:
        moves = [(0, outs[0].at[0]), (3, outs[0].at[1]), (1, outs[1].at[0]), (2, outs[1].at[1])]
        moves = [(out.at[m], target) for m, target in moves]
    else:
        moves = [(out, outs[0])]
    copies = [
        pltpu.make_async_copy(source, target, out_sems.at[n])
        for n, (source, target) in enumerate(moves)
    ]
    for copy in copies:
        copy.start()
    for copy in copies:
        copy.wait()


def collect_kernel(first, count, extras, info, *refs):
    pieces = refs[:4]
    outs = refs[len(refs) - 3 - len(extras) : len(refs) - 2]
    buf, sem = refs[len(refs) - 2 :]
    ix, ik = info[1], info[2]
    for n, piece in enumerate(pieces):
        index = (ix ^ (n // 2)) * 2 + (ik ^ (n % 2))
        for t in range(count):
            buf[t, index] = piece[t].astype(F32)
        at = count
        for e, length in enumerate(extras):
            for t in range(length):
                outs[1 + e][index, t] = piece[at + t].astype(F32)
            at += length
    copy = pltpu.make_async_copy(buf, outs[0].at[pl.ds(first, count)], sem)
    copy.start()
    copy.wait()


def pack_kernel(share, info, full, marks, *refs):
    iy, ix = info[0], info[1]
    rims = refs[4]
    for n in range(4):
        other = (iy ^ (n // 2)) * 2 + (ix ^ (n % 2))
        for z in range(full.shape[-1] // (4 * share)):
            lane = pl.multiple_of((z * 4 + other) * share, 128)
            value = full[:, :, pl.ds(lane, share)]
            refs[n][:, :, z * share : (z + 1) * share] = value

            @pl.when(iy == 0)
            def _(value=value, other=other, z=z):
                rims[other, :, :RIM, z * share : (z + 1) * share] = value[:, :RIM]

            @pl.when(iy == 1)
            def _(value=value, other=other, z=z):
                rims[other, :, :REACH, z * share : (z + 1) * share] = value[:, 64 - REACH :]

    for n in range(4):
        for q in range(8):
            rims[n, q, REACH : REACH + 1, :] = marks[...]


def unpack_kernel(share, info, *refs):
    iy, ix = info[0], info[1]
    full = refs[4]
    for n in range(4):
        other = (iy ^ (n // 2)) * 2 + (ix ^ (n % 2))
        for z in range(full.shape[-1] // (4 * share)):
            lane = pl.multiple_of((z * 4 + other) * share, 128)
            full[:, :, pl.ds(lane, share)] = refs[n][:, :, z * share : (z + 1) * share]


def across_kernel(share, info, *refs):
    tiles, out, rows, zero = refs[:8], *refs[8:11]
    window, acc, sems = refs[11:]
    ik, cut = info[2], info[3]
    for copy in tile_copies(info, tiles, window, sems):
        copy.wait()
    acc[...] = jnp.zeros_like(acc)
    for q in range(32):
        value = window[REACH + q, PAD : PAD + 128, :]
        turned = value.T
        for z in range(turned.shape[0] // share):
            low = turned[z * share : z * share + share // 2]
            high = turned[z * share + share // 2 : (z + 1) * share]
            out[z * share // 2 : (z + 1) * share // 2, q * 128 : (q + 1) * 128] = jnp.where(
                ik == 0, low, high
            )
        acc[(q >= cut).astype(jnp.int32)] += value.astype(F32)
    rows[...] = acc[1]
    zero[...] = jnp.sum(acc[0], axis=0, keepdims=True)


VMEM = pl.BlockSpec(memory_space=pltpu.VMEM)
SMEM = pl.BlockSpec(memory_space=pltpu.SMEM)
ANY = pl.BlockSpec(memory_space=pl.ANY)


def call(kernel, name, flops, in_specs, out_shape, scratch, args, out_specs=None, aliases=None):
    return pl.pallas_call(
        kernel,
        name=name,
        in_specs=in_specs,
        out_specs=out_specs or jax.tree.map(lambda _: VMEM, out_shape),
        out_shape=out_shape,
        input_output_aliases=aliases or {},
        scratch_shapes=scratch,
        compiler_params=pltpu.CompilerParams(vmem_limit_bytes=VMEM_LIMIT),
        cost_estimate=pl.CostEstimate(flops=flops, bytes_accessed=10**7, transcendentals=0),
    )(*args)


def per_device(
    feature_map,
    image_ids,
    point_weight,
    atrous_weight,
    pool_weight,
    project_weight,
    bn_gain,
    bn_shift,
    out_grad,
):
    rows, cols, chans = feature_map.shape
    feat = point_weight.shape[1]
    pixels = rows * cols
    zs = lax.axis_size("z")
    axes = ("k", "x", "y", "z")
    iz, iy, ix, ik = (lax.axis_index(a) for a in ("z", "y", "x", "k"))
    row_count = 2 * zs
    total = float(pixels * row_count * 4)
    images = rows * row_count // IMG_ROWS + 1
    share = chans // (4 * zs)
    mine = chans // 4
    spreads = [REACH * (b + 1) // 3 for b in range(3)]
    def pick(first, second, index):
        return jnp.where(index == 0, first, second)

    def rim(x, depth):
        return pick(x[:, :depth], x[:, rows - depth :], iy)

    def beyond(x, dy, dx):
        pairs = []
        for z in range(zs):
            for y in range(2):
                far = z - 1 + 2 * y
                if 0 <= far < zs:
                    for i in range(2):
                        target = (far * 2 + (y ^ dy)) * 2 + (i ^ dx)
                        pairs.append(((z * 2 + y) * 2 + i, target))
        return lax.ppermute(x, ("z", "y", "x"), pairs)

    with jax.named_scope("marks"):
        strip_own = jnp.max(image_ids, axis=1)
        edge_own = pick(strip_own[:REACH], strip_own[rows - REACH :], iy)
        zero_own = jnp.sum((image_ids[0] == 0).astype(jnp.int32))
        marks = jnp.concatenate([strip_own, edge_own, zero_own[None]])
        marks = jnp.pad(marks, (0, mine - marks.shape[0])).astype(BF)[None]

    places = jnp.stack([iy, ix, ik, ik, iz]).astype(jnp.int32)
    turned = feature_map.transpose(1, 0, 2)
    aligned = share % 128 == 0
    with jax.named_scope("spread_features"):
        if aligned:
            tile_shape = jax.ShapeDtypeStruct((cols, rows, mine), BF)
            *tiles, brims = call(
                partial(pack_kernel, share),
                "pack",
                0,
                [SMEM, VMEM, VMEM],
                [tile_shape] * 4 + [jax.ShapeDtypeStruct((4, cols, RIM, mine), BF)],
                [],
                [places, turned, marks],
            )
        else:
            packed = turned.reshape(cols, rows, zs, 2, 2, share).transpose(3, 4, 0, 1, 2, 5)
            packed = packed.reshape(4, cols, rows, mine)
            tiles = [
                lax.dynamic_index_in_dim(packed, (iy ^ dy) * 2 + (ix ^ dx), 0, False)
                for dy in range(2)
                for dx in range(2)
            ]
            brims = pick(packed[:, :, :REACH], packed[:, :, rows - REACH :], iy)
            brims = jnp.pad(brims, ((0, 0), (0, 0), (0, RIM - REACH), (0, 0)))
            brims = brims.at[:, :, REACH].set(marks)
        note = jnp.broadcast_to(marks[None, None], (4, cols, 1, mine))
        own, to_x, to_y, to_d = tiles
        mains = [own, swap(to_x, "x"), swap(to_y, "y"), crossed(to_d)]
        halo, mains = lax.optimization_barrier((beyond(brims, 0, 0), mains))
        halo = lax.dynamic_update_slice_in_dim(halo, note, REACH + 1, axis=2)
        halo = lax.all_to_all(halo, ("y", "x"), 0, 0)
        halos = [halo, swap(halo, "k")]

    mains = mains + [swap(g, "k") for g in mains]
    with jax.named_scope("marks"):
        told = jnp.stack([h[:, 0, REACH : REACH + 2] for h in halos]).astype(jnp.int32)
        told = told.reshape(2, 2, 2, 2, mine)
        strips = jnp.max(told[:, :, :, 1, :rows], axis=(0, 2))
        edges = jnp.max(told[:, :, :, 0, rows : rows + REACH], axis=(0, 2))
        cut = jnp.sum(told[:, 0, :, 1, rows + REACH])
        strip_plane = strips.reshape(2 * rows)
        top, bottom = edges[1], edges[0]
        strip_tall = jnp.concatenate([top, strip_plane, bottom])
        masks = jnp.stack(
            [
                jnp.stack(
                    [
                        strip_plane
                        == lax.slice_in_dim(strip_tall, REACH + s * d, REACH + s * d + 2 * rows)
                        for s in (-1, 1)
                    ]
                )
                for d in spreads
            ]
        )
        masks = jnp.broadcast_to(masks[..., None], (3, 2, 2 * rows, 128)).astype(BF)
        info = jnp.stack([iy, ix, ik, cut, iz]).astype(jnp.int32)


    local_ids = image_ids.T.reshape(pixels)
    image_range = jnp.arange(images, dtype=jnp.int32)
    table = local_ids[:, None] == image_range[None, :]

    point_view = point_weight.reshape(zs, 2, 2, share, feat)
    atrous_view = atrous_weight.reshape(3, 3, 3, zs, 2, 2, share, feat)

    def forward(units):
        shape = (2, cols, rows, feat)
        return call(
            partial(forward_kernel, units, spreads, mine),
            "forward_taps",
            2 * 2048 * mine * 256 * 15,
            [SMEM] + [ANY] * 8 + [VMEM] * 3 + [ANY] * 2,
            [jax.ShapeDtypeStruct(shape, F32), jax.ShapeDtypeStruct(shape, BF)] * 2,
            [
                pltpu.VMEM((32 + 2 * REACH, 2 * PAD + 128, mine), BF),
                pltpu.VMEM((zs, share, feat), BF),
                pltpu.VMEM((2, 3, 3, zs, share, feat), BF),
                pltpu.VMEM((8, 128, feat), F32),
                pltpu.SemaphoreType.DMA((16,)),
                pltpu.SemaphoreType.DMA((2, 9)),
            ],
            [info, *mains, *halos, masks, point_view, atrous_view],
        )

    def reduce_first(parts):
        keep_x, send_x, keep_y, send_y = parts
        return keep_x, swap(send_x, "x"), keep_y, swap(send_y, "y")

    def reduce_middle(parts):
        keep_x, got_x, keep_y, got_y = parts
        more_x = (keep_x[1] + got_x[1].astype(F32)).astype(BF)
        more_y = (keep_y[1] + got_y[1].astype(F32)).astype(BF)
        return more_x, more_y

    def reduce_last(parts, last_x, last_y):
        keep_x, got_x, keep_y, got_y = parts
        value_x = keep_x[0] + got_x[0].astype(F32) + last_x.astype(F32)
        value_y = keep_y[0] + got_y[0].astype(F32) + last_y.astype(F32)
        return [value_x.reshape(pixels, feat), value_y.reshape(pixels, feat)]

    early = forward([None, 0])
    early_got = reduce_first(early)
    late = forward([1, 2])
    early_got, late = lax.optimization_barrier((early_got, late))
    late_got = reduce_first(late)
    early_more = reduce_middle(early_got)
    early_last = [swap(early_more[0], "y"), swap(early_more[1], "x")]

    half = share // 2
    strip_table = strip_plane[:, None] == image_range[None, :]
    with jax.named_scope("across"):
        mains_late, early_last = lax.optimization_barrier((mains, early_last))
        if aligned:
            across, row_sums, zero_sums = call(
                partial(across_kernel, share),
                "across",
                2 * 10**9,
                [SMEM] + [ANY] * 8,
                [
                    jax.ShapeDtypeStruct((mine // 2, 32 * 2 * rows), BF),
                    jax.ShapeDtypeStruct((2 * rows, mine), F32),
                    jax.ShapeDtypeStruct((1, mine), F32),
                ],
                [
                    pltpu.VMEM((32 + 2 * REACH, 2 * PAD + 128, mine), BF),
                    pltpu.VMEM((2, 2 * rows, mine), F32),
                    pltpu.SemaphoreType.DMA((16,)),
                ],
                [info, *mains_late],
            )
        else:
            columns = []
            for x in range(2):
                for k in range(2):
                    index = [(ik ^ k) * 4 + (iy ^ y) * 2 + (ix ^ x) for y in range(2)]
                    stack = [lax.select_n(n.astype(jnp.int32), *mains_late) for n in index]
                    columns.append(jnp.concatenate(stack, axis=1))
            plane = jnp.concatenate(columns, axis=0)
            in_strip = (jnp.arange(32) >= cut)[:, None, None]
            row_sums = jnp.sum(jnp.where(in_strip, plane.astype(F32), 0.0), axis=0)
            zero_sums = jnp.sum(jnp.where(in_strip, 0.0, plane.astype(F32)), axis=(0, 1))[None]
            plane = plane.reshape(32, 2 * rows, zs, 2, half)
            plane = lax.dynamic_index_in_dim(plane, ik, 3, False)
            across = plane.reshape(32 * 2 * rows, mine // 2).T

    with jax.named_scope("image_sums"):
        sums = lax.dot_general(
            strip_table.astype(F32),
            row_sums,
            (((0,), (0,)), ((), ())),
            precision=lax.Precision.HIGHEST,
        )
        sums = jnp.where(image_range[:, None] == 0, zero_sums, sums)
        pool_mine = pool_weight.reshape(zs, 2, 2, share, feat)
        pool_mine = lax.dynamic_slice(
            pool_mine, (0, iy, ix, 0, 0), (zs, 1, 1, share, feat)
        ).reshape(mine, feat)
        per_image_part = 0.5 * exact(sums, pool_mine.astype(F32))
        strip_rows = jnp.sum(strip_table.astype(F32), axis=0)
        strip_rows = jnp.where((iy == 0) & (ix == 0) & (ik == 0), strip_rows, 0.0)
        strip_rows = jnp.pad(strip_rows, (0, -images % feat)).reshape(-1, feat)

    late_got, across, sums = lax.optimization_barrier((late_got, across, sums))
    late_more = reduce_middle(late_got)
    branches = reduce_last(early_got, *early_last)
    branches += reduce_last(late_got, swap(late_more[0], "y"), swap(late_more[1], "x"))

    first = jnp.concatenate([moments(value) for value in branches], axis=0)
    first = allsum(jnp.concatenate([first, per_image_part, strip_rows], axis=0))
    strip_rows = first[8 + images :].reshape(-1)[:images]
    counts = jnp.where(
        image_range == 0,
        (cut * (rows * row_count)).astype(F32),
        strip_rows * (4 * cols - cut).astype(F32),
    )
    per_image = first[8 : 8 + images] / counts[:, None]
    first = first[:8].reshape(4, 2, feat).transpose(1, 0, 2).reshape(2, 4 * feat)
    weighted = counts[:, None] * per_image
    pool_stats = jnp.stack([jnp.sum(weighted, axis=0), jnp.sum(weighted * per_image, axis=0)])
    four = 4 * feat
    flat_gain, flat_shift = bn_gain[:4].reshape(four), bn_shift[:4].reshape(four)
    mean = first[0] / total
    scale = lax.rsqrt(first[1] / total - mean * mean + EPSILON)
    normed = (jnp.concatenate(branches, axis=1) - mean) * scale
    lifted = normed * flat_gain + flat_shift
    mean4 = pool_stats[0] / total
    scale4 = lax.rsqrt(pool_stats[1] / total - mean4 * mean4 + EPSILON)
    normed4 = (per_image - mean4) * scale4
    lifted4 = normed4 * bn_gain[4] + bn_shift[4]
    joined = smooth(lifted).astype(BF)
    joined4 = smooth(lifted4).astype(BF)
    table_float = table.astype(F32)
    head = dot(joined, project_weight[:four]) + exact(
        table_float, dot(joined4, project_weight[four:])
    )
    head_stats = allsum(moments(head))
    head_mean = head_stats[0] / total
    head_scale = lax.rsqrt(head_stats[1] / total - head_mean * head_mean + EPSILON)
    head_norm = (head - head_mean) * head_scale
    head_lift = head_norm * bn_gain[5] + bn_shift[5]
    output = smooth(head_lift).astype(BF).reshape(cols, rows, feat)
    cotangent = out_grad.transpose(1, 0, 2).reshape(pixels, feat).astype(F32)
    head_grad = cotangent * smooth_slope(head_lift)
    head_back = allsum(
        jnp.stack([jnp.sum(head_grad, axis=0), jnp.sum(head_grad * head_norm, axis=0)])
    )
    head_slope = (
        bn_gain[5]
        * head_scale
        * (head_grad - head_back[0] / total - head_norm * head_back[1] / total)
    ).astype(BF)
    joined_grad = lax.dot_general(
        head_slope, project_weight[:four], (((1,), (1,)), ((), ())), preferred_element_type=F32
    )
    grads = joined_grad * smooth_slope(lifted)
    image_heads = jnp.einsum(
        "pi,pf->if", table.astype(BF), head_slope, preferred_element_type=F32
    )
    rear = jnp.concatenate(
        [
            jnp.stack([jnp.sum(grads, axis=0), jnp.sum(grads * normed, axis=0)]).reshape(8, feat),
            image_heads,
        ],
        axis=0,
    )
    rear = allsum(rear)
    shift_back, gain_back = rear[:4].reshape(four), rear[4:8].reshape(four)
    slopes = (
        flat_gain * scale * (grads - shift_back / total - normed * gain_back / total)
    ).astype(BF)

    with jax.named_scope("project_grad"):
        project_inputs = joined, head_slope

    with jax.named_scope("spread_slopes"):
        point_tile, *tiles_out = [
            slopes[:, k * feat : (k + 1) * feat].reshape(cols, rows, feat) for k in range(4)
        ]
        brim = beyond(rim(tiles_out[0], 16), 0, 0)
        deep = rim(tiles_out[2], 32)
        brims = jnp.concatenate([rim(tiles_out[1], 16), deep[:, :16], deep[:, 16:]], axis=2)
        brims = beyond(brims, 0, 0)

        def both_cores(got):
            return got + [swap(g, "k") for g in got]

        tile3 = jnp.concatenate([tiles_out[0], brim], axis=1)
        got3 = [tile3, swap(tile3, "x"), swap(tile3, "y"), crossed(tile3)]
        left, right = gate(project_inputs, tile3)
        project_part = lax.dot_general(
            left, right, (((0,), (0,)), ((), ())), preferred_element_type=F32
        )
        blocks = project_part.astype(BF).reshape(4, feat, feat)
        blocks = lax.all_to_all(blocks, ("x", "k"), 0, 0)
        across, blocks = lax.optimization_barrier((across, blocks))
        project_sum = jnp.sum(blocks.astype(F32), axis=0)
        project_low = project_sum.astype(BF)
        project_got = z_swap(project_low, 1)
        got3, brims = lax.optimization_barrier((got3, brims))
        edges = [brims[:, :, i * feat : (i + 1) * feat] for i in range(3)]
        tile2 = jnp.concatenate([tiles_out[1], edges[0]], axis=1)
        tile1 = jnp.concatenate([tiles_out[2], edges[1], edges[2], point_tile], axis=1)
        group3 = both_cores(got3)
        tile2, group3, output = lax.optimization_barrier((tile2, group3, output))
        output = output.transpose(1, 0, 2)
        arrived2 = [tile2, swap(tile2, "x"), swap(tile2, "y"), crossed(tile2)]

    rear, sums = gate((rear, sums), tile3)
    image_heads = rear[8:]
    grads4 = smooth_slope(lifted4) * exact(image_heads, project_weight[four:].astype(F32).T)
    shift4, gain4 = jnp.sum(grads4, axis=0), jnp.sum(grads4 * normed4, axis=0)
    image_slope = (
        bn_gain[4]
        * scale4
        * (grads4 - counts[:, None] * (shift4 / total + normed4 * gain4 / total))
    )
    image_low = image_slope.astype(BF)
    spread_back = (
        lax.dot_general(
            image_low, pool_mine, (((1,), (1,)), ((), ())), preferred_element_type=F32
        )
        / counts[:, None]
    )
    strip_back = exact(strip_table.astype(F32), spread_back)
    sums_mine = lax.dynamic_index_in_dim(sums.reshape(images, zs, 2, half), ik, 2, False)
    pool_part = lax.dot_general(
        sums_mine.reshape(images, mine // 2),
        image_low.astype(F32) / counts[:, None],
        (((0,), (0,)), ((), ())),
        precision=lax.Precision.HIGHEST,
    )

    def weight_grad(b, tiles, lanes_at, more=()):
        taps = 8 + len(lanes_at) + len(more)
        return call(
            partial(weight_kernel, spreads[b], b, lanes_at, feat),
            "weight_taps",
            2 * 4096 * (mine // 2) * 256 * 15,
            [SMEM] + [ANY] * 8 + [VMEM] * (2 + len(more)),
            [jax.ShapeDtypeStruct((2, taps, half, feat), BF)] * 2
            if zs == 4
            else [jax.ShapeDtypeStruct((zs, taps, half, feat), BF)],
            [
                pltpu.VMEM((len(lanes_at), 32 + 2 * REACH, 2 * PAD + 128, feat), BF),
                pltpu.VMEM((zs, taps, half, feat), BF),
                pltpu.SemaphoreType.DMA((2, 16)),
                pltpu.SemaphoreType.DMA((4,)),
            ],
            [info, *tiles, masks, across, *more],
            out_specs=[ANY] * (2 if zs == 4 else 1),
        )

    def collect(pieces, first, buffer):
        count = 9 if buffer else 18
        extras = [1, 1] if buffer else [pieces[0].shape[0] - count]
        grad = jax.ShapeDtypeStruct((27, 4, half, feat), F32)
        sides = [jax.ShapeDtypeStruct((4, n, half, feat), F32) for n in extras]
        return call(
            partial(collect_kernel, first, count, extras),
            "collect",
            6 * 10**9,
            [SMEM] + [VMEM] * 4 + [ANY] * len(buffer),
            [grad, *sides],
            [pltpu.VMEM((count, 4, half, feat), F32), pltpu.SemaphoreType.DMA],
            [places, *pieces, *buffer],
            out_specs=[ANY] + [VMEM] * len(extras),
            aliases={5: 0} if buffer else {},
        )

    def scatter_first(part):
        if zs != 4:
            return lax.psum_scatter(part[0], "z", scatter_dimension=0, tiled=True), None
        return part[0], z_swap(part[1], 1)

    def scatter_second(state):
        keep, got = state
        if zs != 4:
            return keep, None
        more = (keep[1].astype(F32) + got[1].astype(F32)).astype(BF)
        return keep[0].astype(F32) + got[0].astype(F32), z_swap(more, 3)

    def scatter_last(state):
        keep, got = state
        if zs != 4:
            return keep[0]
        return (keep + got.astype(F32)).astype(BF)

    across, pool_part, spread_back, strip_back = lax.optimization_barrier(
        (across, pool_part, spread_back, strip_back)
    )
    part3 = weight_grad(0, group3, [(0, 16)])
    arrived2, part3, project_got = lax.optimization_barrier((arrived2, part3, project_got))
    project_sum = project_low.astype(F32) + project_got.astype(F32)
    step = 2
    while step < zs // 2:
        project_sum = project_sum + z_swap(project_sum, step)
        step *= 2
    project_low = project_sum.astype(BF)
    project_got = z_swap(project_low, step)
    group2 = both_cores(arrived2)
    tile1, group2 = lax.optimization_barrier((tile1, group2))
    arrived1 = [tile1, swap(tile1, "x"), swap(tile1, "y"), crossed(tile1)]
    sums3 = scatter_first(part3)
    part2 = weight_grad(1, group2, [(0, 16)])
    part2, group2, project_got, sums3 = lax.optimization_barrier(
        (part2, group2, project_got, sums3)
    )
    sums2, sums3 = scatter_first(part2), scatter_second(sums3)
    project_low = (project_low.astype(F32) + project_got.astype(F32)).astype(BF)
    project_low = gate(project_low, part2)

    def input_part(chosen, groups, pointed, more, outs):
        n = len(chosen)
        scratch = [
            pltpu.VMEM((n, 32 + 2 * REACH, 2 * PAD + 128, feat), BF),
            pltpu.VMEM((n, 3, zs, share, 3 * feat), BF),
        ]
        if pointed:
            scratch += [pltpu.VMEM((zs, share, feat), BF), pltpu.VMEM((2, 8, 128, mine), F32)]
        scratch += [pltpu.SemaphoreType.DMA((n, 16)), pltpu.SemaphoreType.DMA((n, 9))]
        return call(
            partial(input_kernel, chosen, spreads, feat, pointed),
            "input_taps",
            2 * 2048 * mine * 256 * 20,
            [SMEM] + [ANY] * 8 * len(groups) + [VMEM] + [ANY] * 2 + [VMEM] * len(more),
            outs,
            scratch,
            [info, *[t for g in groups for t in g], masks, point_view, atrous_view, *more],
        )

    with jax.named_scope("input_grad"):
        sums_so_far = input_part(
            [(0, 0, 0, 16), (1, 1, 0, 16)],
            [group3, group2],
            False,
            [],
            jax.ShapeDtypeStruct((2, cols, 2 * rows, mine), F32),
        )
    arrived1, sums_so_far, sums2, sums3 = lax.optimization_barrier(
        (arrived1, sums_so_far, sums2, sums3)
    )
    group1 = both_cores(arrived1)
    sums2 = scatter_second(sums2)
    project_got = swap(gate(project_low, arrived1), "y")
    part1 = weight_grad(2, group1, [(0, 32), (96, 0)], [pool_part])
    sums3, sums2, project_got, part1 = lax.optimization_barrier(
        (sums3, sums2, project_got, part1)
    )
    project_sum = project_low.astype(F32) + project_got.astype(F32)
    project_sum = project_sum.astype(BF).reshape(feat // half, half, feat)
    joint = jnp.concatenate([scatter_last(sums3), scatter_last(sums2), project_sum], axis=0)
    joint_x = swap(joint, "x")
    sums1 = scatter_first(part1)
    with jax.named_scope("input_grad"):
        group1, part1 = lax.optimization_barrier((group1, part1))
        shape = jax.ShapeDtypeStruct((cols, rows, mine), BF)
        own, to_x, to_y, to_d = input_part(
            [(2, 0, 0, 32), (None, 0, 96, 0)],
            [group1],
            True,
            [sums_so_far, spread_back[:1], strip_back],
            [shape] * 4,
        )
        sums1, joint_x = gate((sums1, joint_x), own)
        got = [own, swap(to_x, "x"), swap(to_y, "y"), crossed(to_d)]
        sums1 = scatter_second(sums1)
        joint, joint_x = lax.optimization_barrier((joint, joint_x))
        pieces32 = [joint, swap(joint, "k"), joint_x, swap(joint_x, "k")]
        grad, project_all = collect(pieces32, 0, [])
        got, sums1, grad = lax.optimization_barrier((got, sums1, grad))
        if aligned:
            input_turned = call(
                partial(unpack_kernel, share),
                "unpack",
                4 * 10**9,
                [SMEM] + [VMEM] * 4,
                jax.ShapeDtypeStruct((cols, rows, chans), BF),
                [],
                [places, *got],
            )
        else:
            planes = []
            for y in range(2):
                for x in range(2):
                    index = ((iy ^ y) * 2 + (ix ^ x)).astype(jnp.int32)
                    planes.append(lax.select_n(index, *got).reshape(cols, rows, zs, share))
            input_turned = jnp.stack(planes, axis=3).reshape(cols, rows, chans)
        input_grad = input_turned.transpose(1, 0, 2)

    with jax.named_scope("project_grad"):
        project_pool = lax.dot_general(
            joined4.astype(F32),
            image_heads,
            (((0,), (0,)), ((), ())),
            precision=lax.Precision.HIGHEST,
        )
        project_grad = jnp.concatenate([project_all.reshape(four, feat), project_pool], axis=0)

    done = scatter_last(sums1)
    done_x = swap(done, "x")
    done_x, grad, input_grad = lax.optimization_barrier((done_x, grad, input_grad))
    pieces1 = [done, swap(done, "k"), done_x, swap(done_x, "k")]
    grad, point_grad, pool_grad = collect(pieces1, 18, [grad])
    atrous_grad = grad.reshape(3, 3, 3, 4 * half, feat)
    point_grad, pool_grad = (v.reshape(4 * half, feat) for v in (point_grad, pool_grad))

    gain_grad = jnp.concatenate([rear[4:8], gain4[None], head_back[1][None]], axis=0)
    shift_grad = jnp.concatenate([rear[:4], shift4[None], head_back[0][None]], axis=0)
    return (
        output,
        input_grad,
        point_grad,
        atrous_grad,
        pool_grad,
        project_grad,
        gain_grad,
        shift_grad,
    )


def solution(mesh):
    row, col = mesh.devices.shape
    fine = Mesh(mesh.devices.reshape(row // 2, 2, col // 2, 2), ("z", "y", "x", "k"))
    rows, cols = ("z", "y"), ("x", "k")
    placed = (
        P(rows, cols, None),
        P(rows, cols),
        P(),
        P(),
        P(),
        P(),
        P(),
        P(),
        P(rows, cols, None),
    )
    return jax.shard_map(
        per_device,
        mesh=fine,
        in_specs=placed,
        out_specs=(
            P(rows, cols, None),
            P(rows, cols, None),
            P(rows, None),
            P(None, None, None, rows, None),
            P(rows, None),
            P(),
            P(),
            P(),
        ),
        check_vma=False,
    )
```

```python
from functools import partial

import jax
import jax.numpy as jnp
from jax import lax
from jax.experimental import pallas as pl
from jax.experimental.pallas import tpu as pltpu
from jax.sharding import Mesh, PartitionSpec as P

REACH = 18
IMG_ROWS = 32
EPSILON = 1e-05
PAD = 32
RIM = 24
SWAP = [(0, 1), (1, 0)]
BF = jnp.bfloat16
F32 = jnp.float32
VMEM_LIMIT = 60 * 2**20


def dot(a, b):
    return jnp.dot(a, b, preferred_element_type=F32)


def exact(a, b):
    return jnp.dot(a, b, precision=lax.Precision.HIGHEST, preferred_element_type=F32)


def gate(x, *deps):
    return lax.optimization_barrier((x, deps))[0]


def swap(x, axis):
    return lax.ppermute(x, axis, SWAP)


def z_swap(x, step):
    count = lax.axis_size("z")
    return lax.ppermute(x, "z", [(i, i ^ step) for i in range(count)])


def crossed(x):
    return lax.ppermute(x, ("y", "x"), [(i, 3 - i) for i in range(4)])


def quad(x, axes):
    near, far, last = (
        lax.ppermute(x, axes, [(i, i ^ step) for i in range(4)]) for step in (1, 2, 3)
    )
    return (x + near) + (far + last)


def z_sum(x):
    count = lax.axis_size("z")
    if count == 4:
        return quad(x, "z")
    step = 1
    while step < count:
        x = x + lax.ppermute(x, "z", [(i, i ^ step) for i in range(count)])
        step *= 2
    return x


def plane_sum(x):
    return quad(x, ("y", "x"))


def allsum(x):
    x = plane_sum(z_sum(x))
    return x + swap(x, "k")


def smooth(value):
    return jax.nn.gelu(value, approximate=True)


def smooth_slope(value):
    root = 0.7978845608028654
    square = value * value
    tanh = jnp.tanh(root * (value + 0.044715 * value * square))
    return 0.5 * (1.0 + tanh) + 0.5 * value * (1.0 - tanh * tanh) * root * (
        1.0 + 3 * 0.044715 * square
    )


def moments(value):
    return jnp.stack([jnp.sum(value, axis=0), jnp.sum(value * value, axis=0)])


def place_of(info, n):
    dk, dy, dx = n // 4, n // 2 % 2, n % 2
    col = ((info[1] ^ dx) * 2 + (info[2] ^ dk)) * 8
    return REACH + col, info[0] ^ dy


def tile_copies(info, tiles, window, sems, main=0, rim=0):
    copies = []
    for n, tile in enumerate(tiles):
        col, y = place_of(info, n)
        row = pl.multiple_of(PAD + y * 64, 16)
        copies.append(
            pltpu.make_async_copy(
                tile.at[:, pl.ds(main, 64)],
                window.at[pl.ds(col, 8), pl.ds(row, 64)],
                sems.at[n],
            )
        )
        if rim:
            row = pl.multiple_of(jnp.where(y == 0, PAD + 128, PAD - rim), 16)
            copies.append(
                pltpu.make_async_copy(
                    tile.at[:, pl.ds(main + 64, rim)],
                    window.at[pl.ds(col, 8), pl.ds(row, rim)],
                    sems.at[8 + n],
                )
            )
    for copy in copies:
        copy.start()
    return copies


def place_rims(info, rims, window):
    for dk, rim in enumerate(rims):
        for n in range(4):
            col = REACH + ((n % 2) * 2 + (info[2] ^ dk)) * 8
            row = PAD + 128 if n < 2 else PAD - REACH
            for q in range(8):
                window[col + q, row : row + REACH, :] = rim[n, q, :REACH]


def shift_rows(window, masks, b, q, i, spread, sign, cut, ok=None):
    start = PAD + sign * (i - 1) * spread
    value = window[REACH + q, start : start + 128, :]
    if i != 1:
        keep = masks[b, 1 if sign * (i - 1) > 0 else 0]
        keep = jnp.where(q >= cut, keep, jnp.ones_like(keep))
        if ok is not None:
            keep = jnp.where(ok, keep, jnp.zeros_like(keep))
        value = value * jnp.concatenate([keep] * (value.shape[1] // 128), axis=1)
    elif ok is not None:
        value = jnp.where(ok, value, jnp.zeros_like(value))
    return value


def tap_rows(window, masks, b, col, width, spread, sign, cut):
    return jnp.concatenate(
        [
            jnp.concatenate(
                [shift_rows(window, masks, b, col + u, i, spread, sign, cut) for i in range(3)],
                axis=1,
            )
            for u in range(width)
        ],
        axis=0,
    )


def branch_sum(window, masks, b, col, spread, sign, cut, product, acc, fresh):
    width = 2

    def inside(j, e):
        source = col + e + sign * (j - 1) * spread
        return (source >= 0) & (source < 32) & ((source < cut) == (col + e < cut))

    def center(e):
        return product(1, tap_rows(window, masks, b, col + e, width, spread, sign, cut))

    def side(j, e):
        source = col + e + sign * (j - 1) * spread
        part = product(j, tap_rows(window, masks, b, source, width, spread, sign, cut))
        return jnp.concatenate(
            [
                jnp.where(inside(j, e + u), part[u * 128 : u * 128 + 128], 0.0)
                for u in range(width)
            ],
            axis=0,
        )

    def put(e, value, first):
        value = value.reshape(width, 128, acc.shape[-1])
        if first:
            acc[pl.ds(e, width)] = value
        else:
            acc[pl.ds(e, width)] += value

    dense = spread == REACH // 3
    for e in range(0, 8, width):
        value = center(e)
        if dense:
            value = value + side(0, e) + side(2, e)
        put(e, value, fresh)
    if dense:
        return

    def block(t, carry):
        j, half = (t // 2) * 2, (t % 2) * 4
        some = inside(j, half)
        for e in range(1, 4):
            some = some | inside(j, half + e)

        @pl.when(some)
        def _():
            for e in range(0, 4, width):
                put(half + e, side(j, half + e), False)

        return carry

    lax.fori_loop(0, 4, block, 0)


def forward_kernel(units, spreads, lanes, info, *refs):
    mains, rims = refs[:8], refs[8:10]
    masks, point, weights = refs[10:13]
    outs = refs[13:17]
    window, point_buf, weight_buf, acc, sems, weight_sems = refs[17:]
    iy, ix, ik, cut = info[0], info[1], info[2], info[3]
    copies = tile_copies(info, mains, window, sems)
    loads = []
    for n, b in enumerate(units):
        if b is None:
            loads.append(
                [pltpu.make_async_copy(point.at[:, iy, ix], point_buf, weight_sems.at[n, 0])]
            )
        else:
            loads.append(
                [
                    pltpu.make_async_copy(
                        weights.at[b, i, j, :, iy, ix],
                        weight_buf.at[n, j, i],
                        weight_sems.at[n, 3 * j + i],
                    )
                    for j in range(3)
                    for i in range(3)
                ]
            )
        for copy in loads[n]:
            copy.start()
    place_rims(info, rims, window)
    for copy in copies:
        copy.wait()
    for n, b in enumerate(units):
        for copy in loads[n]:
            copy.wait()
        keep, send = outs[2 * n : 2 * n + 2]
        for dx in (1, 0):
            col = (ix ^ dx) * 16 + ik * 8
            if b is None:
                source = window[pl.ds(REACH + col, 8), PAD : PAD + 128, :].reshape(1024, lanes)
                acc[...] = dot(source, point_buf[...].reshape(lanes, 256)).reshape(8, 128, 256)
            else:

                def product(j, rows, n=n):
                    return dot(rows, weight_buf[n, j].reshape(3 * lanes, 256))

                branch_sum(window, masks, b, col, spreads[b], 1, cut, product, acc, True)
            for dy in range(2):
                row = pl.multiple_of((iy ^ dy) * 64, 64)
                value = acc[:, pl.ds(row, 64), :]
                if (dy if n else dx) == 0:
                    keep[dx if n else dy] = value
                else:
                    send[dx if n else dy] = value.astype(BF)


def input_kernel(chosen, spreads, lanes, pointed, info, *refs):
    count = 8 * (1 + max(c[1] for c in chosen))
    tiles, masks, point, weights = refs[:count], refs[count], refs[count + 1], refs[count + 2]
    rest = refs[count + 3 :]
    if pointed:
        before, edge, strip = rest[:3]
        outs = rest[3:7]
        windows, weight_buf, point_buf, acc, sems, weight_sems = rest[7:]
    else:
        (result,) = rest[:1]
        windows, weight_buf, sems, weight_sems = rest[1:]
        acc = result
    iy, ix, ik, cut = info[0], info[1], info[2], info[3]
    mine = acc.shape[-1]
    fetches, loads = [], []
    for n, (b, first, main, rim) in enumerate(chosen):
        group = tiles[8 * first : 8 * first + 8]
        fetches.append(tile_copies(info, group, windows.at[n], sems.at[n], main, rim))
        if b is None:
            loads.append(
                [pltpu.make_async_copy(point.at[:, iy, ix], point_buf, weight_sems.at[n, 0])]
            )
        else:
            loads.append(
                [
                    pltpu.make_async_copy(
                        weights.at[b, i, j, :, iy, ix],
                        weight_buf.at[n, j, :, :, pl.ds(i * lanes, lanes)],
                        weight_sems.at[n, 3 * j + i],
                    )
                    for j in range(3)
                    for i in range(3)
                ]
            )
        for copy in loads[n]:
            copy.start()

    def times(a, w):
        return lax.dot_general(
            a, w.reshape(mine, w.shape[-1]), (((1,), (1,)), ((), ())), preferred_element_type=F32
        )

    for n, (b, _, _, _) in enumerate(chosen):
        for copy in fetches[n] + loads[n]:
            copy.wait()
        window = windows.at[n]
        for dx in range(2):
            col = (ix ^ dx) * 16 + ik * 8
            if b is None:
                for e in range(0, 8, 2):
                    source = window[pl.ds(REACH + col + e, 2), PAD : PAD + 128, :]
                    value = times(source.reshape(256, lanes), point_buf[...])
                    for u in range(2):
                        pool = jnp.where(col + e + u < cut, edge[...], strip[...])
                        acc[dx, e + u] += (
                            before[dx, e + u] + value[u * 128 : u * 128 + 128] + pool
                        )
            else:

                def product(j, rows, n=n):
                    return times(rows, weight_buf[n, j])

                branch_sum(
                    window, masks, b, col, spreads[b], -1, cut, product, acc.at[dx], n == 0
                )
    if pointed:
        for dx in range(2):
            for dy in range(2):
                row = pl.multiple_of((iy ^ dy) * 64, 64)
                outs[dy * 2 + dx][...] = acc[dx, :, pl.ds(row, 64), :].astype(BF)


def weight_kernel(spread, b, sources, lanes, info, *refs):
    tiles = refs[:8]
    masks, across = refs[8:10]
    pooled = len(sources) > 1
    outs = refs[10 + pooled : -4]
    windows, out, sems, out_sems = refs[-4:]
    cut = info[3]
    parts = out.shape[0]
    each = out.shape[2]
    paired = len(outs) == 2
    fetches = [
        tile_copies(info, tiles, windows.at[n], sems.at[n], main, rim)
        for n, (main, rim) in enumerate(sources)
    ]

    def emit(t, value):
        for z in range(parts):
            out[info[4] ^ z if paired else z, t] = value[z * each : (z + 1) * each].astype(BF)

    for copy in fetches[0]:
        copy.wait()
    window = windows.at[0]
    for j in (1, 0, 2):
        move = (j - 1) * spread
        columns = [p for p in range(32) if 0 <= p + move < 32]
        total = None
        for at in range(0, len(columns), 8):
            group = columns[at : at + 8]
            right = []
            for p in group:
                ok = None if j == 1 else ((p < cut) == (p + move < cut))
                right.append(
                    jnp.concatenate(
                        [shift_rows(window, masks, b, p, i, spread, -1, cut, ok) for i in range(3)],
                        axis=1,
                    )
                )
            first, last = (group[0] + move) * 128, (group[-1] + move + 1) * 128
            part = dot(across[:, first:last], jnp.concatenate(right, axis=0))
            total = part if total is None else total + part
        for i in range(3):
            emit(3 * i + j, total[:, i * lanes : (i + 1) * lanes])
    if len(sources) > 1:
        for copy in fetches[1]:
            copy.wait()
        plain = windows[1, REACH : REACH + 32, PAD : PAD + 128, :].reshape(32 * 128, lanes)
        emit(9, dot(across[...], plain))
        emit(10, refs[10][...])
    if paired:
        moves = [(0, outs[0].at[0]), (3, outs[0].at[1]), (1, outs[1].at[0]), (2, outs[1].at[1])]
        moves = [(out.at[m], target) for m, target in moves]
    else:
        moves = [(out, outs[0])]
    copies = [
        pltpu.make_async_copy(source, target, out_sems.at[n])
        for n, (source, target) in enumerate(moves)
    ]
    for copy in copies:
        copy.start()
    for copy in copies:
        copy.wait()


def collect_kernel(first, count, extras, info, *refs):
    pieces = refs[:4]
    outs = refs[len(refs) - 3 - len(extras) : len(refs) - 2]
    buf, sem = refs[len(refs) - 2 :]
    ix, ik = info[1], info[2]
    if len(extras) == 1:
        outs[1][4] = refs[4][...]
    for n, piece in enumerate(pieces):
        index = (ix ^ (n // 2)) * 2 + (ik ^ (n % 2))
        for t in range(count):
            buf[t, index] = piece[t].astype(F32)
        at = count
        for e, length in enumerate(extras):
            for t in range(length):
                outs[1 + e][index, t] = piece[at + t].astype(F32)
            at += length
    copy = pltpu.make_async_copy(buf, outs[0].at[pl.ds(first, count)], sem)
    copy.start()
    copy.wait()


def pack_kernel(share, info, full, marks, *refs):
    iy, ix = info[0], info[1]
    rims = refs[4]
    for n in range(4):
        other = (iy ^ (n // 2)) * 2 + (ix ^ (n % 2))
        for z in range(full.shape[-1] // (4 * share)):
            lane = pl.multiple_of((z * 4 + other) * share, 128)
            value = jnp.swapaxes(full[:, :, pl.ds(lane, share)], 0, 1)
            refs[n][:, :, z * share : (z + 1) * share] = value

            @pl.when(iy == 0)
            def _(value=value, other=other, z=z):
                rims[other, :, :RIM, z * share : (z + 1) * share] = value[:, :RIM]

            @pl.when(iy == 1)
            def _(value=value, other=other, z=z):
                rims[other, :, :REACH, z * share : (z + 1) * share] = value[:, 64 - REACH :]

    for n in range(4):
        for q in range(8):
            rims[n, q, REACH : REACH + 1, :] = marks[...]


def unpack_kernel(share, info, *refs):
    iy, ix = info[0], info[1]
    full = refs[4]
    for n in range(4):
        other = (iy ^ (n // 2)) * 2 + (ix ^ (n % 2))
        for z in range(full.shape[-1] // (4 * share)):
            lane = pl.multiple_of((z * 4 + other) * share, 128)
            value = refs[n][:, :, z * share : (z + 1) * share]
            full[:, :, pl.ds(lane, share)] = jnp.swapaxes(value, 0, 1)


def across_kernel(share, info, *refs):
    tiles, out, rows, zero = refs[:8], *refs[8:11]
    window, acc, sems = refs[11:]
    ik, cut = info[2], info[3]
    for copy in tile_copies(info, tiles, window, sems):
        copy.wait()
    acc[...] = jnp.zeros_like(acc)
    for q in range(32):
        value = window[REACH + q, PAD : PAD + 128, :]
        turned = value.T
        for z in range(turned.shape[0] // share):
            low = turned[z * share : z * share + share // 2]
            high = turned[z * share + share // 2 : (z + 1) * share]
            out[z * share // 2 : (z + 1) * share // 2, q * 128 : (q + 1) * 128] = jnp.where(
                ik == 0, low, high
            )
        acc[(q >= cut).astype(jnp.int32)] += value.astype(F32)
    rows[...] = acc[1]
    zero[...] = jnp.sum(acc[0], axis=0, keepdims=True)


VMEM = pl.BlockSpec(memory_space=pltpu.VMEM)
SMEM = pl.BlockSpec(memory_space=pltpu.SMEM)
ANY = pl.BlockSpec(memory_space=pl.ANY)


def call(kernel, name, flops, in_specs, out_shape, scratch, args, out_specs=None, aliases=None):
    return pl.pallas_call(
        kernel,
        name=name,
        in_specs=in_specs,
        out_specs=out_specs or jax.tree.map(lambda _: VMEM, out_shape),
        out_shape=out_shape,
        input_output_aliases=aliases or {},
        scratch_shapes=scratch,
        compiler_params=pltpu.CompilerParams(vmem_limit_bytes=VMEM_LIMIT),
        cost_estimate=pl.CostEstimate(flops=flops, bytes_accessed=10**7, transcendentals=0),
    )(*args)


def per_device(
    feature_map,
    image_ids,
    point_weight,
    atrous_weight,
    pool_weight,
    project_weight,
    bn_gain,
    bn_shift,
    out_grad,
):
    rows, cols, chans = feature_map.shape
    feat = point_weight.shape[1]
    pixels = rows * cols
    zs = lax.axis_size("z")
    axes = ("k", "x", "y", "z")
    iz, iy, ix, ik = (lax.axis_index(a) for a in ("z", "y", "x", "k"))
    row_count = 2 * zs
    total = float(pixels * row_count * 4)
    images = rows * row_count // IMG_ROWS + 1
    share = chans // (4 * zs)
    mine = chans // 4
    spreads = [REACH * (b + 1) // 3 for b in range(3)]
    def pick(first, second, index):
        return jnp.where(index == 0, first, second)

    def rim(x, depth):
        return pick(x[:, :depth], x[:, rows - depth :], iy)

    def beyond(x, dy, dx):
        pairs = []
        for z in range(zs):
            for y in range(2):
                far = z - 1 + 2 * y
                if 0 <= far < zs:
                    for i in range(2):
                        target = (far * 2 + (y ^ dy)) * 2 + (i ^ dx)
                        pairs.append(((z * 2 + y) * 2 + i, target))
        return lax.ppermute(x, ("z", "y", "x"), pairs)

    with jax.named_scope("marks"):
        strip_own = jnp.max(image_ids, axis=1)
        edge_own = pick(strip_own[:REACH], strip_own[rows - REACH :], iy)
        zero_own = jnp.sum((image_ids[0] == 0).astype(jnp.int32))
        marks = jnp.concatenate([strip_own, edge_own, zero_own[None]])
        marks = jnp.pad(marks, (0, mine - marks.shape[0])).astype(BF)[None]

    places = jnp.stack([iy, ix, ik, ik, iz]).astype(jnp.int32)
    aligned = share % 128 == 0
    with jax.named_scope("spread_features"):
        if aligned:
            tile_shape = jax.ShapeDtypeStruct((cols, rows, mine), BF)
            *tiles, brims = call(
                partial(pack_kernel, share),
                "pack",
                0,
                [SMEM, VMEM, VMEM],
                [tile_shape] * 4 + [jax.ShapeDtypeStruct((4, cols, RIM, mine), BF)],
                [],
                [places, feature_map, marks],
            )
        else:
            packed = feature_map.transpose(1, 0, 2).reshape(cols, rows, zs, 2, 2, share)
            packed = packed.transpose(3, 4, 0, 1, 2, 5)
            packed = packed.reshape(4, cols, rows, mine)
            tiles = [
                lax.dynamic_index_in_dim(packed, (iy ^ dy) * 2 + (ix ^ dx), 0, False)
                for dy in range(2)
                for dx in range(2)
            ]
            brims = pick(packed[:, :, :REACH], packed[:, :, rows - REACH :], iy)
            brims = jnp.pad(brims, ((0, 0), (0, 0), (0, RIM - REACH), (0, 0)))
            brims = brims.at[:, :, REACH].set(marks)
        note = jnp.broadcast_to(marks[None, None], (4, cols, 1, mine))
        own, to_x, to_y, to_d = tiles
        mains = [own, swap(to_x, "x"), swap(to_y, "y"), crossed(to_d)]
        halo, mains = lax.optimization_barrier((beyond(brims, 0, 0), mains))
        halo = lax.dynamic_update_slice_in_dim(halo, note, REACH + 1, axis=2)
        halo = lax.all_to_all(halo, ("y", "x"), 0, 0)
        halos = [halo, swap(halo, "k")]

    mains = mains + [swap(g, "k") for g in mains]
    with jax.named_scope("marks"):
        told = jnp.stack([h[:, 0, REACH : REACH + 2] for h in halos]).astype(jnp.int32)
        told = told.reshape(2, 2, 2, 2, mine)
        strips = jnp.max(told[:, :, :, 1, :rows], axis=(0, 2))
        edges = jnp.max(told[:, :, :, 0, rows : rows + REACH], axis=(0, 2))
        cut = jnp.sum(told[:, 0, :, 1, rows + REACH])
        strip_plane = strips.reshape(2 * rows)
        top, bottom = edges[1], edges[0]
        strip_tall = jnp.concatenate([top, strip_plane, bottom])
        masks = jnp.stack(
            [
                jnp.stack(
                    [
                        strip_plane
                        == lax.slice_in_dim(strip_tall, REACH + s * d, REACH + s * d + 2 * rows)
                        for s in (-1, 1)
                    ]
                )
                for d in spreads
            ]
        )
        masks = jnp.broadcast_to(masks[..., None], (3, 2, 2 * rows, 128)).astype(BF)
        info = jnp.stack([iy, ix, ik, cut, iz]).astype(jnp.int32)


    local_ids = image_ids.T.reshape(pixels)
    image_range = jnp.arange(images, dtype=jnp.int32)
    table = local_ids[:, None] == image_range[None, :]

    point_view = point_weight.reshape(zs, 2, 2, share, feat)
    atrous_view = atrous_weight.reshape(3, 3, 3, zs, 2, 2, share, feat)

    def forward(units):
        shape = (2, cols, rows, feat)
        return call(
            partial(forward_kernel, units, spreads, mine),
            "forward_taps",
            2 * 2048 * mine * 256 * 15,
            [SMEM] + [ANY] * 8 + [VMEM] * 3 + [ANY] * 2,
            [jax.ShapeDtypeStruct(shape, F32), jax.ShapeDtypeStruct(shape, BF)] * 2,
            [
                pltpu.VMEM((32 + 2 * REACH, 2 * PAD + 128, mine), BF),
                pltpu.VMEM((zs, share, feat), BF),
                pltpu.VMEM((2, 3, 3, zs, share, feat), BF),
                pltpu.VMEM((8, 128, feat), F32),
                pltpu.SemaphoreType.DMA((16,)),
                pltpu.SemaphoreType.DMA((2, 9)),
            ],
            [info, *mains, *halos, masks, point_view, atrous_view],
        )

    def reduce_first(parts):
        keep_x, send_x, keep_y, send_y = parts
        return keep_x, swap(send_x, "x"), keep_y, swap(send_y, "y")

    def reduce_middle(parts):
        keep_x, got_x, keep_y, got_y = parts
        more_x = (keep_x[1] + got_x[1].astype(F32)).astype(BF)
        more_y = (keep_y[1] + got_y[1].astype(F32)).astype(BF)
        return more_x, more_y

    def reduce_last(parts, last_x, last_y):
        keep_x, got_x, keep_y, got_y = parts
        value_x = keep_x[0] + got_x[0].astype(F32) + last_x.astype(F32)
        value_y = keep_y[0] + got_y[0].astype(F32) + last_y.astype(F32)
        return [value_x.reshape(pixels, feat), value_y.reshape(pixels, feat)]

    early = forward([None, 0])
    early_got = reduce_first(early)
    late = forward([1, 2])
    early_got, late = lax.optimization_barrier((early_got, late))
    late_got = reduce_first(late)
    early_more = reduce_middle(early_got)
    early_last = [swap(early_more[0], "y"), swap(early_more[1], "x")]

    half = share // 2
    strip_table = strip_plane[:, None] == image_range[None, :]
    with jax.named_scope("across"):
        mains_late, early_last = lax.optimization_barrier((mains, early_last))
        if aligned:
            across, row_sums, zero_sums = call(
                partial(across_kernel, share),
                "across",
                2 * 10**9,
                [SMEM] + [ANY] * 8,
                [
                    jax.ShapeDtypeStruct((mine // 2, 32 * 2 * rows), BF),
                    jax.ShapeDtypeStruct((2 * rows, mine), F32),
                    jax.ShapeDtypeStruct((1, mine), F32),
                ],
                [
                    pltpu.VMEM((32 + 2 * REACH, 2 * PAD + 128, mine), BF),
                    pltpu.VMEM((2, 2 * rows, mine), F32),
                    pltpu.SemaphoreType.DMA((16,)),
                ],
                [info, *mains_late],
            )
        else:
            columns = []
            for x in range(2):
                for k in range(2):
                    index = [(ik ^ k) * 4 + (iy ^ y) * 2 + (ix ^ x) for y in range(2)]
                    stack = [lax.select_n(n.astype(jnp.int32), *mains_late) for n in index]
                    columns.append(jnp.concatenate(stack, axis=1))
            plane = jnp.concatenate(columns, axis=0)
            in_strip = (jnp.arange(32) >= cut)[:, None, None]
            row_sums = jnp.sum(jnp.where(in_strip, plane.astype(F32), 0.0), axis=0)
            zero_sums = jnp.sum(jnp.where(in_strip, 0.0, plane.astype(F32)), axis=(0, 1))[None]
            plane = plane.reshape(32, 2 * rows, zs, 2, half)
            plane = lax.dynamic_index_in_dim(plane, ik, 3, False)
            across = plane.reshape(32 * 2 * rows, mine // 2).T

    with jax.named_scope("image_sums"):
        sums = lax.dot_general(
            strip_table.astype(F32),
            row_sums,
            (((0,), (0,)), ((), ())),
            precision=lax.Precision.HIGHEST,
        )
        sums = jnp.where(image_range[:, None] == 0, zero_sums, sums)
        pool_mine = pool_weight.reshape(zs, 2, 2, share, feat)
        pool_mine = lax.dynamic_slice(
            pool_mine, (0, iy, ix, 0, 0), (zs, 1, 1, share, feat)
        ).reshape(mine, feat)
        per_image_part = 0.5 * exact(sums, pool_mine.astype(F32))
        strip_rows = jnp.sum(strip_table.astype(F32), axis=0)
        strip_rows = jnp.where((iy == 0) & (ix == 0) & (ik == 0), strip_rows, 0.0)
        strip_rows = jnp.pad(strip_rows, (0, -images % feat)).reshape(-1, feat)

    late_got, across, sums = lax.optimization_barrier((late_got, across, sums))
    late_more = reduce_middle(late_got)
    branches = reduce_last(early_got, *early_last)
    branches += reduce_last(late_got, swap(late_more[0], "y"), swap(late_more[1], "x"))

    first = jnp.concatenate([moments(value) for value in branches], axis=0)
    first = allsum(jnp.concatenate([first, per_image_part, strip_rows], axis=0))
    strip_rows = first[8 + images :].reshape(-1)[:images]
    counts = jnp.where(
        image_range == 0,
        (cut * (rows * row_count)).astype(F32),
        strip_rows * (4 * cols - cut).astype(F32),
    )
    per_image = first[8 : 8 + images] / counts[:, None]
    first = first[:8].reshape(4, 2, feat).transpose(1, 0, 2).reshape(2, 4 * feat)
    weighted = counts[:, None] * per_image
    pool_stats = jnp.stack([jnp.sum(weighted, axis=0), jnp.sum(weighted * per_image, axis=0)])
    four = 4 * feat
    flat_gain, flat_shift = bn_gain[:4].reshape(four), bn_shift[:4].reshape(four)
    mean = first[0] / total
    scale = lax.rsqrt(first[1] / total - mean * mean + EPSILON)
    normed = (jnp.concatenate(branches, axis=1) - mean) * scale
    lifted = normed * flat_gain + flat_shift
    mean4 = pool_stats[0] / total
    scale4 = lax.rsqrt(pool_stats[1] / total - mean4 * mean4 + EPSILON)
    normed4 = (per_image - mean4) * scale4
    lifted4 = normed4 * bn_gain[4] + bn_shift[4]
    joined = smooth(lifted).astype(BF)
    joined4 = smooth(lifted4).astype(BF)
    table_float = table.astype(F32)
    head = dot(joined, project_weight[:four]) + exact(
        table_float, dot(joined4, project_weight[four:])
    )
    head_stats = allsum(moments(head))
    head_mean = head_stats[0] / total
    head_scale = lax.rsqrt(head_stats[1] / total - head_mean * head_mean + EPSILON)
    head_norm = (head - head_mean) * head_scale
    head_lift = head_norm * bn_gain[5] + bn_shift[5]
    output = smooth(head_lift).astype(BF).reshape(cols, rows, feat)
    cotangent = out_grad.transpose(1, 0, 2).reshape(pixels, feat).astype(F32)
    head_grad = cotangent * smooth_slope(head_lift)
    head_back = allsum(
        jnp.stack([jnp.sum(head_grad, axis=0), jnp.sum(head_grad * head_norm, axis=0)])
    )
    head_slope = (
        bn_gain[5]
        * head_scale
        * (head_grad - head_back[0] / total - head_norm * head_back[1] / total)
    ).astype(BF)
    joined_grad = lax.dot_general(
        head_slope, project_weight[:four], (((1,), (1,)), ((), ())), preferred_element_type=F32
    )
    grads = joined_grad * smooth_slope(lifted)
    image_heads = jnp.einsum(
        "pi,pf->if", table.astype(BF), head_slope, preferred_element_type=F32
    )
    rear = jnp.concatenate(
        [
            jnp.stack([jnp.sum(grads, axis=0), jnp.sum(grads * normed, axis=0)]).reshape(8, feat),
            image_heads,
        ],
        axis=0,
    )
    rear = allsum(rear)
    shift_back, gain_back = rear[:4].reshape(four), rear[4:8].reshape(four)
    slopes = (
        flat_gain * scale * (grads - shift_back / total - normed * gain_back / total)
    ).astype(BF)

    with jax.named_scope("project_grad"):
        project_inputs = joined, head_slope

    with jax.named_scope("spread_slopes"):
        point_tile, *tiles_out = [
            slopes[:, k * feat : (k + 1) * feat].reshape(cols, rows, feat) for k in range(4)
        ]
        brim = beyond(rim(tiles_out[0], 16), 0, 0)
        deep = rim(tiles_out[2], 32)
        brims = jnp.concatenate([rim(tiles_out[1], 16), deep[:, :16], deep[:, 16:]], axis=2)
        brims = beyond(brims, 0, 0)

        def both_cores(got):
            return got + [swap(g, "k") for g in got]

        tile3 = jnp.concatenate([tiles_out[0], brim], axis=1)
        got3 = [tile3, swap(tile3, "x"), swap(tile3, "y"), crossed(tile3)]
        left, right = gate(project_inputs, tile3)
        project_part = lax.dot_general(
            left, right, (((0,), (0,)), ((), ())), preferred_element_type=F32
        )
        blocks = project_part.astype(BF).reshape(4, feat, feat)
        blocks = lax.all_to_all(blocks, ("x", "k"), 0, 0)
        across, blocks = lax.optimization_barrier((across, blocks))
        project_sum = jnp.sum(blocks.astype(F32), axis=0)
        project_low = project_sum.astype(BF)
        project_got = z_swap(project_low, 1)
        got3, brims = lax.optimization_barrier((got3, brims))
        edges = [brims[:, :, i * feat : (i + 1) * feat] for i in range(3)]
        tile2 = jnp.concatenate([tiles_out[1], edges[0]], axis=1)
        tile1 = jnp.concatenate([tiles_out[2], edges[1], edges[2], point_tile], axis=1)
        group3 = both_cores(got3)
        tile2, group3, output = lax.optimization_barrier((tile2, group3, output))
        output = output.transpose(1, 0, 2)
        arrived2 = [tile2, swap(tile2, "x"), swap(tile2, "y"), crossed(tile2)]

    rear, sums = gate((rear, sums), tile3)
    image_heads = rear[8:]
    grads4 = smooth_slope(lifted4) * exact(image_heads, project_weight[four:].astype(F32).T)
    shift4, gain4 = jnp.sum(grads4, axis=0), jnp.sum(grads4 * normed4, axis=0)
    image_slope = (
        bn_gain[4]
        * scale4
        * (grads4 - counts[:, None] * (shift4 / total + normed4 * gain4 / total))
    )
    image_low = image_slope.astype(BF)
    spread_back = (
        lax.dot_general(
            image_low, pool_mine, (((1,), (1,)), ((), ())), preferred_element_type=F32
        )
        / counts[:, None]
    )
    strip_back = exact(strip_table.astype(F32), spread_back)
    sums_mine = lax.dynamic_index_in_dim(sums.reshape(images, zs, 2, half), ik, 2, False)
    pool_part = lax.dot_general(
        sums_mine.reshape(images, mine // 2),
        image_low.astype(F32) / counts[:, None],
        (((0,), (0,)), ((), ())),
        precision=lax.Precision.HIGHEST,
    )

    def weight_grad(b, tiles, lanes_at, more=()):
        taps = 8 + len(lanes_at) + len(more)
        return call(
            partial(weight_kernel, spreads[b], b, lanes_at, feat),
            "weight_taps",
            2 * 4096 * (mine // 2) * 256 * 15,
            [SMEM] + [ANY] * 8 + [VMEM] * (2 + len(more)),
            [jax.ShapeDtypeStruct((2, taps, half, feat), BF)] * 2
            if zs == 4
            else [jax.ShapeDtypeStruct((zs, taps, half, feat), BF)],
            [
                pltpu.VMEM((len(lanes_at), 32 + 2 * REACH, 2 * PAD + 128, feat), BF),
                pltpu.VMEM((zs, taps, half, feat), BF),
                pltpu.SemaphoreType.DMA((2, 16)),
                pltpu.SemaphoreType.DMA((4,)),
            ],
            [info, *tiles, masks, across, *more],
            out_specs=[ANY] * (2 if zs == 4 else 1),
        )

    def collect(pieces, first, buffer, pool=None):
        count = 9 if buffer else 18
        extras = [1, 1] if buffer else [pieces[0].shape[0] - count]
        grad = jax.ShapeDtypeStruct((27, 4, half, feat), F32)
        sides = [jax.ShapeDtypeStruct((4, n, half, feat), F32) for n in extras]
        if pool is not None:
            sides = [jax.ShapeDtypeStruct((5, *pool.shape), F32)]
        given = buffer if pool is None else [pool]
        return call(
            partial(collect_kernel, first, count, extras),
            "collect",
            6 * 10**9,
            [SMEM] + [VMEM] * 4 + [VMEM if pool is not None else ANY],
            [grad, *sides],
            [pltpu.VMEM((count, 4, half, feat), F32), pltpu.SemaphoreType.DMA],
            [places, *pieces, *given],
            out_specs=[ANY] + [VMEM] * len(extras),
            aliases={5: 0} if buffer else {},
        )

    def scatter_first(part):
        if zs != 4:
            return lax.psum_scatter(part[0], "z", scatter_dimension=0, tiled=True), None
        return part[0], z_swap(part[1], 1)

    def scatter_second(state):
        keep, got = state
        if zs != 4:
            return keep, None
        more = (keep[1].astype(F32) + got[1].astype(F32)).astype(BF)
        return keep[0].astype(F32) + got[0].astype(F32), z_swap(more, 3)

    def scatter_last(state):
        keep, got = state
        if zs != 4:
            return keep[0]
        return (keep + got.astype(F32)).astype(BF)

    across, pool_part, spread_back, strip_back = lax.optimization_barrier(
        (across, pool_part, spread_back, strip_back)
    )
    part3 = weight_grad(0, group3, [(0, 16)])
    arrived2, part3, project_got = lax.optimization_barrier((arrived2, part3, project_got))
    project_sum = project_low.astype(F32) + project_got.astype(F32)
    step = 2
    while step < zs // 2:
        project_sum = project_sum + z_swap(project_sum, step)
        step *= 2
    project_low = project_sum.astype(BF)
    project_got = z_swap(project_low, step)
    group2 = both_cores(arrived2)
    tile1, group2 = lax.optimization_barrier((tile1, group2))
    arrived1 = [tile1, swap(tile1, "x"), swap(tile1, "y"), crossed(tile1)]
    sums3 = scatter_first(part3)
    part2 = weight_grad(1, group2, [(0, 16)])
    part2, group2, project_got, sums3 = lax.optimization_barrier(
        (part2, group2, project_got, sums3)
    )
    sums2, sums3 = scatter_first(part2), scatter_second(sums3)
    project_low = (project_low.astype(F32) + project_got.astype(F32)).astype(BF)
    project_low = gate(project_low, part2)

    def input_part(chosen, groups, pointed, more, outs):
        n = len(chosen)
        scratch = [
            pltpu.VMEM((n, 32 + 2 * REACH, 2 * PAD + 128, feat), BF),
            pltpu.VMEM((n, 3, zs, share, 3 * feat), BF),
        ]
        if pointed:
            scratch += [pltpu.VMEM((zs, share, feat), BF), pltpu.VMEM((2, 8, 128, mine), F32)]
        scratch += [pltpu.SemaphoreType.DMA((n, 16)), pltpu.SemaphoreType.DMA((n, 9))]
        return call(
            partial(input_kernel, chosen, spreads, feat, pointed),
            "input_taps",
            2 * 2048 * mine * 256 * 20,
            [SMEM] + [ANY] * 8 * len(groups) + [VMEM] + [ANY] * 2 + [VMEM] * len(more),
            outs,
            scratch,
            [info, *[t for g in groups for t in g], masks, point_view, atrous_view, *more],
        )

    with jax.named_scope("input_grad"):
        sums_so_far = input_part(
            [(0, 0, 0, 16), (1, 1, 0, 16)],
            [group3, group2],
            False,
            [],
            jax.ShapeDtypeStruct((2, cols, 2 * rows, mine), F32),
        )
    arrived1, sums_so_far, sums2, sums3 = lax.optimization_barrier(
        (arrived1, sums_so_far, sums2, sums3)
    )
    group1 = both_cores(arrived1)
    sums2 = scatter_second(sums2)
    project_got = swap(gate(project_low, arrived1), "y")
    part1 = weight_grad(2, group1, [(0, 32), (96, 0)], [pool_part])
    sums3, sums2, project_got, part1 = lax.optimization_barrier(
        (sums3, sums2, project_got, part1)
    )
    project_sum = project_low.astype(F32) + project_got.astype(F32)
    project_sum = project_sum.astype(BF).reshape(feat // half, half, feat)
    joint = jnp.concatenate([scatter_last(sums3), scatter_last(sums2), project_sum], axis=0)
    joint_x = swap(joint, "x")
    sums1 = scatter_first(part1)
    with jax.named_scope("input_grad"):
        group1, part1 = lax.optimization_barrier((group1, part1))
        shape = jax.ShapeDtypeStruct((cols, rows, mine), BF)
        own, to_x, to_y, to_d = input_part(
            [(2, 0, 0, 32), (None, 0, 96, 0)],
            [group1],
            True,
            [sums_so_far, spread_back[:1], strip_back],
            [shape] * 4,
        )
        sums1, joint_x = gate((sums1, joint_x), own)
        got = [own, swap(to_x, "x"), swap(to_y, "y"), crossed(to_d)]
        sums1 = scatter_second(sums1)
        joint, joint_x = lax.optimization_barrier((joint, joint_x))
        pieces32 = [joint, swap(joint, "k"), joint_x, swap(joint_x, "k")]
        project_pool = lax.dot_general(
            joined4.astype(F32),
            image_heads,
            (((0,), (0,)), ((), ())),
            precision=lax.Precision.HIGHEST,
        ).reshape(feat // half, half, feat)
        grad, project_grad = collect(pieces32, 0, [], project_pool)
        project_grad = project_grad.reshape(5 * feat, feat)
        got, sums1, grad = lax.optimization_barrier((got, sums1, grad))
        if aligned:
            input_grad = call(
                partial(unpack_kernel, share),
                "unpack",
                4 * 10**9,
                [SMEM] + [VMEM] * 4,
                jax.ShapeDtypeStruct((rows, cols, chans), BF),
                [],
                [places, *got],
            )
        else:
            planes = []
            for y in range(2):
                for x in range(2):
                    index = ((iy ^ y) * 2 + (ix ^ x)).astype(jnp.int32)
                    planes.append(lax.select_n(index, *got).reshape(cols, rows, zs, share))
            input_grad = jnp.stack(planes, axis=3).reshape(cols, rows, chans).transpose(1, 0, 2)

    done = scatter_last(sums1)
    done_x = swap(done, "x")
    done_x, grad, input_grad = lax.optimization_barrier((done_x, grad, input_grad))
    pieces1 = [done, swap(done, "k"), done_x, swap(done_x, "k")]
    grad, point_grad, pool_grad = collect(pieces1, 18, [grad])
    atrous_grad = grad.reshape(3, 3, 3, 4 * half, feat)
    point_grad, pool_grad = (v.reshape(4 * half, feat) for v in (point_grad, pool_grad))

    gain_grad = jnp.concatenate([rear[4:8], gain4[None], head_back[1][None]], axis=0)
    shift_grad = jnp.concatenate([rear[:4], shift4[None], head_back[0][None]], axis=0)
    return (
        output,
        input_grad,
        point_grad,
        atrous_grad,
        pool_grad,
        project_grad,
        gain_grad,
        shift_grad,
    )


def solution(mesh):
    row, col = mesh.devices.shape
    fine = Mesh(mesh.devices.reshape(row // 2, 2, col // 2, 2), ("z", "y", "x", "k"))
    rows, cols = ("z", "y"), ("x", "k")
    placed = (
        P(rows, cols, None),
        P(rows, cols),
        P(),
        P(),
        P(),
        P(),
        P(),
        P(),
        P(rows, cols, None),
    )
    return jax.shard_map(
        per_device,
        mesh=fine,
        in_specs=placed,
        out_specs=(
            P(rows, cols, None),
            P(rows, cols, None),
            P(rows, None),
            P(None, None, None, rows, None),
            P(rows, None),
            P(),
            P(),
            P(),
        ),
        check_vma=False,
    )
```

```python
from functools import partial

import jax
import jax.numpy as jnp
from jax import lax
from jax.experimental import pallas as pl
from jax.experimental.pallas import tpu as pltpu
from jax.sharding import Mesh, PartitionSpec as P

REACH = 18
IMG_ROWS = 32
EPSILON = 1e-05
PAD = 32
RIM = 24
SWAP = [(0, 1), (1, 0)]
BF = jnp.bfloat16
F32 = jnp.float32
VMEM_LIMIT = 60 * 2**20


def dot(a, b):
    return jnp.dot(a, b, preferred_element_type=F32)


def exact(a, b):
    return jnp.dot(a, b, precision=lax.Precision.HIGHEST, preferred_element_type=F32)


def gate(x, *deps):
    return lax.optimization_barrier((x, deps))[0]


def swap(x, axis):
    return lax.ppermute(x, axis, SWAP)


def z_swap(x, step):
    count = lax.axis_size("z")
    return lax.ppermute(x, "z", [(i, i ^ step) for i in range(count)])


def crossed(x):
    return lax.ppermute(x, ("y", "x"), [(i, 3 - i) for i in range(4)])


def quad(x, axes):
    near, far, last = (
        lax.ppermute(x, axes, [(i, i ^ step) for i in range(4)]) for step in (1, 2, 3)
    )
    return (x + near) + (far + last)


def z_sum(x):
    count = lax.axis_size("z")
    if count == 4:
        return quad(x, "z")
    step = 1
    while step < count:
        x = x + lax.ppermute(x, "z", [(i, i ^ step) for i in range(count)])
        step *= 2
    return x


def plane_sum(x):
    return quad(x, ("y", "x"))


def allsum(x):
    x = plane_sum(z_sum(x))
    return x + swap(x, "k")


def smooth(value):
    return jax.nn.gelu(value, approximate=True)


def smooth_slope(value):
    root = 0.7978845608028654
    square = value * value
    tanh = jnp.tanh(root * (value + 0.044715 * value * square))
    return 0.5 * (1.0 + tanh) + 0.5 * value * (1.0 - tanh * tanh) * root * (
        1.0 + 3 * 0.044715 * square
    )


def moments(value):
    return jnp.stack([jnp.sum(value, axis=0), jnp.sum(value * value, axis=0)])


def place_of(info, n):
    dk, dy, dx = n // 4, n // 2 % 2, n % 2
    col = ((info[1] ^ dx) * 2 + (info[2] ^ dk)) * 8
    return REACH + col, info[0] ^ dy


def tile_copies(info, tiles, window, sems, main=0, rim=0):
    copies = []
    for n, tile in enumerate(tiles):
        col, y = place_of(info, n)
        row = pl.multiple_of(PAD + y * 64, 16)
        copies.append(
            pltpu.make_async_copy(
                tile.at[:, pl.ds(main, 64)],
                window.at[pl.ds(col, 8), pl.ds(row, 64)],
                sems.at[n],
            )
        )
        if rim:
            row = pl.multiple_of(jnp.where(y == 0, PAD + 128, PAD - rim), 16)
            copies.append(
                pltpu.make_async_copy(
                    tile.at[:, pl.ds(main + 64, rim)],
                    window.at[pl.ds(col, 8), pl.ds(row, rim)],
                    sems.at[8 + n],
                )
            )
    for copy in copies:
        copy.start()
    return copies


def place_rims(info, rims, window):
    for dk, rim in enumerate(rims):
        for n in range(4):
            col = REACH + ((n % 2) * 2 + (info[2] ^ dk)) * 8
            row = PAD + 128 if n < 2 else PAD - REACH
            for q in range(8):
                window[col + q, row : row + REACH, :] = rim[n, q, :REACH]


def shift_rows(window, masks, b, q, i, spread, sign, cut, ok=None):
    start = PAD + sign * (i - 1) * spread
    value = window[REACH + q, start : start + 128, :]
    if i != 1:
        keep = masks[b, 1 if sign * (i - 1) > 0 else 0]
        keep = jnp.where(q >= cut, keep, jnp.ones_like(keep))
        if ok is not None:
            keep = jnp.where(ok, keep, jnp.zeros_like(keep))
        value = value * jnp.concatenate([keep] * (value.shape[1] // 128), axis=1)
    elif ok is not None:
        value = jnp.where(ok, value, jnp.zeros_like(value))
    return value


def tap_rows(window, masks, b, col, width, spread, sign, cut):
    return jnp.concatenate(
        [
            jnp.concatenate(
                [shift_rows(window, masks, b, col + u, i, spread, sign, cut) for i in range(3)],
                axis=1,
            )
            for u in range(width)
        ],
        axis=0,
    )


def branch_sum(window, masks, b, col, spread, sign, cut, product, acc, fresh):
    width = 2

    def inside(j, e):
        source = col + e + sign * (j - 1) * spread
        return (source >= 0) & (source < 32) & ((source < cut) == (col + e < cut))

    def center(e):
        return product(1, tap_rows(window, masks, b, col + e, width, spread, sign, cut))

    def side(j, e):
        source = col + e + sign * (j - 1) * spread
        part = product(j, tap_rows(window, masks, b, source, width, spread, sign, cut))
        return jnp.concatenate(
            [
                jnp.where(inside(j, e + u), part[u * 128 : u * 128 + 128], 0.0)
                for u in range(width)
            ],
            axis=0,
        )

    def put(e, value, first):
        value = value.reshape(width, 128, acc.shape[-1])
        if first:
            acc[pl.ds(e, width)] = value
        else:
            acc[pl.ds(e, width)] += value

    dense = spread == REACH // 3
    for e in range(0, 8, width):
        value = center(e)
        if dense:
            value = value + side(0, e) + side(2, e)
        put(e, value, fresh)
    if dense:
        return

    def block(t, carry):
        j, half = (t // 2) * 2, (t % 2) * 4
        some = inside(j, half)
        for e in range(1, 4):
            some = some | inside(j, half + e)

        @pl.when(some)
        def _():
            for e in range(0, 4, width):
                put(half + e, side(j, half + e), False)

        return carry

    lax.fori_loop(0, 4, block, 0)


def forward_kernel(units, spreads, lanes, info, *refs):
    mains, rims = refs[:8], refs[8:10]
    masks, point, weights = refs[10:13]
    outs = refs[13:17]
    window, point_buf, weight_buf, acc, sems, weight_sems = refs[17:]
    iy, ix, ik, cut = info[0], info[1], info[2], info[3]
    copies = tile_copies(info, mains, window, sems)
    loads = []
    for n, b in enumerate(units):
        if b is None:
            loads.append(
                [pltpu.make_async_copy(point.at[:, iy, ix], point_buf, weight_sems.at[n, 0])]
            )
        else:
            loads.append(
                [
                    pltpu.make_async_copy(
                        weights.at[b, i, j, :, iy, ix],
                        weight_buf.at[n, j, i],
                        weight_sems.at[n, 3 * j + i],
                    )
                    for j in range(3)
                    for i in range(3)
                ]
            )
        for copy in loads[n]:
            copy.start()
    place_rims(info, rims, window)
    for copy in copies:
        copy.wait()
    for n, b in enumerate(units):
        for copy in loads[n]:
            copy.wait()
        keep, send = outs[2 * n : 2 * n + 2]
        for dx in (1, 0):
            col = (ix ^ dx) * 16 + ik * 8
            if b is None:
                source = window[pl.ds(REACH + col, 8), PAD : PAD + 128, :].reshape(1024, lanes)
                acc[...] = dot(source, point_buf[...].reshape(lanes, 256)).reshape(8, 128, 256)
            else:

                def product(j, rows, n=n):
                    return dot(rows, weight_buf[n, j].reshape(3 * lanes, 256))

                branch_sum(window, masks, b, col, spreads[b], 1, cut, product, acc, True)
            for dy in range(2):
                row = pl.multiple_of((iy ^ dy) * 64, 64)
                value = acc[:, pl.ds(row, 64), :]
                if (dy if n else dx) == 0:
                    keep[dx if n else dy] = value
                else:
                    send[dx if n else dy] = value.astype(BF)


def input_kernel(chosen, spreads, lanes, pointed, info, *refs):
    count = 8 * (1 + max(c[1] for c in chosen))
    tiles, masks, point, weights = refs[:count], refs[count], refs[count + 1], refs[count + 2]
    rest = refs[count + 3 :]
    if pointed:
        before, edge, strip = rest[:3]
        outs = rest[3:7]
        windows, weight_buf, point_buf, acc, sems, weight_sems = rest[7:]
    else:
        (result,) = rest[:1]
        windows, weight_buf, sems, weight_sems = rest[1:]
        acc = result
    iy, ix, ik, cut = info[0], info[1], info[2], info[3]
    mine = acc.shape[-1]
    fetches, loads = [], []
    for n, (b, first, main, rim) in enumerate(chosen):
        group = tiles[8 * first : 8 * first + 8]
        fetches.append(tile_copies(info, group, windows.at[n], sems.at[n], main, rim))
        if b is None:
            loads.append(
                [pltpu.make_async_copy(point.at[:, iy, ix], point_buf, weight_sems.at[n, 0])]
            )
        else:
            loads.append(
                [
                    pltpu.make_async_copy(
                        weights.at[b, i, j, :, iy, ix],
                        weight_buf.at[n, j, :, :, pl.ds(i * lanes, lanes)],
                        weight_sems.at[n, 3 * j + i],
                    )
                    for j in range(3)
                    for i in range(3)
                ]
            )
        for copy in loads[n]:
            copy.start()

    def times(a, w):
        return lax.dot_general(
            a, w.reshape(mine, w.shape[-1]), (((1,), (1,)), ((), ())), preferred_element_type=F32
        )

    for n, (b, _, _, _) in enumerate(chosen):
        for copy in fetches[n] + loads[n]:
            copy.wait()
        window = windows.at[n]
        for dx in range(2):
            col = (ix ^ dx) * 16 + ik * 8
            if b is None:
                for e in range(0, 8, 2):
                    source = window[pl.ds(REACH + col + e, 2), PAD : PAD + 128, :]
                    value = times(source.reshape(256, lanes), point_buf[...])
                    for u in range(2):
                        pool = jnp.where(col + e + u < cut, edge[...], strip[...])
                        acc[dx, e + u] += (
                            before[dx, e + u] + value[u * 128 : u * 128 + 128] + pool
                        )
            else:

                def product(j, rows, n=n):
                    return times(rows, weight_buf[n, j])

                branch_sum(
                    window, masks, b, col, spreads[b], -1, cut, product, acc.at[dx], n == 0
                )
    if pointed:
        for dx in range(2):
            for dy in range(2):
                row = pl.multiple_of((iy ^ dy) * 64, 64)
                outs[dy * 2 + dx][...] = acc[dx, :, pl.ds(row, 64), :].astype(BF)


def weight_kernel(spread, b, sources, lanes, info, *refs):
    tiles = refs[:8]
    masks, across = refs[8:10]
    pooled = len(sources) > 1
    outs = refs[10 + pooled : -4]
    windows, out, sems, out_sems = refs[-4:]
    cut = info[3]
    parts = out.shape[0]
    each = out.shape[2]
    paired = len(outs) == 2
    fetches = [
        tile_copies(info, tiles, windows.at[n], sems.at[n], main, rim)
        for n, (main, rim) in enumerate(sources)
    ]

    def emit(t, value):
        for z in range(parts):
            out[info[4] ^ z if paired else z, t] = value[z * each : (z + 1) * each].astype(BF)

    for copy in fetches[0]:
        copy.wait()
    window = windows.at[0]
    for j in (1, 0, 2):
        move = (j - 1) * spread
        columns = [p for p in range(32) if 0 <= p + move < 32]
        total = None
        for at in range(0, len(columns), 8):
            group = columns[at : at + 8]
            right = []
            for p in group:
                ok = None if j == 1 else ((p < cut) == (p + move < cut))
                right.append(
                    jnp.concatenate(
                        [shift_rows(window, masks, b, p, i, spread, -1, cut, ok) for i in range(3)],
                        axis=1,
                    )
                )
            first, last = (group[0] + move) * 128, (group[-1] + move + 1) * 128
            part = dot(across[:, first:last], jnp.concatenate(right, axis=0))
            total = part if total is None else total + part
        for i in range(3):
            emit(3 * i + j, total[:, i * lanes : (i + 1) * lanes])
    if len(sources) > 1:
        for copy in fetches[1]:
            copy.wait()
        plain = windows[1, REACH : REACH + 32, PAD : PAD + 128, :].reshape(32 * 128, lanes)
        emit(9, dot(across[...], plain))
        emit(10, refs[10][...])
    if paired:
        moves = [(0, outs[0].at[0]), (3, outs[0].at[1]), (1, outs[1].at[0]), (2, outs[1].at[1])]
        moves = [(out.at[m], target) for m, target in moves]
    else:
        moves = [(out, outs[0])]
    copies = [
        pltpu.make_async_copy(source, target, out_sems.at[n])
        for n, (source, target) in enumerate(moves)
    ]
    for copy in copies:
        copy.start()
    for copy in copies:
        copy.wait()


def collect_kernel(first, count, extras, info, *refs):
    pieces = refs[:4]
    outs = refs[len(refs) - 3 - len(extras) : len(refs) - 2]
    buf, sem = refs[len(refs) - 2 :]
    ix, ik = info[1], info[2]
    if len(extras) == 1:
        outs[1][4] = refs[4][...]
    for n, piece in enumerate(pieces):
        index = (ix ^ (n // 2)) * 2 + (ik ^ (n % 2))
        for t in range(count):
            buf[t, index] = piece[t].astype(F32)
        at = count
        for e, length in enumerate(extras):
            for t in range(length):
                outs[1 + e][index, t] = piece[at + t].astype(F32)
            at += length
    copy = pltpu.make_async_copy(buf, outs[0].at[pl.ds(first, count)], sem)
    copy.start()
    copy.wait()


def pack_kernel(share, info, full, marks, *refs):
    iy, ix = info[0], info[1]
    rims = refs[4]
    for n in range(4):
        other = (iy ^ (n // 2)) * 2 + (ix ^ (n % 2))
        for z in range(full.shape[-1] // (4 * share)):
            lane = pl.multiple_of((z * 4 + other) * share, 128)
            value = jnp.swapaxes(full[:, :, pl.ds(lane, share)], 0, 1)
            refs[n][:, :, z * share : (z + 1) * share] = value

            @pl.when(iy == 0)
            def _(value=value, other=other, z=z):
                rims[other, :, :RIM, z * share : (z + 1) * share] = value[:, :RIM]

            @pl.when(iy == 1)
            def _(value=value, other=other, z=z):
                rims[other, :, :REACH, z * share : (z + 1) * share] = value[:, 64 - REACH :]

    for n in range(4):
        for q in range(8):
            rims[n, q, REACH : REACH + 1, :] = marks[...]


def unpack_kernel(share, info, *refs):
    iy, ix = info[0], info[1]
    full = refs[4]
    for n in range(4):
        other = (iy ^ (n // 2)) * 2 + (ix ^ (n % 2))
        for z in range(full.shape[-1] // (4 * share)):
            lane = pl.multiple_of((z * 4 + other) * share, 128)
            value = refs[n][:, :, z * share : (z + 1) * share]
            full[:, :, pl.ds(lane, share)] = jnp.swapaxes(value, 0, 1)


def across_kernel(share, info, *refs):
    tiles, out, rows, zero = refs[:8], *refs[8:11]
    window, acc, sems = refs[11:]
    ik, cut = info[2], info[3]
    for copy in tile_copies(info, tiles, window, sems):
        copy.wait()
    acc[...] = jnp.zeros_like(acc)
    for q in range(32):
        value = window[REACH + q, PAD : PAD + 128, :]
        turned = value.T
        for z in range(turned.shape[0] // share):
            low = turned[z * share : z * share + share // 2]
            high = turned[z * share + share // 2 : (z + 1) * share]
            out[z * share // 2 : (z + 1) * share // 2, q * 128 : (q + 1) * 128] = jnp.where(
                ik == 0, low, high
            )
        acc[(q >= cut).astype(jnp.int32)] += value.astype(F32)
    rows[...] = acc[1]
    zero[...] = jnp.sum(acc[0], axis=0, keepdims=True)


VMEM = pl.BlockSpec(memory_space=pltpu.VMEM)
SMEM = pl.BlockSpec(memory_space=pltpu.SMEM)
ANY = pl.BlockSpec(memory_space=pl.ANY)


def call(kernel, name, flops, in_specs, out_shape, scratch, args, out_specs=None, aliases=None):
    return pl.pallas_call(
        kernel,
        name=name,
        in_specs=in_specs,
        out_specs=out_specs or jax.tree.map(lambda _: VMEM, out_shape),
        out_shape=out_shape,
        input_output_aliases=aliases or {},
        scratch_shapes=scratch,
        compiler_params=pltpu.CompilerParams(vmem_limit_bytes=VMEM_LIMIT),
        cost_estimate=pl.CostEstimate(flops=flops, bytes_accessed=10**7, transcendentals=0),
    )(*args)


def per_device(
    feature_map,
    image_ids,
    point_weight,
    atrous_weight,
    pool_weight,
    project_weight,
    bn_gain,
    bn_shift,
    out_grad,
):
    rows, cols, chans = feature_map.shape
    feat = point_weight.shape[1]
    pixels = rows * cols
    zs = lax.axis_size("z")
    axes = ("k", "x", "y", "z")
    iz, iy, ix, ik = (lax.axis_index(a) for a in ("z", "y", "x", "k"))
    row_count = 2 * zs
    total = float(pixels * row_count * 4)
    images = rows * row_count // IMG_ROWS + 1
    share = chans // (4 * zs)
    mine = chans // 4
    spreads = [REACH * (b + 1) // 3 for b in range(3)]
    def pick(first, second, index):
        return jnp.where(index == 0, first, second)

    def rim(x, depth):
        return pick(x[:, :depth], x[:, rows - depth :], iy)

    def beyond(x, dy, dx):
        pairs = []
        for z in range(zs):
            for y in range(2):
                far = z - 1 + 2 * y
                if 0 <= far < zs:
                    for i in range(2):
                        target = (far * 2 + (y ^ dy)) * 2 + (i ^ dx)
                        pairs.append(((z * 2 + y) * 2 + i, target))
        return lax.ppermute(x, ("z", "y", "x"), pairs)

    with jax.named_scope("marks"):
        strip_own = jnp.max(image_ids, axis=1)
        edge_own = pick(strip_own[:REACH], strip_own[rows - REACH :], iy)
        zero_own = jnp.sum((image_ids[0] == 0).astype(jnp.int32))
        marks = jnp.concatenate([strip_own, edge_own, zero_own[None]])
        marks = jnp.pad(marks, (0, mine - marks.shape[0])).astype(BF)[None]

    places = jnp.stack([iy, ix, ik, ik, iz]).astype(jnp.int32)
    aligned = share % 128 == 0
    with jax.named_scope("spread_features"):
        if aligned:
            tile_shape = jax.ShapeDtypeStruct((cols, rows, mine), BF)
            *tiles, brims = call(
                partial(pack_kernel, share),
                "pack",
                0,
                [SMEM, VMEM, VMEM],
                [tile_shape] * 4 + [jax.ShapeDtypeStruct((4, cols, RIM, mine), BF)],
                [],
                [places, feature_map, marks],
            )
        else:
            packed = feature_map.transpose(1, 0, 2).reshape(cols, rows, zs, 2, 2, share)
            packed = packed.transpose(3, 4, 0, 1, 2, 5)
            packed = packed.reshape(4, cols, rows, mine)
            tiles = [
                lax.dynamic_index_in_dim(packed, (iy ^ dy) * 2 + (ix ^ dx), 0, False)
                for dy in range(2)
                for dx in range(2)
            ]
            brims = pick(packed[:, :, :REACH], packed[:, :, rows - REACH :], iy)
            brims = jnp.pad(brims, ((0, 0), (0, 0), (0, RIM - REACH), (0, 0)))
            brims = brims.at[:, :, REACH].set(marks)
        note = jnp.broadcast_to(marks[None, None], (4, cols, 1, mine))
        own, to_x, to_y, to_d = tiles
        mains = [own, swap(to_x, "x"), swap(to_y, "y"), crossed(to_d)]
        halo, mains = lax.optimization_barrier((beyond(brims, 0, 0), mains))
        halo = lax.dynamic_update_slice_in_dim(halo, note, REACH + 1, axis=2)
        halo = lax.all_to_all(halo, ("y", "x"), 0, 0)
        halos = [halo, swap(halo, "k")]

    mains = mains + [swap(g, "k") for g in mains]
    with jax.named_scope("marks"):
        told = jnp.stack([h[:, 0, REACH : REACH + 2] for h in halos]).astype(jnp.int32)
        told = told.reshape(2, 2, 2, 2, mine)
        strips = jnp.max(told[:, :, :, 1, :rows], axis=(0, 2))
        edges = jnp.max(told[:, :, :, 0, rows : rows + REACH], axis=(0, 2))
        cut = jnp.sum(told[:, 0, :, 1, rows + REACH])
        strip_plane = strips.reshape(2 * rows)
        top, bottom = edges[1], edges[0]
        strip_tall = jnp.concatenate([top, strip_plane, bottom])
        masks = jnp.stack(
            [
                jnp.stack(
                    [
                        strip_plane
                        == lax.slice_in_dim(strip_tall, REACH + s * d, REACH + s * d + 2 * rows)
                        for s in (-1, 1)
                    ]
                )
                for d in spreads
            ]
        )
        masks = jnp.broadcast_to(masks[..., None], (3, 2, 2 * rows, 128)).astype(BF)
        info = jnp.stack([iy, ix, ik, cut, iz]).astype(jnp.int32)


    local_ids = image_ids.T.reshape(pixels)
    image_range = jnp.arange(images, dtype=jnp.int32)
    table = local_ids[:, None] == image_range[None, :]

    point_view = point_weight.reshape(zs, 2, 2, share, feat)
    atrous_view = atrous_weight.reshape(3, 3, 3, zs, 2, 2, share, feat)

    def forward(units):
        shape = (2, cols, rows, feat)
        return call(
            partial(forward_kernel, units, spreads, mine),
            "forward_taps",
            2 * 2048 * mine * 256 * 15,
            [SMEM] + [ANY] * 8 + [VMEM] * 3 + [ANY] * 2,
            [jax.ShapeDtypeStruct(shape, F32), jax.ShapeDtypeStruct(shape, BF)] * 2,
            [
                pltpu.VMEM((32 + 2 * REACH, 2 * PAD + 128, mine), BF),
                pltpu.VMEM((zs, share, feat), BF),
                pltpu.VMEM((2, 3, 3, zs, share, feat), BF),
                pltpu.VMEM((8, 128, feat), F32),
                pltpu.SemaphoreType.DMA((16,)),
                pltpu.SemaphoreType.DMA((2, 9)),
            ],
            [info, *mains, *halos, masks, point_view, atrous_view],
        )

    def reduce_first(parts):
        keep_x, send_x, keep_y, send_y = parts
        return keep_x, swap(send_x, "x"), keep_y, swap(send_y, "y")

    def reduce_middle(parts):
        keep_x, got_x, keep_y, got_y = parts
        more_x = (keep_x[1] + got_x[1].astype(F32)).astype(BF)
        more_y = (keep_y[1] + got_y[1].astype(F32)).astype(BF)
        return more_x, more_y

    def reduce_last(parts, last_x, last_y):
        keep_x, got_x, keep_y, got_y = parts
        value_x = keep_x[0] + got_x[0].astype(F32) + last_x.astype(F32)
        value_y = keep_y[0] + got_y[0].astype(F32) + last_y.astype(F32)
        return [value_x.reshape(pixels, feat), value_y.reshape(pixels, feat)]

    early = forward([None, 0])
    early_got = reduce_first(early)
    late = forward([1, 2])
    early_got, late = lax.optimization_barrier((early_got, late))
    late_got = reduce_first(late)
    early_more = reduce_middle(early_got)
    early_last = [swap(early_more[0], "y"), swap(early_more[1], "x")]

    half = share // 2
    strip_table = strip_plane[:, None] == image_range[None, :]
    with jax.named_scope("across"):
        mains_late, early_last = lax.optimization_barrier((mains, early_last))
        if aligned:
            across, row_sums, zero_sums = call(
                partial(across_kernel, share),
                "across",
                2 * 10**9,
                [SMEM] + [ANY] * 8,
                [
                    jax.ShapeDtypeStruct((mine // 2, 32 * 2 * rows), BF),
                    jax.ShapeDtypeStruct((2 * rows, mine), F32),
                    jax.ShapeDtypeStruct((1, mine), F32),
                ],
                [
                    pltpu.VMEM((32 + 2 * REACH, 2 * PAD + 128, mine), BF),
                    pltpu.VMEM((2, 2 * rows, mine), F32),
                    pltpu.SemaphoreType.DMA((16,)),
                ],
                [info, *mains_late],
            )
        else:
            columns = []
            for x in range(2):
                for k in range(2):
                    index = [(ik ^ k) * 4 + (iy ^ y) * 2 + (ix ^ x) for y in range(2)]
                    stack = [lax.select_n(n.astype(jnp.int32), *mains_late) for n in index]
                    columns.append(jnp.concatenate(stack, axis=1))
            plane = jnp.concatenate(columns, axis=0)
            in_strip = (jnp.arange(32) >= cut)[:, None, None]
            row_sums = jnp.sum(jnp.where(in_strip, plane.astype(F32), 0.0), axis=0)
            zero_sums = jnp.sum(jnp.where(in_strip, 0.0, plane.astype(F32)), axis=(0, 1))[None]
            plane = plane.reshape(32, 2 * rows, zs, 2, half)
            plane = lax.dynamic_index_in_dim(plane, ik, 3, False)
            across = plane.reshape(32 * 2 * rows, mine // 2).T

    with jax.named_scope("image_sums"):
        sums = lax.dot_general(
            strip_table.astype(F32),
            row_sums,
            (((0,), (0,)), ((), ())),
            precision=lax.Precision.HIGHEST,
        )
        sums = jnp.where(image_range[:, None] == 0, zero_sums, sums)
        pool_mine = pool_weight.reshape(zs, 2, 2, share, feat)
        pool_mine = lax.dynamic_slice(
            pool_mine, (0, iy, ix, 0, 0), (zs, 1, 1, share, feat)
        ).reshape(mine, feat)
        per_image_part = 0.5 * exact(sums, pool_mine.astype(F32))
        strip_rows = jnp.sum(strip_table.astype(F32), axis=0)
        strip_rows = jnp.where((iy == 0) & (ix == 0) & (ik == 0), strip_rows, 0.0)
        strip_rows = jnp.pad(strip_rows, (0, -images % feat)).reshape(-1, feat)

    late_got, across, sums = lax.optimization_barrier((late_got, across, sums))
    late_more = reduce_middle(late_got)
    branches = reduce_last(early_got, *early_last)
    branches += reduce_last(late_got, swap(late_more[0], "y"), swap(late_more[1], "x"))

    first = jnp.concatenate([moments(value) for value in branches], axis=0)
    first = allsum(jnp.concatenate([first, per_image_part, strip_rows], axis=0))
    strip_rows = first[8 + images :].reshape(-1)[:images]
    counts = jnp.where(
        image_range == 0,
        (cut * (rows * row_count)).astype(F32),
        strip_rows * (4 * cols - cut).astype(F32),
    )
    per_image = first[8 : 8 + images] / counts[:, None]
    first = first[:8].reshape(4, 2, feat).transpose(1, 0, 2).reshape(2, 4 * feat)
    weighted = counts[:, None] * per_image
    pool_stats = jnp.stack([jnp.sum(weighted, axis=0), jnp.sum(weighted * per_image, axis=0)])
    four = 4 * feat
    flat_gain, flat_shift = bn_gain[:4].reshape(four), bn_shift[:4].reshape(four)
    mean = first[0] / total
    scale = lax.rsqrt(first[1] / total - mean * mean + EPSILON)
    normed = (jnp.concatenate(branches, axis=1) - mean) * scale
    lifted = normed * flat_gain + flat_shift
    mean4 = pool_stats[0] / total
    scale4 = lax.rsqrt(pool_stats[1] / total - mean4 * mean4 + EPSILON)
    normed4 = (per_image - mean4) * scale4
    lifted4 = normed4 * bn_gain[4] + bn_shift[4]
    joined = smooth(lifted).astype(BF)
    joined4 = smooth(lifted4).astype(BF)
    table_float = table.astype(F32)
    head = dot(joined, project_weight[:four]) + exact(
        table_float, dot(joined4, project_weight[four:])
    )
    head_stats = allsum(moments(head))
    head_mean = head_stats[0] / total
    head_scale = lax.rsqrt(head_stats[1] / total - head_mean * head_mean + EPSILON)
    head_norm = (head - head_mean) * head_scale
    head_lift = head_norm * bn_gain[5] + bn_shift[5]
    output = smooth(head_lift).astype(BF).reshape(cols, rows, feat)
    cotangent = out_grad.transpose(1, 0, 2).reshape(pixels, feat).astype(F32)
    head_grad = cotangent * smooth_slope(head_lift)
    head_back = allsum(
        jnp.stack([jnp.sum(head_grad, axis=0), jnp.sum(head_grad * head_norm, axis=0)])
    )
    head_slope = (
        bn_gain[5]
        * head_scale
        * (head_grad - head_back[0] / total - head_norm * head_back[1] / total)
    ).astype(BF)
    joined_grad = lax.dot_general(
        head_slope, project_weight[:four], (((1,), (1,)), ((), ())), preferred_element_type=F32
    )
    grads = joined_grad * smooth_slope(lifted)
    image_heads = jnp.einsum(
        "pi,pf->if", table.astype(BF), head_slope, preferred_element_type=F32
    )
    rear = jnp.concatenate(
        [
            jnp.stack([jnp.sum(grads, axis=0), jnp.sum(grads * normed, axis=0)]).reshape(8, feat),
            image_heads,
        ],
        axis=0,
    )
    rear = allsum(rear)
    shift_back, gain_back = rear[:4].reshape(four), rear[4:8].reshape(four)
    slopes = (
        flat_gain * scale * (grads - shift_back / total - normed * gain_back / total)
    ).astype(BF)

    with jax.named_scope("project_grad"):
        project_inputs = joined, head_slope

    with jax.named_scope("spread_slopes"):
        point_tile, *tiles_out = [
            slopes[:, k * feat : (k + 1) * feat].reshape(cols, rows, feat) for k in range(4)
        ]
        brim = beyond(rim(tiles_out[0], 16), 0, 0)
        deep = rim(tiles_out[2], 32)
        brims = jnp.concatenate([rim(tiles_out[1], 16), deep[:, :16], deep[:, 16:]], axis=2)
        brims = beyond(brims, 0, 0)

        def both_cores(got):
            return got + [swap(g, "k") for g in got]

        tile3 = jnp.concatenate([tiles_out[0], brim], axis=1)
        got3 = [tile3, swap(tile3, "x"), swap(tile3, "y"), crossed(tile3)]
        left, right = gate(project_inputs, tile3)
        project_part = lax.dot_general(
            left, right, (((0,), (0,)), ((), ())), preferred_element_type=F32
        )
        blocks = project_part.astype(BF).reshape(4, feat, feat)
        blocks = lax.all_to_all(blocks, ("x", "k"), 0, 0)
        across, blocks = lax.optimization_barrier((across, blocks))
        project_sum = jnp.sum(blocks.astype(F32), axis=0)
        project_low = project_sum.astype(BF)
        project_got = z_swap(project_low, 1)
        got3, brims = lax.optimization_barrier((got3, brims))
        edges = [brims[:, :, i * feat : (i + 1) * feat] for i in range(3)]
        tile2 = jnp.concatenate([tiles_out[1], edges[0]], axis=1)
        tile1 = jnp.concatenate([tiles_out[2], edges[1], edges[2], point_tile], axis=1)
        group3 = both_cores(got3)
        tile2, group3, output = lax.optimization_barrier((tile2, group3, output))
        output = output.transpose(1, 0, 2)
        arrived2 = [tile2, swap(tile2, "x"), swap(tile2, "y"), crossed(tile2)]

    rear, sums = gate((rear, sums), tile3)
    image_heads = rear[8:]
    grads4 = smooth_slope(lifted4) * exact(image_heads, project_weight[four:].astype(F32).T)
    shift4, gain4 = jnp.sum(grads4, axis=0), jnp.sum(grads4 * normed4, axis=0)
    image_slope = (
        bn_gain[4]
        * scale4
        * (grads4 - counts[:, None] * (shift4 / total + normed4 * gain4 / total))
    )
    image_low = image_slope.astype(BF)
    spread_back = (
        lax.dot_general(
            image_low, pool_mine, (((1,), (1,)), ((), ())), preferred_element_type=F32
        )
        / counts[:, None]
    )
    strip_back = exact(strip_table.astype(F32), spread_back)
    sums_mine = lax.dynamic_index_in_dim(sums.reshape(images, zs, 2, half), ik, 2, False)
    pool_part = lax.dot_general(
        sums_mine.reshape(images, mine // 2),
        image_low.astype(F32) / counts[:, None],
        (((0,), (0,)), ((), ())),
        precision=lax.Precision.HIGHEST,
    )

    def weight_grad(b, tiles, lanes_at, more=()):
        taps = 8 + len(lanes_at) + len(more)
        return call(
            partial(weight_kernel, spreads[b], b, lanes_at, feat),
            "weight_taps",
            2 * 4096 * (mine // 2) * 256 * 15,
            [SMEM] + [ANY] * 8 + [VMEM] * (2 + len(more)),
            [jax.ShapeDtypeStruct((2, taps, half, feat), BF)] * 2
            if zs == 4
            else [jax.ShapeDtypeStruct((zs, taps, half, feat), BF)],
            [
                pltpu.VMEM((len(lanes_at), 32 + 2 * REACH, 2 * PAD + 128, feat), BF),
                pltpu.VMEM((zs, taps, half, feat), BF),
                pltpu.SemaphoreType.DMA((2, 16)),
                pltpu.SemaphoreType.DMA((4,)),
            ],
            [info, *tiles, masks, across, *more],
            out_specs=[ANY] * (2 if zs == 4 else 1),
        )

    def collect(pieces, first, buffer, pool=None):
        count = 9 if buffer else 18
        extras = [1, 1] if buffer else [pieces[0].shape[0] - count]
        grad = jax.ShapeDtypeStruct((27, 4, half, feat), F32)
        sides = [jax.ShapeDtypeStruct((4, n, half, feat), F32) for n in extras]
        if pool is not None:
            sides = [jax.ShapeDtypeStruct((5, *pool.shape), F32)]
        given = buffer if pool is None else [pool]
        return call(
            partial(collect_kernel, first, count, extras),
            "collect",
            6 * 10**9,
            [SMEM] + [VMEM] * 4 + [VMEM if pool is not None else ANY],
            [grad, *sides],
            [pltpu.VMEM((count, 4, half, feat), F32), pltpu.SemaphoreType.DMA],
            [places, *pieces, *given],
            out_specs=[ANY] + [VMEM] * len(extras),
            aliases={5: 0} if buffer else {},
        )

    def scatter_first(part):
        if zs != 4:
            return lax.psum_scatter(part[0], "z", scatter_dimension=0, tiled=True), None
        return part[0], z_swap(part[1], 1)

    def scatter_second(state):
        keep, got = state
        if zs != 4:
            return keep, None
        more = (keep[1].astype(F32) + got[1].astype(F32)).astype(BF)
        return keep[0].astype(F32) + got[0].astype(F32), z_swap(more, 3)

    def scatter_last(state):
        keep, got = state
        if zs != 4:
            return keep[0]
        return (keep + got.astype(F32)).astype(BF)

    across, pool_part, spread_back, strip_back = lax.optimization_barrier(
        (across, pool_part, spread_back, strip_back)
    )
    part3 = weight_grad(0, group3, [(0, 16)])
    arrived2, part3, project_got = lax.optimization_barrier((arrived2, part3, project_got))
    project_sum = project_low.astype(F32) + project_got.astype(F32)
    step = 2
    while step < zs // 2:
        project_sum = project_sum + z_swap(project_sum, step)
        step *= 2
    project_low = project_sum.astype(BF)
    project_got = z_swap(project_low, step)
    group2 = both_cores(arrived2)
    tile1, group2 = lax.optimization_barrier((tile1, group2))
    arrived1 = [tile1, swap(tile1, "x"), swap(tile1, "y"), crossed(tile1)]
    sums3 = scatter_first(part3)
    part2 = weight_grad(1, group2, [(0, 16)])
    part2, group2, project_got, sums3 = lax.optimization_barrier(
        (part2, group2, project_got, sums3)
    )
    sums2, sums3 = scatter_first(part2), scatter_second(sums3)
    project_low = (project_low.astype(F32) + project_got.astype(F32)).astype(BF)
    project_low = gate(project_low, part2)

    def input_part(chosen, groups, pointed, more, outs):
        n = len(chosen)
        scratch = [
            pltpu.VMEM((n, 32 + 2 * REACH, 2 * PAD + 128, feat), BF),
            pltpu.VMEM((n, 3, zs, share, 3 * feat), BF),
        ]
        if pointed:
            scratch += [pltpu.VMEM((zs, share, feat), BF), pltpu.VMEM((2, 8, 128, mine), F32)]
        scratch += [pltpu.SemaphoreType.DMA((n, 16)), pltpu.SemaphoreType.DMA((n, 9))]
        return call(
            partial(input_kernel, chosen, spreads, feat, pointed),
            "input_taps",
            2 * 2048 * mine * 256 * 20,
            [SMEM] + [ANY] * 8 * len(groups) + [VMEM] + [ANY] * 2 + [VMEM] * len(more),
            outs,
            scratch,
            [info, *[t for g in groups for t in g], masks, point_view, atrous_view, *more],
        )

    with jax.named_scope("input_grad"):
        sums_so_far = input_part(
            [(0, 0, 0, 16), (1, 1, 0, 16)],
            [group3, group2],
            False,
            [],
            jax.ShapeDtypeStruct((2, cols, 2 * rows, mine), F32),
        )
    arrived1, sums_so_far, sums2, sums3 = lax.optimization_barrier(
        (arrived1, sums_so_far, sums2, sums3)
    )
    group1 = both_cores(arrived1)
    sums2 = scatter_second(sums2)
    project_got = swap(gate(project_low, arrived1), "y")
    part1 = weight_grad(2, group1, [(0, 32), (96, 0)], [pool_part])
    sums3, sums2, project_got, part1 = lax.optimization_barrier(
        (sums3, sums2, project_got, part1)
    )
    project_sum = project_low.astype(F32) + project_got.astype(F32)
    project_sum = project_sum.astype(BF).reshape(feat // half, half, feat)
    joint = jnp.concatenate([scatter_last(sums3), scatter_last(sums2), project_sum], axis=0)
    joint_x = swap(joint, "x")
    sums1 = scatter_first(part1)
    with jax.named_scope("input_grad"):
        group1, part1 = lax.optimization_barrier((group1, part1))
        shape = jax.ShapeDtypeStruct((cols, rows, mine), BF)
        own, to_x, to_y, to_d = input_part(
            [(2, 0, 0, 32), (None, 0, 96, 0)],
            [group1],
            True,
            [sums_so_far, spread_back[:1], strip_back],
            [shape] * 4,
        )
        sums1, joint_x = gate((sums1, joint_x), own)
        got = [own, swap(to_x, "x"), swap(to_y, "y"), crossed(to_d)]
        sums1 = scatter_second(sums1)
        got, sums1 = lax.optimization_barrier((got, sums1))
        joint, joint_x = gate((joint, joint_x), got)
        pieces32 = [joint, swap(joint, "k"), joint_x, swap(joint_x, "k")]
        project_pool = lax.dot_general(
            joined4.astype(F32),
            image_heads,
            (((0,), (0,)), ((), ())),
            precision=lax.Precision.HIGHEST,
        ).reshape(feat // half, half, feat)
        grad, project_grad = collect(pieces32, 0, [], project_pool)
        project_grad = project_grad.reshape(5 * feat, feat)
        if aligned:
            input_grad = call(
                partial(unpack_kernel, share),
                "unpack",
                4 * 10**9,
                [SMEM] + [VMEM] * 4,
                jax.ShapeDtypeStruct((rows, cols, chans), BF),
                [],
                [places, *got],
            )
        else:
            planes = []
            for y in range(2):
                for x in range(2):
                    index = ((iy ^ y) * 2 + (ix ^ x)).astype(jnp.int32)
                    planes.append(lax.select_n(index, *got).reshape(cols, rows, zs, share))
            input_grad = jnp.stack(planes, axis=3).reshape(cols, rows, chans).transpose(1, 0, 2)

    done = scatter_last(sums1)
    done_x = swap(done, "x")
    done_x, grad, input_grad = lax.optimization_barrier((done_x, grad, input_grad))
    pieces1 = [done, swap(done, "k"), done_x, swap(done_x, "k")]
    grad, point_grad, pool_grad = collect(pieces1, 18, [grad])
    atrous_grad = grad.reshape(3, 3, 3, 4 * half, feat)
    point_grad, pool_grad = (v.reshape(4 * half, feat) for v in (point_grad, pool_grad))

    gain_grad = jnp.concatenate([rear[4:8], gain4[None], head_back[1][None]], axis=0)
    shift_grad = jnp.concatenate([rear[:4], shift4[None], head_back[0][None]], axis=0)
    return (
        output,
        input_grad,
        point_grad,
        atrous_grad,
        pool_grad,
        project_grad,
        gain_grad,
        shift_grad,
    )


def solution(mesh):
    row, col = mesh.devices.shape
    fine = Mesh(mesh.devices.reshape(row // 2, 2, col // 2, 2), ("z", "y", "x", "k"))
    rows, cols = ("z", "y"), ("x", "k")
    placed = (
        P(rows, cols, None),
        P(rows, cols),
        P(),
        P(),
        P(),
        P(),
        P(),
        P(),
        P(rows, cols, None),
    )
    return jax.shard_map(
        per_device,
        mesh=fine,
        in_specs=placed,
        out_specs=(
            P(rows, cols, None),
            P(rows, cols, None),
            P(rows, None),
            P(None, None, None, rows, None),
            P(rows, None),
            P(),
            P(),
            P(),
        ),
        check_vma=False,
    )
```

```python
from functools import partial

import jax
import jax.numpy as jnp
from jax import lax
from jax.experimental import pallas as pl
from jax.experimental.pallas import tpu as pltpu
from jax.sharding import Mesh, PartitionSpec as P

REACH = 18
IMG_ROWS = 32
EPSILON = 1e-05
PAD = 32
RIM = 24
SWAP = [(0, 1), (1, 0)]
BF = jnp.bfloat16
F32 = jnp.float32
VMEM_LIMIT = 60 * 2**20


def dot(a, b):
    return jnp.dot(a, b, preferred_element_type=F32)


def exact(a, b):
    return jnp.dot(a, b, precision=lax.Precision.HIGHEST, preferred_element_type=F32)


def gate(x, *deps):
    return lax.optimization_barrier((x, deps))[0]


def swap(x, axis):
    return lax.ppermute(x, axis, SWAP)


def z_swap(x, step):
    count = lax.axis_size("z")
    return lax.ppermute(x, "z", [(i, i ^ step) for i in range(count)])


def crossed(x):
    return lax.ppermute(x, ("y", "x"), [(i, 3 - i) for i in range(4)])


def quad(x, axes):
    near, far, last = (
        lax.ppermute(x, axes, [(i, i ^ step) for i in range(4)]) for step in (1, 2, 3)
    )
    return (x + near) + (far + last)


def z_sum(x):
    count = lax.axis_size("z")
    if count == 4:
        return quad(x, "z")
    step = 1
    while step < count:
        x = x + lax.ppermute(x, "z", [(i, i ^ step) for i in range(count)])
        step *= 2
    return x


def plane_sum(x):
    return quad(x, ("y", "x"))


def allsum(x):
    x = plane_sum(z_sum(x))
    return x + swap(x, "k")


def smooth(value):
    return jax.nn.gelu(value, approximate=True)


def smooth_slope(value):
    root = 0.7978845608028654
    square = value * value
    tanh = jnp.tanh(root * (value + 0.044715 * value * square))
    return 0.5 * (1.0 + tanh) + 0.5 * value * (1.0 - tanh * tanh) * root * (
        1.0 + 3 * 0.044715 * square
    )


def moments(value):
    return jnp.stack([jnp.sum(value, axis=0), jnp.sum(value * value, axis=0)])


def place_of(info, n):
    dk, dy, dx = n // 4, n // 2 % 2, n % 2
    col = ((info[1] ^ dx) * 2 + (info[2] ^ dk)) * 8
    return REACH + col, info[0] ^ dy


def tile_copies(info, tiles, window, sems, main=0, rim=0):
    copies = []
    for n, tile in enumerate(tiles):
        col, y = place_of(info, n)
        row = pl.multiple_of(PAD + y * 64, 16)
        copies.append(
            pltpu.make_async_copy(
                tile.at[:, pl.ds(main, 64)],
                window.at[pl.ds(col, 8), pl.ds(row, 64)],
                sems.at[n],
            )
        )
        if rim:
            row = pl.multiple_of(jnp.where(y == 0, PAD + 128, PAD - rim), 16)
            copies.append(
                pltpu.make_async_copy(
                    tile.at[:, pl.ds(main + 64, rim)],
                    window.at[pl.ds(col, 8), pl.ds(row, rim)],
                    sems.at[8 + n],
                )
            )
    for copy in copies:
        copy.start()
    return copies


def place_rims(info, rims, window):
    for dk, rim in enumerate(rims):
        for n in range(4):
            col = REACH + ((n % 2) * 2 + (info[2] ^ dk)) * 8
            row = PAD + 128 if n < 2 else PAD - REACH
            for q in range(8):
                window[col + q, row : row + REACH, :] = rim[n, q, :REACH]


def shift_rows(window, masks, b, q, i, spread, sign, cut, ok=None):
    start = PAD + sign * (i - 1) * spread
    value = window[REACH + q, start : start + 128, :]
    if i != 1:
        keep = masks[b, 1 if sign * (i - 1) > 0 else 0]
        keep = jnp.where(q >= cut, keep, jnp.ones_like(keep))
        if ok is not None:
            keep = jnp.where(ok, keep, jnp.zeros_like(keep))
        value = value * jnp.concatenate([keep] * (value.shape[1] // 128), axis=1)
    elif ok is not None:
        value = jnp.where(ok, value, jnp.zeros_like(value))
    return value


def tap_rows(window, masks, b, col, width, spread, sign, cut):
    return jnp.concatenate(
        [
            jnp.concatenate(
                [shift_rows(window, masks, b, col + u, i, spread, sign, cut) for i in range(3)],
                axis=1,
            )
            for u in range(width)
        ],
        axis=0,
    )


def branch_sum(window, masks, b, col, spread, sign, cut, product, acc, fresh):
    width = 2

    def inside(j, e):
        source = col + e + sign * (j - 1) * spread
        return (source >= 0) & (source < 32) & ((source < cut) == (col + e < cut))

    def center(e):
        return product(1, tap_rows(window, masks, b, col + e, width, spread, sign, cut))

    def side(j, e):
        source = col + e + sign * (j - 1) * spread
        part = product(j, tap_rows(window, masks, b, source, width, spread, sign, cut))
        return jnp.concatenate(
            [
                jnp.where(inside(j, e + u), part[u * 128 : u * 128 + 128], 0.0)
                for u in range(width)
            ],
            axis=0,
        )

    def put(e, value, first):
        value = value.reshape(width, 128, acc.shape[-1])
        if first:
            acc[pl.ds(e, width)] = value
        else:
            acc[pl.ds(e, width)] += value

    dense = spread == REACH // 3
    for e in range(0, 8, width):
        value = center(e)
        if dense:
            value = value + side(0, e) + side(2, e)
        put(e, value, fresh)
    if dense:
        return

    def block(t, carry):
        j, half = (t // 2) * 2, (t % 2) * 4
        some = inside(j, half)
        for e in range(1, 4):
            some = some | inside(j, half + e)

        @pl.when(some)
        def _():
            for e in range(0, 4, width):
                put(half + e, side(j, half + e), False)

        return carry

    lax.fori_loop(0, 4, block, 0)


def forward_kernel(units, spreads, lanes, info, *refs):
    mains, rims = refs[:8], refs[8:10]
    masks, point, weights = refs[10:13]
    outs = refs[13:17]
    window, point_buf, weight_buf, acc, sems, weight_sems = refs[17:]
    iy, ix, ik, cut = info[0], info[1], info[2], info[3]
    copies = tile_copies(info, mains, window, sems)
    loads = []
    for n, b in enumerate(units):
        if b is None:
            loads.append(
                [pltpu.make_async_copy(point.at[:, iy, ix], point_buf, weight_sems.at[n, 0])]
            )
        else:
            loads.append(
                [
                    pltpu.make_async_copy(
                        weights.at[b, i, j, :, iy, ix],
                        weight_buf.at[n, j, i],
                        weight_sems.at[n, 3 * j + i],
                    )
                    for j in range(3)
                    for i in range(3)
                ]
            )
        for copy in loads[n]:
            copy.start()
    place_rims(info, rims, window)
    for copy in copies:
        copy.wait()
    for n, b in enumerate(units):
        for copy in loads[n]:
            copy.wait()
        keep, send = outs[2 * n : 2 * n + 2]
        for dx in (1, 0):
            col = (ix ^ dx) * 16 + ik * 8
            if b is None:
                source = window[pl.ds(REACH + col, 8), PAD : PAD + 128, :].reshape(1024, lanes)
                acc[...] = dot(source, point_buf[...].reshape(lanes, 256)).reshape(8, 128, 256)
            else:

                def product(j, rows, n=n):
                    return dot(rows, weight_buf[n, j].reshape(3 * lanes, 256))

                branch_sum(window, masks, b, col, spreads[b], 1, cut, product, acc, True)
            for dy in range(2):
                row = pl.multiple_of((iy ^ dy) * 64, 64)
                value = acc[:, pl.ds(row, 64), :]
                if (dy if n else dx) == 0:
                    keep[dx if n else dy] = value
                else:
                    send[dx if n else dy] = value.astype(BF)


def input_kernel(chosen, spreads, lanes, pointed, info, *refs):
    count = 8 * (1 + max(c[1] for c in chosen))
    tiles, masks, point, weights = refs[:count], refs[count], refs[count + 1], refs[count + 2]
    rest = refs[count + 3 :]
    if pointed:
        before, edge, strip = rest[:3]
        outs = rest[3:7]
        windows, weight_buf, point_buf, acc, sems, weight_sems = rest[7:]
    else:
        (result,) = rest[:1]
        windows, weight_buf, sems, weight_sems = rest[1:]
        acc = result
    iy, ix, ik, cut = info[0], info[1], info[2], info[3]
    mine = acc.shape[-1]
    fetches, loads = [], []
    for n, (b, first, main, rim) in enumerate(chosen):
        group = tiles[8 * first : 8 * first + 8]
        fetches.append(tile_copies(info, group, windows.at[n], sems.at[n], main, rim))
        if b is None:
            loads.append(
                [pltpu.make_async_copy(point.at[:, iy, ix], point_buf, weight_sems.at[n, 0])]
            )
        else:
            loads.append(
                [
                    pltpu.make_async_copy(
                        weights.at[b, i, j, :, iy, ix],
                        weight_buf.at[n, j, :, :, pl.ds(i * lanes, lanes)],
                        weight_sems.at[n, 3 * j + i],
                    )
                    for j in range(3)
                    for i in range(3)
                ]
            )
        for copy in loads[n]:
            copy.start()

    def times(a, w):
        return lax.dot_general(
            a, w.reshape(mine, w.shape[-1]), (((1,), (1,)), ((), ())), preferred_element_type=F32
        )

    for n, (b, _, _, _) in enumerate(chosen):
        for copy in fetches[n] + loads[n]:
            copy.wait()
        window = windows.at[n]
        for dx in range(2):
            col = (ix ^ dx) * 16 + ik * 8
            if b is None:
                for e in range(0, 8, 2):
                    source = window[pl.ds(REACH + col + e, 2), PAD : PAD + 128, :]
                    value = times(source.reshape(256, lanes), point_buf[...])
                    for u in range(2):
                        pool = jnp.where(col + e + u < cut, edge[...], strip[...])
                        acc[dx, e + u] += (
                            before[dx, e + u] + value[u * 128 : u * 128 + 128] + pool
                        )
            else:

                def product(j, rows, n=n):
                    return times(rows, weight_buf[n, j])

                branch_sum(
                    window, masks, b, col, spreads[b], -1, cut, product, acc.at[dx], n == 0
                )
    if pointed:
        for dx in range(2):
            for dy in range(2):
                row = pl.multiple_of((iy ^ dy) * 64, 64)
                outs[dy * 2 + dx][...] = acc[dx, :, pl.ds(row, 64), :].astype(BF)


def weight_kernel(spread, b, sources, lanes, info, *refs):
    tiles = refs[:8]
    masks, across = refs[8:10]
    pooled = len(sources) > 1
    outs = refs[10 + pooled : -4]
    windows, out, sems, out_sems = refs[-4:]
    cut = info[3]
    parts = out.shape[0]
    each = out.shape[2]
    paired = len(outs) == 2
    fetches = [
        tile_copies(info, tiles, windows.at[n], sems.at[n], main, rim)
        for n, (main, rim) in enumerate(sources)
    ]

    def emit(t, value):
        for z in range(parts):
            out[info[4] ^ z if paired else z, t] = value[z * each : (z + 1) * each].astype(BF)

    for copy in fetches[0]:
        copy.wait()
    window = windows.at[0]
    for j in (1, 0, 2):
        move = (j - 1) * spread
        columns = [p for p in range(32) if 0 <= p + move < 32]
        total = None
        for at in range(0, len(columns), 8):
            group = columns[at : at + 8]
            right = []
            for p in group:
                ok = None if j == 1 else ((p < cut) == (p + move < cut))
                right.append(
                    jnp.concatenate(
                        [shift_rows(window, masks, b, p, i, spread, -1, cut, ok) for i in range(3)],
                        axis=1,
                    )
                )
            first, last = (group[0] + move) * 128, (group[-1] + move + 1) * 128
            part = dot(across[:, first:last], jnp.concatenate(right, axis=0))
            total = part if total is None else total + part
        for i in range(3):
            emit(3 * i + j, total[:, i * lanes : (i + 1) * lanes])
    if len(sources) > 1:
        for copy in fetches[1]:
            copy.wait()
        plain = windows[1, REACH : REACH + 32, PAD : PAD + 128, :].reshape(32 * 128, lanes)
        emit(9, dot(across[...], plain))
        emit(10, refs[10][...])
    if paired:
        moves = [(0, outs[0].at[0]), (3, outs[0].at[1]), (1, outs[1].at[0]), (2, outs[1].at[1])]
        moves = [(out.at[m], target) for m, target in moves]
    else:
        moves = [(out, outs[0])]
    copies = [
        pltpu.make_async_copy(source, target, out_sems.at[n])
        for n, (source, target) in enumerate(moves)
    ]
    for copy in copies:
        copy.start()
    for copy in copies:
        copy.wait()


def collect_kernel(first, count, extras, info, *refs):
    pieces = refs[:4]
    outs = refs[len(refs) - 3 - len(extras) : len(refs) - 2]
    buf, sem = refs[len(refs) - 2 :]
    ix, ik = info[1], info[2]
    if len(extras) == 1:
        outs[1][4] = refs[4][...]
    for n, piece in enumerate(pieces):
        index = (ix ^ (n // 2)) * 2 + (ik ^ (n % 2))
        for t in range(count):
            buf[t, index] = piece[t].astype(F32)
        at = count
        for e, length in enumerate(extras):
            for t in range(length):
                outs[1 + e][index, t] = piece[at + t].astype(F32)
            at += length
    copy = pltpu.make_async_copy(buf, outs[0].at[pl.ds(first, count)], sem)
    copy.start()
    copy.wait()


def pack_kernel(share, info, full, marks, *refs):
    iy, ix = info[0], info[1]
    rims = refs[4]
    for n in range(4):
        other = (iy ^ (n // 2)) * 2 + (ix ^ (n % 2))
        for z in range(full.shape[-1] // (4 * share)):
            lane = pl.multiple_of((z * 4 + other) * share, 128)
            value = jnp.swapaxes(full[:, :, pl.ds(lane, share)], 0, 1)
            refs[n][:, :, z * share : (z + 1) * share] = value

            @pl.when(iy == 0)
            def _(value=value, other=other, z=z):
                rims[other, :, :RIM, z * share : (z + 1) * share] = value[:, :RIM]

            @pl.when(iy == 1)
            def _(value=value, other=other, z=z):
                rims[other, :, :REACH, z * share : (z + 1) * share] = value[:, 64 - REACH :]

    for n in range(4):
        for q in range(8):
            rims[n, q, REACH : REACH + 1, :] = marks[...]


def unpack_kernel(share, info, *refs):
    iy, ix = info[0], info[1]
    full = refs[4]
    for n in range(4):
        other = (iy ^ (n // 2)) * 2 + (ix ^ (n % 2))
        for z in range(full.shape[-1] // (4 * share)):
            lane = pl.multiple_of((z * 4 + other) * share, 128)
            value = refs[n][:, :, z * share : (z + 1) * share]
            full[:, :, pl.ds(lane, share)] = jnp.swapaxes(value, 0, 1)


def across_kernel(share, info, *refs):
    tiles, out, rows, zero = refs[:8], *refs[8:11]
    window, acc, sems = refs[11:]
    ik, cut = info[2], info[3]
    for copy in tile_copies(info, tiles, window, sems):
        copy.wait()
    acc[...] = jnp.zeros_like(acc)
    for q in range(32):
        value = window[REACH + q, PAD : PAD + 128, :]
        turned = value.T
        for z in range(turned.shape[0] // share):
            low = turned[z * share : z * share + share // 2]
            high = turned[z * share + share // 2 : (z + 1) * share]
            out[z * share // 2 : (z + 1) * share // 2, q * 128 : (q + 1) * 128] = jnp.where(
                ik == 0, low, high
            )
        acc[(q >= cut).astype(jnp.int32)] += value.astype(F32)
    rows[...] = acc[1]
    zero[...] = jnp.sum(acc[0], axis=0, keepdims=True)


VMEM = pl.BlockSpec(memory_space=pltpu.VMEM)
SMEM = pl.BlockSpec(memory_space=pltpu.SMEM)
ANY = pl.BlockSpec(memory_space=pl.ANY)


def call(kernel, name, flops, in_specs, out_shape, scratch, args, out_specs=None, aliases=None):
    return pl.pallas_call(
        kernel,
        name=name,
        in_specs=in_specs,
        out_specs=out_specs or jax.tree.map(lambda _: VMEM, out_shape),
        out_shape=out_shape,
        input_output_aliases=aliases or {},
        scratch_shapes=scratch,
        compiler_params=pltpu.CompilerParams(vmem_limit_bytes=VMEM_LIMIT),
        cost_estimate=pl.CostEstimate(flops=flops, bytes_accessed=10**7, transcendentals=0),
    )(*args)


def per_device(
    feature_map,
    image_ids,
    point_weight,
    atrous_weight,
    pool_weight,
    project_weight,
    bn_gain,
    bn_shift,
    out_grad,
):
    rows, cols, chans = feature_map.shape
    feat = point_weight.shape[1]
    pixels = rows * cols
    zs = lax.axis_size("z")
    axes = ("k", "x", "y", "z")
    iz, iy, ix, ik = (lax.axis_index(a) for a in ("z", "y", "x", "k"))
    row_count = 2 * zs
    total = float(pixels * row_count * 4)
    images = rows * row_count // IMG_ROWS + 1
    share = chans // (4 * zs)
    mine = chans // 4
    spreads = [REACH * (b + 1) // 3 for b in range(3)]
    def pick(first, second, index):
        return jnp.where(index == 0, first, second)

    def rim(x, depth):
        return pick(x[:, :depth], x[:, rows - depth :], iy)

    def beyond(x, dy, dx):
        pairs = []
        for z in range(zs):
            for y in range(2):
                far = z - 1 + 2 * y
                if 0 <= far < zs:
                    for i in range(2):
                        target = (far * 2 + (y ^ dy)) * 2 + (i ^ dx)
                        pairs.append(((z * 2 + y) * 2 + i, target))
        return lax.ppermute(x, ("z", "y", "x"), pairs)

    with jax.named_scope("marks"):
        strip_own = jnp.max(image_ids, axis=1)
        edge_own = pick(strip_own[:REACH], strip_own[rows - REACH :], iy)
        zero_own = jnp.sum((image_ids[0] == 0).astype(jnp.int32))
        marks = jnp.concatenate([strip_own, edge_own, zero_own[None]])
        marks = jnp.pad(marks, (0, mine - marks.shape[0])).astype(BF)[None]

    places = jnp.stack([iy, ix, ik, ik, iz]).astype(jnp.int32)
    aligned = share % 128 == 0
    with jax.named_scope("spread_features"):
        if aligned:
            tile_shape = jax.ShapeDtypeStruct((cols, rows, mine), BF)
            *tiles, brims = call(
                partial(pack_kernel, share),
                "pack",
                0,
                [SMEM, VMEM, VMEM],
                [tile_shape] * 4 + [jax.ShapeDtypeStruct((4, cols, RIM, mine), BF)],
                [],
                [places, feature_map, marks],
            )
        else:
            packed = feature_map.transpose(1, 0, 2).reshape(cols, rows, zs, 2, 2, share)
            packed = packed.transpose(3, 4, 0, 1, 2, 5)
            packed = packed.reshape(4, cols, rows, mine)
            tiles = [
                lax.dynamic_index_in_dim(packed, (iy ^ dy) * 2 + (ix ^ dx), 0, False)
                for dy in range(2)
                for dx in range(2)
            ]
            brims = pick(packed[:, :, :REACH], packed[:, :, rows - REACH :], iy)
            brims = jnp.pad(brims, ((0, 0), (0, 0), (0, RIM - REACH), (0, 0)))
            brims = brims.at[:, :, REACH].set(marks)
        note = jnp.broadcast_to(marks[None, None], (4, cols, 1, mine))
        own, to_x, to_y, to_d = tiles
        mains = [own, swap(to_x, "x"), swap(to_y, "y"), crossed(to_d)]
        halo, mains = lax.optimization_barrier((beyond(brims, 0, 0), mains))
        halo = lax.dynamic_update_slice_in_dim(halo, note, REACH + 1, axis=2)
        halo = lax.all_to_all(halo, ("y", "x"), 0, 0)
        halos = [halo, swap(halo, "k")]

    mains = mains + [swap(g, "k") for g in mains]
    with jax.named_scope("marks"):
        told = jnp.stack([h[:, 0, REACH : REACH + 2] for h in halos]).astype(jnp.int32)
        told = told.reshape(2, 2, 2, 2, mine)
        strips = jnp.max(told[:, :, :, 1, :rows], axis=(0, 2))
        edges = jnp.max(told[:, :, :, 0, rows : rows + REACH], axis=(0, 2))
        cut = jnp.sum(told[:, 0, :, 1, rows + REACH])
        strip_plane = strips.reshape(2 * rows)
        top, bottom = edges[1], edges[0]
        strip_tall = jnp.concatenate([top, strip_plane, bottom])
        masks = jnp.stack(
            [
                jnp.stack(
                    [
                        strip_plane
                        == lax.slice_in_dim(strip_tall, REACH + s * d, REACH + s * d + 2 * rows)
                        for s in (-1, 1)
                    ]
                )
                for d in spreads
            ]
        )
        masks = jnp.broadcast_to(masks[..., None], (3, 2, 2 * rows, 128)).astype(BF)
        info = jnp.stack([iy, ix, ik, cut, iz]).astype(jnp.int32)


    local_ids = image_ids.T.reshape(pixels)
    image_range = jnp.arange(images, dtype=jnp.int32)
    table = local_ids[:, None] == image_range[None, :]

    point_view = point_weight.reshape(zs, 2, 2, share, feat)
    atrous_view = atrous_weight.reshape(3, 3, 3, zs, 2, 2, share, feat)

    def forward(units):
        shape = (2, cols, rows, feat)
        return call(
            partial(forward_kernel, units, spreads, mine),
            "forward_taps",
            2 * 2048 * mine * 256 * 15,
            [SMEM] + [ANY] * 8 + [VMEM] * 3 + [ANY] * 2,
            [jax.ShapeDtypeStruct(shape, F32), jax.ShapeDtypeStruct(shape, BF)] * 2,
            [
                pltpu.VMEM((32 + 2 * REACH, 2 * PAD + 128, mine), BF),
                pltpu.VMEM((zs, share, feat), BF),
                pltpu.VMEM((2, 3, 3, zs, share, feat), BF),
                pltpu.VMEM((8, 128, feat), F32),
                pltpu.SemaphoreType.DMA((16,)),
                pltpu.SemaphoreType.DMA((2, 9)),
            ],
            [info, *mains, *halos, masks, point_view, atrous_view],
        )

    def reduce_first(parts):
        keep_x, send_x, keep_y, send_y = parts
        return keep_x, swap(send_x, "x"), keep_y, swap(send_y, "y")

    def reduce_middle(parts):
        keep_x, got_x, keep_y, got_y = parts
        more_x = (keep_x[1] + got_x[1].astype(F32)).astype(BF)
        more_y = (keep_y[1] + got_y[1].astype(F32)).astype(BF)
        return more_x, more_y

    def reduce_last(parts, last_x, last_y):
        keep_x, got_x, keep_y, got_y = parts
        value_x = keep_x[0] + got_x[0].astype(F32) + last_x.astype(F32)
        value_y = keep_y[0] + got_y[0].astype(F32) + last_y.astype(F32)
        return [value_x.reshape(pixels, feat), value_y.reshape(pixels, feat)]

    early = forward([None, 0])
    early_got = reduce_first(early)
    late = forward([1, 2])
    early_got, late = lax.optimization_barrier((early_got, late))
    late_got = reduce_first(late)
    early_more = reduce_middle(early_got)
    early_last = [swap(early_more[0], "y"), swap(early_more[1], "x")]

    half = share // 2
    strip_table = strip_plane[:, None] == image_range[None, :]
    with jax.named_scope("across"):
        mains_late, early_last = lax.optimization_barrier((mains, early_last))
        if aligned:
            across, row_sums, zero_sums = call(
                partial(across_kernel, share),
                "across",
                2 * 10**9,
                [SMEM] + [ANY] * 8,
                [
                    jax.ShapeDtypeStruct((mine // 2, 32 * 2 * rows), BF),
                    jax.ShapeDtypeStruct((2 * rows, mine), F32),
                    jax.ShapeDtypeStruct((1, mine), F32),
                ],
                [
                    pltpu.VMEM((32 + 2 * REACH, 2 * PAD + 128, mine), BF),
                    pltpu.VMEM((2, 2 * rows, mine), F32),
                    pltpu.SemaphoreType.DMA((16,)),
                ],
                [info, *mains_late],
            )
        else:
            columns = []
            for x in range(2):
                for k in range(2):
                    index = [(ik ^ k) * 4 + (iy ^ y) * 2 + (ix ^ x) for y in range(2)]
                    stack = [lax.select_n(n.astype(jnp.int32), *mains_late) for n in index]
                    columns.append(jnp.concatenate(stack, axis=1))
            plane = jnp.concatenate(columns, axis=0)
            in_strip = (jnp.arange(32) >= cut)[:, None, None]
            row_sums = jnp.sum(jnp.where(in_strip, plane.astype(F32), 0.0), axis=0)
            zero_sums = jnp.sum(jnp.where(in_strip, 0.0, plane.astype(F32)), axis=(0, 1))[None]
            plane = plane.reshape(32, 2 * rows, zs, 2, half)
            plane = lax.dynamic_index_in_dim(plane, ik, 3, False)
            across = plane.reshape(32 * 2 * rows, mine // 2).T

    with jax.named_scope("image_sums"):
        sums = lax.dot_general(
            strip_table.astype(F32),
            row_sums,
            (((0,), (0,)), ((), ())),
            precision=lax.Precision.HIGHEST,
        )
        sums = jnp.where(image_range[:, None] == 0, zero_sums, sums)
        pool_mine = pool_weight.reshape(zs, 2, 2, share, feat)
        pool_mine = lax.dynamic_slice(
            pool_mine, (0, iy, ix, 0, 0), (zs, 1, 1, share, feat)
        ).reshape(mine, feat)
        per_image_part = 0.5 * exact(sums, pool_mine.astype(F32))
        strip_rows = jnp.sum(strip_table.astype(F32), axis=0)
        strip_rows = jnp.where((iy == 0) & (ix == 0) & (ik == 0), strip_rows, 0.0)
        strip_rows = jnp.pad(strip_rows, (0, -images % feat)).reshape(-1, feat)

    late_got, across, sums = lax.optimization_barrier((late_got, across, sums))
    late_more = reduce_middle(late_got)
    branches = reduce_last(early_got, *early_last)
    branches += reduce_last(late_got, swap(late_more[0], "y"), swap(late_more[1], "x"))

    first = jnp.concatenate([moments(value) for value in branches], axis=0)
    first = allsum(jnp.concatenate([first, per_image_part, strip_rows], axis=0))
    strip_rows = first[8 + images :].reshape(-1)[:images]
    counts = jnp.where(
        image_range == 0,
        (cut * (rows * row_count)).astype(F32),
        strip_rows * (4 * cols - cut).astype(F32),
    )
    per_image = first[8 : 8 + images] / counts[:, None]
    first = first[:8].reshape(4, 2, feat).transpose(1, 0, 2).reshape(2, 4 * feat)
    weighted = counts[:, None] * per_image
    pool_stats = jnp.stack([jnp.sum(weighted, axis=0), jnp.sum(weighted * per_image, axis=0)])
    four = 4 * feat
    flat_gain, flat_shift = bn_gain[:4].reshape(four), bn_shift[:4].reshape(four)
    mean = first[0] / total
    scale = lax.rsqrt(first[1] / total - mean * mean + EPSILON)
    normed = (jnp.concatenate(branches, axis=1) - mean) * scale
    lifted = normed * flat_gain + flat_shift
    mean4 = pool_stats[0] / total
    scale4 = lax.rsqrt(pool_stats[1] / total - mean4 * mean4 + EPSILON)
    normed4 = (per_image - mean4) * scale4
    lifted4 = normed4 * bn_gain[4] + bn_shift[4]
    joined = smooth(lifted).astype(BF)
    joined4 = smooth(lifted4).astype(BF)
    table_float = table.astype(F32)
    head = dot(joined, project_weight[:four]) + exact(
        table_float, dot(joined4, project_weight[four:])
    )
    head_stats = allsum(moments(head))
    head_mean = head_stats[0] / total
    head_scale = lax.rsqrt(head_stats[1] / total - head_mean * head_mean + EPSILON)
    head_norm = (head - head_mean) * head_scale
    head_lift = head_norm * bn_gain[5] + bn_shift[5]
    output = smooth(head_lift).astype(BF).reshape(cols, rows, feat)
    cotangent = out_grad.transpose(1, 0, 2).reshape(pixels, feat).astype(F32)
    head_grad = cotangent * smooth_slope(head_lift)
    head_back = allsum(
        jnp.stack([jnp.sum(head_grad, axis=0), jnp.sum(head_grad * head_norm, axis=0)])
    )
    head_slope = (
        bn_gain[5]
        * head_scale
        * (head_grad - head_back[0] / total - head_norm * head_back[1] / total)
    ).astype(BF)
    joined_grad = lax.dot_general(
        head_slope, project_weight[:four], (((1,), (1,)), ((), ())), preferred_element_type=F32
    )
    grads = joined_grad * smooth_slope(lifted)
    image_heads = jnp.einsum(
        "pi,pf->if", table.astype(BF), head_slope, preferred_element_type=F32
    )
    rear = jnp.concatenate(
        [
            jnp.stack([jnp.sum(grads, axis=0), jnp.sum(grads * normed, axis=0)]).reshape(8, feat),
            image_heads,
        ],
        axis=0,
    )
    rear = allsum(rear)
    shift_back, gain_back = rear[:4].reshape(four), rear[4:8].reshape(four)
    slopes = (
        flat_gain * scale * (grads - shift_back / total - normed * gain_back / total)
    ).astype(BF)

    with jax.named_scope("project_grad"):
        project_inputs = joined, head_slope

    with jax.named_scope("spread_slopes"):
        point_tile, *tiles_out = [
            slopes[:, k * feat : (k + 1) * feat].reshape(cols, rows, feat) for k in range(4)
        ]
        brim = beyond(rim(tiles_out[0], 16), 0, 0)
        deep = rim(tiles_out[2], 32)
        brims = jnp.concatenate([rim(tiles_out[1], 16), deep[:, :16], deep[:, 16:]], axis=2)
        brims, brim = lax.optimization_barrier((brims, brim))
        brims = beyond(brims, 0, 0)

        def both_cores(got):
            return got + [swap(g, "k") for g in got]

        tile3 = jnp.concatenate([tiles_out[0], brim], axis=1)
        got3 = [tile3, swap(tile3, "x"), swap(tile3, "y"), crossed(tile3)]
        left, right = gate(project_inputs, tile3)
        project_part = lax.dot_general(
            left, right, (((0,), (0,)), ((), ())), preferred_element_type=F32
        )
        blocks = project_part.astype(BF).reshape(4, feat, feat)
        blocks = lax.all_to_all(blocks, ("x", "k"), 0, 0)
        across, blocks = lax.optimization_barrier((across, blocks))
        project_sum = jnp.sum(blocks.astype(F32), axis=0)
        project_low = project_sum.astype(BF)
        project_got = z_swap(project_low, 1)
        got3, brims = lax.optimization_barrier((got3, brims))
        edges = [brims[:, :, i * feat : (i + 1) * feat] for i in range(3)]
        tile2 = jnp.concatenate([tiles_out[1], edges[0]], axis=1)
        tile1 = jnp.concatenate([tiles_out[2], edges[1], edges[2], point_tile], axis=1)
        group3 = both_cores(got3)
        tile2, group3, output = lax.optimization_barrier((tile2, group3, output))
        output = output.transpose(1, 0, 2)
        arrived2 = [tile2, swap(tile2, "x"), swap(tile2, "y"), crossed(tile2)]

    rear, sums = gate((rear, sums), tile3)
    image_heads = rear[8:]
    grads4 = smooth_slope(lifted4) * exact(image_heads, project_weight[four:].astype(F32).T)
    shift4, gain4 = jnp.sum(grads4, axis=0), jnp.sum(grads4 * normed4, axis=0)
    image_slope = (
        bn_gain[4]
        * scale4
        * (grads4 - counts[:, None] * (shift4 / total + normed4 * gain4 / total))
    )
    image_low = image_slope.astype(BF)
    spread_back = (
        lax.dot_general(
            image_low, pool_mine, (((1,), (1,)), ((), ())), preferred_element_type=F32
        )
        / counts[:, None]
    )
    strip_back = exact(strip_table.astype(F32), spread_back)
    sums_mine = lax.dynamic_index_in_dim(sums.reshape(images, zs, 2, half), ik, 2, False)
    pool_part = lax.dot_general(
        sums_mine.reshape(images, mine // 2),
        image_low.astype(F32) / counts[:, None],
        (((0,), (0,)), ((), ())),
        precision=lax.Precision.HIGHEST,
    )

    def weight_grad(b, tiles, lanes_at, more=()):
        taps = 8 + len(lanes_at) + len(more)
        return call(
            partial(weight_kernel, spreads[b], b, lanes_at, feat),
            "weight_taps",
            2 * 4096 * (mine // 2) * 256 * 15,
            [SMEM] + [ANY] * 8 + [VMEM] * (2 + len(more)),
            [jax.ShapeDtypeStruct((2, taps, half, feat), BF)] * 2
            if zs == 4
            else [jax.ShapeDtypeStruct((zs, taps, half, feat), BF)],
            [
                pltpu.VMEM((len(lanes_at), 32 + 2 * REACH, 2 * PAD + 128, feat), BF),
                pltpu.VMEM((zs, taps, half, feat), BF),
                pltpu.SemaphoreType.DMA((2, 16)),
                pltpu.SemaphoreType.DMA((4,)),
            ],
            [info, *tiles, masks, across, *more],
            out_specs=[ANY] * (2 if zs == 4 else 1),
        )

    def collect(pieces, first, buffer, pool=None):
        count = 9 if buffer else 18
        extras = [1, 1] if buffer else [pieces[0].shape[0] - count]
        grad = jax.ShapeDtypeStruct((27, 4, half, feat), F32)
        sides = [jax.ShapeDtypeStruct((4, n, half, feat), F32) for n in extras]
        if pool is not None:
            sides = [jax.ShapeDtypeStruct((5, *pool.shape), F32)]
        given = buffer if pool is None else [pool]
        return call(
            partial(collect_kernel, first, count, extras),
            "collect",
            6 * 10**9,
            [SMEM] + [VMEM] * 4 + [VMEM if pool is not None else ANY],
            [grad, *sides],
            [pltpu.VMEM((count, 4, half, feat), F32), pltpu.SemaphoreType.DMA],
            [places, *pieces, *given],
            out_specs=[ANY] + [VMEM] * len(extras),
            aliases={5: 0} if buffer else {},
        )

    def scatter_first(part):
        if zs != 4:
            return lax.psum_scatter(part[0], "z", scatter_dimension=0, tiled=True), None
        return part[0], z_swap(part[1], 1)

    def scatter_second(state):
        keep, got = state
        if zs != 4:
            return keep, None
        more = (keep[1].astype(F32) + got[1].astype(F32)).astype(BF)
        return keep[0].astype(F32) + got[0].astype(F32), z_swap(more, 3)

    def scatter_last(state):
        keep, got = state
        if zs != 4:
            return keep[0]
        return (keep + got.astype(F32)).astype(BF)

    project_pool = lax.dot_general(
        joined4.astype(F32),
        image_heads,
        (((0,), (0,)), ((), ())),
        precision=lax.Precision.HIGHEST,
    ).reshape(feat // half, half, feat)
    across, pool_part, spread_back, strip_back, project_pool = lax.optimization_barrier(
        (across, pool_part, spread_back, strip_back, project_pool)
    )
    part3 = weight_grad(0, group3, [(0, 16)])
    arrived2, part3, project_got = lax.optimization_barrier((arrived2, part3, project_got))
    project_sum = project_low.astype(F32) + project_got.astype(F32)
    step = 2
    while step < zs // 2:
        project_sum = project_sum + z_swap(project_sum, step)
        step *= 2
    project_low = project_sum.astype(BF)
    project_got = z_swap(project_low, step)
    group2 = both_cores(arrived2)
    tile1, group2 = lax.optimization_barrier((tile1, group2))
    arrived1 = [tile1, swap(tile1, "x"), swap(tile1, "y"), crossed(tile1)]
    sums3 = scatter_first(part3)
    part2 = weight_grad(1, group2, [(0, 16)])
    part2, group2, project_got, sums3 = lax.optimization_barrier(
        (part2, group2, project_got, sums3)
    )
    sums2, sums3 = scatter_first(part2), scatter_second(sums3)
    project_low = (project_low.astype(F32) + project_got.astype(F32)).astype(BF)
    project_low = gate(project_low, part2)

    def input_part(chosen, groups, pointed, more, outs):
        n = len(chosen)
        scratch = [
            pltpu.VMEM((n, 32 + 2 * REACH, 2 * PAD + 128, feat), BF),
            pltpu.VMEM((n, 3, zs, share, 3 * feat), BF),
        ]
        if pointed:
            scratch += [pltpu.VMEM((zs, share, feat), BF), pltpu.VMEM((2, 8, 128, mine), F32)]
        scratch += [pltpu.SemaphoreType.DMA((n, 16)), pltpu.SemaphoreType.DMA((n, 9))]
        return call(
            partial(input_kernel, chosen, spreads, feat, pointed),
            "input_taps",
            2 * 2048 * mine * 256 * 20,
            [SMEM] + [ANY] * 8 * len(groups) + [VMEM] + [ANY] * 2 + [VMEM] * len(more),
            outs,
            scratch,
            [info, *[t for g in groups for t in g], masks, point_view, atrous_view, *more],
        )

    with jax.named_scope("input_grad"):
        sums_so_far = input_part(
            [(0, 0, 0, 16), (1, 1, 0, 16)],
            [group3, group2],
            False,
            [],
            jax.ShapeDtypeStruct((2, cols, 2 * rows, mine), F32),
        )
    arrived1, sums_so_far, sums2, sums3 = lax.optimization_barrier(
        (arrived1, sums_so_far, sums2, sums3)
    )
    group1 = both_cores(arrived1)
    sums2 = scatter_second(sums2)
    project_got = swap(gate(project_low, arrived1), "y")
    part1 = weight_grad(2, group1, [(0, 32), (96, 0)], [pool_part])
    sums3, sums2, project_got, part1 = lax.optimization_barrier(
        (sums3, sums2, project_got, part1)
    )
    project_sum = project_low.astype(F32) + project_got.astype(F32)
    project_sum = project_sum.astype(BF).reshape(feat // half, half, feat)
    joint = jnp.concatenate([scatter_last(sums3), scatter_last(sums2), project_sum], axis=0)
    joint_x = swap(joint, "x")
    sums1 = scatter_first(part1)
    with jax.named_scope("input_grad"):
        group1, part1 = lax.optimization_barrier((group1, part1))
        shape = jax.ShapeDtypeStruct((cols, rows, mine), BF)
        own, to_x, to_y, to_d = input_part(
            [(2, 0, 0, 32), (None, 0, 96, 0)],
            [group1],
            True,
            [sums_so_far, spread_back[:1], strip_back],
            [shape] * 4,
        )
        sums1, joint_x = gate((sums1, joint_x), own)
        got = [own, swap(to_x, "x"), swap(to_y, "y"), crossed(to_d)]
        sums1 = scatter_second(sums1)
        got, sums1 = lax.optimization_barrier((got, sums1))
        joint, joint_x = gate((joint, joint_x), got)
        pieces32 = [joint, swap(joint, "k"), joint_x, swap(joint_x, "k")]
        grad, project_grad = collect(pieces32, 0, [], project_pool)
        project_grad = project_grad.reshape(5 * feat, feat)
        if aligned:
            input_grad = call(
                partial(unpack_kernel, share),
                "unpack",
                4 * 10**9,
                [SMEM] + [VMEM] * 4,
                jax.ShapeDtypeStruct((rows, cols, chans), BF),
                [],
                [places, *got],
            )
        else:
            planes = []
            for y in range(2):
                for x in range(2):
                    index = ((iy ^ y) * 2 + (ix ^ x)).astype(jnp.int32)
                    planes.append(lax.select_n(index, *got).reshape(cols, rows, zs, share))
            input_grad = jnp.stack(planes, axis=3).reshape(cols, rows, chans).transpose(1, 0, 2)

    done = scatter_last(sums1)
    done_x = swap(done, "x")
    done_x, grad, input_grad = lax.optimization_barrier((done_x, grad, input_grad))
    pieces1 = [done, swap(done, "k"), done_x, swap(done_x, "k")]
    grad, point_grad, pool_grad = collect(pieces1, 18, [grad])
    atrous_grad = grad.reshape(3, 3, 3, 4 * half, feat)
    point_grad, pool_grad = (v.reshape(4 * half, feat) for v in (point_grad, pool_grad))

    gain_grad = jnp.concatenate([rear[4:8], gain4[None], head_back[1][None]], axis=0)
    shift_grad = jnp.concatenate([rear[:4], shift4[None], head_back[0][None]], axis=0)
    return (
        output,
        input_grad,
        point_grad,
        atrous_grad,
        pool_grad,
        project_grad,
        gain_grad,
        shift_grad,
    )


def solution(mesh):
    row, col = mesh.devices.shape
    fine = Mesh(mesh.devices.reshape(row // 2, 2, col // 2, 2), ("z", "y", "x", "k"))
    rows, cols = ("z", "y"), ("x", "k")
    placed = (
        P(rows, cols, None),
        P(rows, cols),
        P(),
        P(),
        P(),
        P(),
        P(),
        P(),
        P(rows, cols, None),
    )
    return jax.shard_map(
        per_device,
        mesh=fine,
        in_specs=placed,
        out_specs=(
            P(rows, cols, None),
            P(rows, cols, None),
            P(rows, None),
            P(None, None, None, rows, None),
            P(rows, None),
            P(),
            P(),
            P(),
        ),
        check_vma=False,
    )
```
